32 devices in a mesh: dp: 8 (over y, x, core), mp: 4 (over z).
Axes of the slice: x: 2, y: 2, z: 4, core: 2. Of those that a mesh axis runs over, the one named last changes fastest.
Arguments:
- inputs: bfloat16 [16384, 768], P('dp'), may hold values from -6 to 6
- cotangent: bfloat16 [16384, 768], P('dp'), may hold values from -6 to 6
- span_table: int32 [32, 2], P('dp'), may hold values from 0 to 486, as said below
- ln1_gain: bfloat16 [768], replicated, may hold values from 0.5 to 1.5
- ln1_shift: bfloat16 [768], replicated, may hold values from -2 to 2
- w_query: bfloat16 [768, 768], P(None, 'mp'), may hold values from -0.21875 to 0.21875
- b_query: bfloat16 [768], P('mp'), may hold values from -2 to 2
- w_key: bfloat16 [768, 768], P(None, 'mp'), may hold values from -0.21875 to 0.21875
- w_value: bfloat16 [768, 768], P(None, 'mp'), may hold values from -0.21875 to 0.21875
- b_value: bfloat16 [768], P('mp'), may hold values from -2 to 2
- w_out: bfloat16 [768, 768], P('mp'), may hold values from -0.875 to 0.875
- b_out: bfloat16 [768], replicated, may hold values from -2 to 2
- ln2_gain: bfloat16 [768], replicated, may hold values from 0.5 to 1.5
- ln2_shift: bfloat16 [768], replicated, may hold values from -2 to 2
- w_up: bfloat16 [768, 3072], P(None, 'mp'), may hold values from -0.21875 to 0.21875
- b_up: bfloat16 [3072], P('mp'), may hold values from -2 to 2
- w_down: bfloat16 [3072, 768], P('mp'), may hold values from -0.109375 to 0.109375
- b_down: bfloat16 [768], replicated, may hold values from -2 to 2
Outputs:
- layer_out: bfloat16 [16384, 768], P(('dp', 'mp'))
- grad_inputs: bfloat16 [16384, 768], P(('dp', 'mp'))
- grad_ln1_gain: float32 [768], replicated
- grad_ln1_shift: float32 [768], replicated
- grad_w_query: float32 [768, 768], P(None, 'mp')
- grad_b_query: float32 [768], P('mp')
- grad_w_key: float32 [768, 768], P(None, 'mp')
- grad_w_value: float32 [768, 768], P(None, 'mp')
- grad_b_value: float32 [768], P('mp')
- grad_w_out: float32 [768, 768], P('mp')
- grad_b_out: float32 [768], replicated
- grad_ln2_gain: float32 [768], replicated
- grad_ln2_shift: float32 [768], replicated
- grad_w_up: float32 [768, 3072], P(None, 'mp')
- grad_b_up: float32 [3072], P('mp')
- grad_w_down: float32 [3072, 768], P('mp')
- grad_b_down: float32 [768], replicated
The draws below stay inside these ranges and needn't reach their ends.
Inputs may be any that keep to these rules, and one draw needn't show every extreme that they name: `span_table`: column 0 is the first masked position and column 1 the number of masked positions, between 26 and 128; each span lies inside its sequence; both extreme lengths occur.
All inputs are finite; a program needn't handle non-finite values.
Results may differ from the reference program's by a relative error of at most 0.019.
Values may be sent and summed in bfloat16 or wider, within the bound.
No kernel may reach another device: no remote copies, remote signals or barrier semaphores. Data moves between devices by JAX's collectives and lax.ppermute only.
A program may use at most 192 MiB of HBM per device.

```python
import jax
import jax.numpy as jnp
from jax import lax

D = 768
H = 12
HD = 64
FF = 3072
LENGTH = 512
SEQS = 32
TOKENS = 16384


def draw_span_table(key, part):
    key = jax.random.fold_in(key, 7)
    keys = jax.random.split(key, 4)
    short_len = LENGTH // 20 + 1
    long_len = LENGTH // 4
    span_lens = jax.random.randint(keys[0], (SEQS,), short_len, long_len + 1)
    span_starts = jax.random.randint(keys[1], (SEQS,), 0, LENGTH - span_lens + 1)
    first_seq = jax.random.randint(keys[2], (), 0, SEQS)
    other_seq = (first_seq + jax.random.randint(keys[3], (), 1, SEQS)) % SEQS
    span_lens = span_lens.at[first_seq].set(long_len).at[other_seq].set(short_len)
    span_starts = span_starts.at[first_seq].set(0).at[other_seq].set(LENGTH - short_len)
    return jnp.stack([span_starts, span_lens], 1).astype(jnp.int32)


def block_levels(own_key, shape, cuts, smallest, largest):
    level = 1.0
    for dim, blocks in cuts:
        draws = jax.random.uniform(jax.random.fold_in(jax.random.fold_in(own_key, 6), dim), (blocks,), jnp.float32, smallest / len(cuts), largest / len(cuts))
        level = level * jnp.repeat(jnp.exp(draws), shape[dim] // blocks).reshape((-1,) + (1,) * (len(shape) - 1 - dim))
    return level


def centred(own_key, dims, width, bound, cuts=(), kind=jnp.bfloat16):
    level = block_levels(own_key, dims, cuts, -0.22, 0.18) if cuts else 1.0
    array = jax.random.normal(own_key, dims, jnp.float32) * width * level
    return jnp.minimum(jnp.maximum(array, -bound), bound).astype(kind)


def setup_inputs(seed: int = 0) -> dict:
    key_list = jax.random.split(jax.random.key(seed), 19)
    return {
        "inputs": centred(key_list[0], (TOKENS, D), 1.0, 6.0, ((0, 8),)),
        "cotangent": centred(key_list[1], (TOKENS, D), 1.0, 6.0, ((0, 8),)),
        "span_table": draw_span_table(jax.random.fold_in(key_list[18], 71), 0),
        "ln1_gain": jnp.clip(1.0 + 0.1 * jax.random.normal(key_list[3], (D,), jnp.float32), 0.5, 1.5).astype(jnp.bfloat16),
        "ln1_shift": centred(key_list[4], (D,), 0.3, 2.0),
        "w_query": centred(key_list[5], (D, D), D ** -0.5, 0.21875, ((1, 4),)),
        "b_query": centred(key_list[6], (D,), 0.3, 2.0, ((0, 4),)),
        "w_key": centred(key_list[7], (D, D), D ** -0.5, 0.21875, ((1, 4),)),
        "w_value": centred(key_list[8], (D, D), D ** -0.5, 0.21875, ((1, 4),)),
        "b_value": centred(key_list[9], (D,), 0.3, 2.0, ((0, 4),)),
        "w_out": centred(key_list[10], (D, D), (D // 16) ** -0.5, 0.875, ((0, 4),)),
        "b_out": centred(key_list[11], (D,), 0.3, 2.0),
        "ln2_gain": jnp.clip(1.0 + 0.1 * jax.random.normal(key_list[12], (D,), jnp.float32), 0.5, 1.5).astype(jnp.bfloat16),
        "ln2_shift": centred(key_list[13], (D,), 0.3, 2.0),
        "w_up": centred(key_list[14], (D, FF), D ** -0.5, 0.21875, ((1, 4),)),
        "b_up": centred(key_list[15], (FF,), 0.3, 2.0, ((0, 4),)),
        "w_down": centred(key_list[16], (FF, D), FF ** -0.5, 0.109375, ((0, 4),)),
        "b_down": centred(key_list[17], (D,), 0.3, 2.0),
    }


@jax.custom_vjp
def low(v):
    return lax.optimization_barrier(v.astype(jnp.bfloat16)).astype(jnp.float32)

@jax.custom_vjp
def low_back(v):
    return v

def low_keep(v):
    return (low(v), None)

def low_pass(kept, grad):
    return (grad,)

def back_keep(v):
    return (v, None)

def back_low(kept, grad):
    return (low(grad),)
low.defvjp(low_keep, low_pass)
low_back.defvjp(back_keep, back_low)
norm_eps = 1e-06

def highest(left, right):
    return jnp.dot(left, right, precision=lax.Precision.HIGHEST, preferred_element_type=jnp.float32)

def layer_norm(values, gain, shift):
    centered = values - lax.optimization_barrier(jnp.mean(values, -1, keepdims=True))
    rstd_rows = lax.rsqrt(lax.optimization_barrier(jnp.mean(centered * centered, -1, keepdims=True)) + norm_eps)
    return centered * rstd_rows * gain + shift

def forward(params, block):
    gain_one, shift_one, w_query, b_query, w_key, w_value, b_value, w_out, b_out, gain_two, shift_two, w_up, b_up, w_down, b_down = params
    normed = low(layer_norm(block, gain_one, shift_one))
    query = low_back(low(highest(normed, w_query) + b_query)).reshape(LENGTH, H, HD)
    key_rows = low_back(low(highest(normed, w_key))).reshape(LENGTH, H, HD)
    value_rows = low_back(low(highest(normed, w_value) + b_value)).reshape(LENGTH, H, HD)
    scores = low_back(jnp.einsum('qhd,khd->hqk', query, key_rows, precision=lax.Precision.HIGHEST) * 0.125)
    attn_prob = low(jax.nn.softmax(scores, axis=-1))
    mixed = jnp.einsum('hqk,khd->qhd', attn_prob, value_rows, precision=lax.Precision.HIGHEST).reshape(LENGTH, D)
    mixed = low_back(low(mixed))
    branch = low_back(highest(mixed, w_out) + b_out)
    resid = block + branch
    normed_two = low(layer_norm(resid, gain_two, shift_two))
    hidden_pre = low_back(highest(normed_two, w_up) + b_up)
    hidden = low(jax.nn.gelu(hidden_pre, approximate=False))
    return resid + highest(hidden, w_down) + b_down

def reference(inputs, cotangent, span_table, ln1_gain, ln1_shift, w_query, b_query, w_key, w_value, b_value, w_out, b_out, ln2_gain, ln2_shift, w_up, b_up, w_down, b_down):
    params = tuple((member.astype(jnp.float32) for member in (ln1_gain, ln1_shift, w_query, b_query, w_key, w_value, b_value, w_out, b_out, ln2_gain, ln2_shift, w_up, b_up, w_down, b_down)))
    positions = jnp.arange(LENGTH, dtype=jnp.int32)
    blocks = inputs.astype(jnp.float32).reshape(SEQS, LENGTH, D)
    cot_blocks = cotangent.astype(jnp.float32).reshape(SEQS, LENGTH, D)

    def scan_step(grad_total, seq_item):
        block, cot_block, span_row = seq_item
        span_mask = ((positions >= span_row[0]) & (positions < span_row[0] + span_row[1])).astype(jnp.float32)
        result, pull_back = jax.vjp(forward, params, block)
        grad_params, grad_block = pull_back(cot_block * span_mask[:, None])
        grad_total = jax.tree.map(jnp.add, grad_total, grad_params)
        return (grad_total, (result.astype(jnp.bfloat16), grad_block.astype(jnp.bfloat16)))
    zeros_init = tuple((jnp.zeros_like(member) for member in params))
    grads, (seq_outs, seq_grads) = lax.scan(scan_step, zeros_init, (blocks, cot_blocks, span_table))
    return (seq_outs.reshape(TOKENS, D), seq_grads.reshape(TOKENS, D), grads[0], grads[1], grads[2], grads[3], grads[4], grads[5], grads[6], grads[7], grads[8], grads[9], grads[10], grads[11], grads[12], grads[13], grads[14])
```

```python
import functools

import jax
import jax.numpy as jnp
from jax import lax
from jax.experimental import pallas as pl
from jax.experimental.pallas import tpu as pltpu
from jax.sharding import PartitionSpec as P

HD = 64
WIN = 128
EPS = 1e-06
SMALL = 16
MIB = 1 << 20

bf16 = jnp.bfloat16
f32 = jnp.float32


def mm(left, right):
    return lax.dot_general(left, right, (((1,), (0,)), ((), ())), preferred_element_type=f32)


def mm_nt(left, right):
    return lax.dot_general(left, right, (((1,), (1,)), ((), ())), preferred_element_type=f32)


def mm_tn(left, right):
    return lax.dot_general(left, right, (((0,), (0,)), ((), ())), preferred_element_type=f32)


def unit_of(values):
    centered = values - jnp.mean(values, -1, keepdims=True)
    rstd = lax.rsqrt(jnp.mean(centered * centered, -1, keepdims=True) + EPS)
    return centered * rstd, rstd


def norm_back(grad_norm, unit, rstd, gain):
    scaled = grad_norm * gain
    return rstd * (
        scaled
        - jnp.mean(scaled, -1, keepdims=True)
        - unit * jnp.mean(scaled * unit, -1, keepdims=True)
    )


def window_of(span_ref, seq, length):
    start = span_ref[seq, 0]
    count = span_ref[seq, 1]
    first = jnp.minimum(start, length - WIN)
    row = lax.broadcasted_iota(jnp.int32, (WIN, length), 0) + first
    col = lax.broadcasted_iota(jnp.int32, (WIN, length), 1)
    pick = row == col
    inside = pick & (row >= start) & (row < start + count)
    return pick.astype(f32).astype(bf16), inside.astype(f32).astype(bf16)


def softmax_parts(query, keys):
    scores = mm_nt(query, keys) * 0.125
    terms = jnp.exp(scores - jnp.max(scores, -1, keepdims=True))
    return terms, 1.0 / jnp.sum(terms, -1, keepdims=True)


def attend(query, keys, values):
    heads = []
    for h in range(keys.shape[1] // HD):
        cols = slice(h * HD, (h + 1) * HD)
        terms, inverse = softmax_parts(query[:, cols], keys[:, cols])
        heads.append(mm(terms.astype(bf16), values[:, cols]) * inverse)
    return jnp.concatenate(heads, 1).astype(bf16)


def attend_back(query, keys, values, grad_mixed):
    grad_q, grad_k, grad_v = [], [], []
    for h in range(keys.shape[1] // HD):
        cols = slice(h * HD, (h + 1) * HD)
        q, k, v, g = query[:, cols], keys[:, cols], values[:, cols], grad_mixed[:, cols]
        terms, inverse = softmax_parts(q, k)
        prob = terms * inverse
        grad_prob = mm_nt(g, v)
        row_dot = jnp.sum(prob * grad_prob, -1, keepdims=True)
        grad_scores = (prob * (grad_prob - row_dot)).astype(bf16)
        grad_q.append(mm(grad_scores, k) * 0.125)
        grad_k.append(mm_tn(grad_scores, q) * 0.125)
        grad_v.append(mm_tn(prob.astype(bf16), g))
    return tuple(jnp.concatenate(part, 1).astype(bf16) for part in (grad_q, grad_k, grad_v))


def gelu_parts(values):
    phi = 0.5 * (1.0 + lax.erf(values * 0.7071067811865476))
    return phi


def first_kernel(
    span_ref, x_ref, cot_ref, gain_ref, shift_ref, wq_ref, wk_ref, wv_ref, bq_ref, bv_ref,
    normed_ref, xw_ref, gw_ref, nw_ref, qw_ref, k_ref, v_ref, mw_ref,
):
    length = x_ref.shape[0]
    x = x_ref[...]
    unit, _ = unit_of(x.astype(f32))
    normed = (unit * gain_ref[...].astype(f32) + shift_ref[...].astype(f32)).astype(bf16)
    normed_ref[...] = normed
    pick, inside = window_of(span_ref, pl.program_id(0), length)
    xw_ref[...] = mm(pick, x).astype(bf16)
    gw_ref[...] = mm(inside, cot_ref[...]).astype(bf16)
    nw = mm(pick, normed).astype(bf16)
    nw_ref[...] = nw
    query = (mm(nw, wq_ref[...]) + bq_ref[...].astype(f32)).astype(bf16)
    keys = mm(normed, wk_ref[...]).astype(bf16)
    values = (mm(normed, wv_ref[...]) + bv_ref[...].astype(f32)).astype(bf16)
    qw_ref[...] = query
    k_ref[...] = keys
    v_ref[...] = values
    mw_ref[...] = attend(query, keys, values)


def ffn_kernel(
    ids_ref, m0_ref, m1_ref, m2_ref, m3_ref, wo0_ref, wo_mine_ref, wo_other_ref, xw_ref, gw_ref,
    bout_ref, gain_ref, shift_ref, wup_ref, bup_ref, wdown_ref,
    keep_ref, send_ref, p0_ref, p1_ref, p2_ref, p3_ref, resid_ref, gown_ref, small_ref,
    wo_s, resid_s, part_s,
):
    own, core, parts = ids_ref[0], ids_ref[1], ids_ref[3]
    half = wo_mine_ref.shape[1]
    for i in range(3):
        wo_s[i, pl.ds(pl.multiple_of(core * half, 16), half), :] = wo_mine_ref[i]
        wo_s[i, pl.ds(pl.multiple_of((1 - core) * half, 16), half), :] = wo_other_ref[i]
    branch = mm(m0_ref[...], wo0_ref[...])
    for i, m_ref in enumerate((m1_ref, m2_ref, m3_ref)):
        branch += mm(m_ref[...], wo_s[i])
    resid = xw_ref[...].astype(f32) + (branch + bout_ref[...].astype(f32))
    resid_s[...] = resid
    unit, _ = unit_of(resid)
    normed = (unit * gain_ref[...].astype(f32) + shift_ref[...].astype(f32)).astype(bf16)
    pre = mm(normed, wup_ref[...]) + bup_ref[...].astype(f32)
    phi = gelu_parts(pre)
    hidden = (pre * phi).astype(bf16)
    slope = phi + pre * (0.3989422804014327 * jnp.exp(-0.5 * pre * pre))
    grad_out = gw_ref[...]
    grad_pre = (slope * mm_nt(grad_out, wdown_ref[...])).astype(bf16)
    grad_up = mm_tn(normed, grad_pre).astype(bf16)
    grad_down = mm_tn(hidden, grad_out).astype(bf16)

    @pl.when(core == 0)
    def _():
        keep_ref[...] = grad_up
        send_ref[...] = grad_down

    @pl.when(core == 1)
    def _():
        keep_ref[...] = grad_down
        send_ref[...] = grad_up

    part_s[...] = mm_nt(grad_pre, wup_ref[...])
    for r, p_ref in enumerate((p0_ref, p1_ref, p2_ref, p3_ref)):
        rows = pl.ds(pl.multiple_of(lax.rem(own + r, parts) * WIN, WIN), WIN)
        p_ref[...] = part_s[rows, :].astype(bf16)
    rows = pl.ds(pl.multiple_of(own * WIN, WIN), WIN)
    resid_ref[...] = resid_s[rows, :]
    gown_ref[...] = gw_ref[rows, :]
    small_ref[...] = jnp.zeros_like(small_ref)
    small_ref[0:1, :] = jnp.sum(grad_pre.astype(f32), 0, keepdims=True)
    small_ref[1:2, :] = jnp.sum(grad_out.astype(f32), 0, keepdims=True)


def norm_two_kernel(p0_ref, p1_ref, p2_ref, p3_ref, resid_ref, gown_ref, gain_ref, gresid_ref, gb_ref):
    grad_norm = p0_ref[...].astype(f32)
    for p_ref in (p1_ref, p2_ref, p3_ref):
        grad_norm += p_ref[...].astype(f32)
    unit, rstd = unit_of(resid_ref[...])
    grad = gown_ref[...].astype(f32) + norm_back(grad_norm, unit, rstd, gain_ref[...].astype(f32))
    gresid_ref[...] = grad
    gb_ref[0:WIN, :] = grad.astype(bf16)
    sums = [jnp.sum(grad_norm * unit, 0, keepdims=True), jnp.sum(grad_norm, 0, keepdims=True)]
    sums.append(jnp.zeros((SMALL - 2, grad.shape[1]), f32))
    gb_ref[WIN : WIN + SMALL, :] = jnp.concatenate(sums, 0).astype(bf16)


def attn_kernel(
    ids_ref, g0_ref, g1_ref, g2_ref, g3_ref, mw_ref, nw_ref, qw_ref, k_ref, v_ref, normed_ref,
    wq_ref, wk_ref, wv_ref, wo_ref, gain_ref, shift_ref, ffn_small_ref,
    keep_ref, send_ref, gb_s, acc_s, col_s,
):
    step = pl.program_id(0)
    width = wq_ref.shape[1]

    @pl.when(step == 0)
    def _():
        for i, g_ref in enumerate((g0_ref, g1_ref, g2_ref, g3_ref)):
            gb_s[i] = g_ref[...]
        acc_s[...] = jnp.zeros_like(acc_s)
        col_s[...] = jnp.zeros_like(col_s)

    block = gb_s[step]
    grad_branch = block[0:WIN]
    grad_mixed = mm_nt(grad_branch, wo_ref[...]).astype(bf16)
    grad_q, grad_k, grad_v = attend_back(qw_ref[...], k_ref[...], v_ref[...], grad_mixed)
    normed = normed_ref[...]
    acc_s[0] += mm_tn(grad_q, nw_ref[...])
    acc_s[1] += mm_tn(grad_k, normed)
    acc_s[2] += mm_tn(grad_v, normed)
    acc_s[3] += mm_tn(mw_ref[...], grad_branch)
    for i, grad in enumerate((grad_q, grad_k, grad_v)):
        col_s[i : i + 1, 0:width] += jnp.sum(grad.astype(f32), 0, keepdims=True)
    col_s[3:4, :] += jnp.sum(grad_branch.astype(f32), 0, keepdims=True)
    col_s[4:6, :] += block[WIN : WIN + 2].astype(f32)

    @pl.when(step == pl.num_programs(0) - 1)
    def _():
        core = ids_ref[1]
        eye = (
            lax.broadcasted_iota(jnp.int32, (width, width), 0)
            == lax.broadcasted_iota(jnp.int32, (width, width), 1)
        )
        eye = eye.astype(f32).astype(bf16)
        sums = jnp.zeros((1, gb_s.shape[2]), f32)
        cols = jnp.zeros((1, gb_s.shape[2]), f32)
        for i, w_ref in enumerate((wq_ref, wk_ref, wv_ref)):
            turned = mm_nt(eye, w_ref[...])
            sums += jnp.sum(turned * acc_s[i], 0, keepdims=True)
            total = col_s[i : i + 1, 0:width]
            high = total.astype(bf16)
            low = (total - high.astype(f32)).astype(bf16)
            both = jnp.concatenate([high, low, jnp.zeros((14, width), bf16)], 0)
            cols += jnp.sum(mm_nt(both, w_ref[...]), 0, keepdims=True)
        gain = (sums - shift_ref[...].astype(f32) * cols) / gain_ref[...].astype(f32)
        small = jnp.concatenate(
            [ffn_small_ref[0:2, :], col_s[3:6, :], gain, cols, col_s[0:1, :], col_s[2:3, :],
             jnp.zeros((SMALL - 9, gb_s.shape[2]), f32)], 0
        ).astype(bf16)
        first = jnp.concatenate([acc_s[0], acc_s[1]], 0).astype(bf16)
        second = jnp.concatenate([acc_s[2], acc_s[3]], 0).astype(bf16)
        rows = first.shape[0]
        keep_ref[rows : rows + SMALL, :] = small
        send_ref[rows : rows + SMALL, :] = small

        @pl.when(core == 0)
        def _():
            keep_ref[0:rows, :] = first
            send_ref[0:rows, :] = second

        @pl.when(core == 1)
        def _():
            keep_ref[0:rows, :] = second
            send_ref[0:rows, :] = first


def split_kernel(small, ids_ref, keep_ref, recv_ref, own_ref, *out_refs):
    chip = ids_ref[2]
    rows = (keep_ref.shape[0] - small) // 4
    outs = (own_ref,) + out_refs
    for flip, out_ref in enumerate(outs):
        part = pl.ds(pl.multiple_of((chip ^ flip) * rows, 16), rows)
        total = keep_ref[part, :].astype(f32) + recv_ref[part, :].astype(f32)
        out_ref[0:rows, :] = total.astype(out_ref.dtype)
    if small:
        part = slice(4 * rows, 4 * rows + small)
        total = keep_ref[part, :].astype(f32) + recv_ref[part, :].astype(f32)
        for out_ref in outs:
            out_ref[rows : rows + small, :] = total.astype(out_ref.dtype)


def total_kernel(own_ref, a_ref, b_ref, c_ref, out_ref, *small_refs):
    total = own_ref[...]
    for ref in (a_ref, b_ref, c_ref):
        total += ref[...].astype(f32)
    rows = out_ref.shape[0]
    out_ref[...] = total[0:rows].astype(bf16)
    if small_refs:
        small_refs[0][...] = total[rows:]


def place_kernel(ids_ref, *refs):
    chip = ids_ref[2]
    out_ref = refs[-1]
    rows = refs[0].shape[0]
    for flip, ref in enumerate(refs[:-1]):
        out_ref[pl.ds(pl.multiple_of((chip ^ flip) * rows, 16), rows), :] = ref[...]


def ffn_out_kernel(ids_ref, mine_ref, other_ref, up_ref, down_ref):
    core = ids_ref[1]

    @pl.when(core == 0)
    def _():
        up_ref[...] = mine_ref[...].astype(f32)
        down_ref[...] = other_ref[...].astype(f32)

    @pl.when(core == 1)
    def _():
        up_ref[...] = other_ref[...].astype(f32)
        down_ref[...] = mine_ref[...].astype(f32)


def attn_out_kernel(ids_ref, mine_ref, other_ref, q_ref, k_ref, v_ref, o_ref):
    core = ids_ref[1]
    width = o_ref.shape[0]

    def write(first_ref, second_ref):
        q_ref[...] = first_ref[0:width, :].astype(f32).T
        k_ref[...] = first_ref[width : 2 * width, :].astype(f32).T
        v_ref[...] = second_ref[0:width, :].astype(f32).T
        o_ref[...] = second_ref[width : 2 * width, :].astype(f32)

    pl.when(core == 0)(lambda: write(mine_ref, other_ref))
    pl.when(core == 1)(lambda: write(other_ref, mine_ref))


def load_pieces(pieces, arrays, ids_ref, first_col, buffer, sems, rel, start):
    width = buffer.shape[-1]
    number = 0
    for array, row, source, part, flip_bit, flip_core in pieces:
        if source != rel:
            continue
        rows = 96
        bit = ids_ref[4 + part] ^ flip_bit
        core = ids_ref[1] ^ flip_core
        place = pl.multiple_of(part * (4 * rows) + (bit * 2 + core) * rows, 16)
        copy = pltpu.make_async_copy(
            arrays[array].at[pl.ds(row, rows), pl.ds(first_col, width)],
            buffer.at[rel, pl.ds(place, rows), :],
            sems.at[rel, number],
        )
        number += 1
        if start:
            copy.start()
        else:
            copy.wait()


def load_bias(arrays, where, first_col, buffer, sems, rel, start):
    array, row = where[rel]
    copy = pltpu.make_async_copy(
        arrays[array].at[pl.ds(row, SMALL), pl.ds(first_col, buffer.shape[-1])],
        buffer.at[rel],
        sems.at[rel],
    )
    if start:
        copy.start()
    else:
        copy.wait()


def local_attn_kernel(
    layout, ids_ref, x_ref, normed_ref, wqkv_ref, wo0_ref, wo_mine_ref, wo_other_ref, bout_ref,
    gain_ref, shift_ref, *refs,
):
    arrays = refs[: layout.count]
    qkv_ref, wo_ref, resid_ref, normed_two_ref = refs[layout.count : layout.count + 4]
    w_s, b_s, acc_s, w_sem, b_sem, own_sem = refs[layout.count + 4 :]
    step = pl.program_id(0)
    width = wo0_ref.shape[0]
    half = wo_mine_ref.shape[1]
    own_copy = pltpu.make_async_copy(wqkv_ref, w_s.at[0], own_sem)

    @pl.when(step == 0)
    def _():
        own_copy.start()
        for rel in range(4):
            load_bias(arrays, layout.bias, layout.qkv_col, b_s, b_sem, rel, True)
        for rel in range(1, 4):
            load_pieces(layout.pieces, arrays, ids_ref, layout.qkv_col, w_s, w_sem, rel, True)
        acc_s[...] = x_ref[...].astype(f32) + bout_ref[...].astype(f32)
        own_copy.wait()
        wo_ref[...] = wo0_ref[...]

    for rel in range(1, 4):

        @pl.when(step == rel)
        def _(rel=rel):
            load_pieces(layout.pieces, arrays, ids_ref, layout.qkv_col, w_s, w_sem, rel, False)
            core = ids_ref[1]
            wo_ref[pl.ds(pl.multiple_of(core * half, 16), half), :] = wo_mine_ref[rel - 1]
            wo_ref[pl.ds(pl.multiple_of((1 - core) * half, 16), half), :] = wo_other_ref[rel - 1]

    for rel in range(4):

        @pl.when(step == rel)
        def _(rel=rel):
            load_bias(arrays, layout.bias, layout.qkv_col, b_s, b_sem, rel, False)

    qkv = (mm(normed_ref[...], w_s[step]) + b_s[step][0:1, :].astype(f32)).astype(bf16)
    qkv_ref[...] = qkv
    mixed = attend(qkv[:, 0:width], qkv[:, width : 2 * width], qkv[:, 2 * width : 3 * width])
    acc_s[...] += mm(mixed, wo_ref[...])

    @pl.when(step == 3)
    def _():
        resid = acc_s[...]
        resid_ref[...] = resid
        unit, _ = unit_of(resid)
        normed_two_ref[...] = (
            unit * gain_ref[...].astype(f32) + shift_ref[...].astype(f32)
        ).astype(bf16)


def local_ffn_kernel(
    layout, ids_ref, resid_ref, normed_ref, wup_ref, wdown_ref, bdown_ref, *refs
):
    arrays = refs[: layout.count]
    out_ref = refs[layout.count]
    up_s, down_s, b_s, acc_s, up_sem, down_sem, b_sem, own_sem = refs[layout.count + 1 :]
    step = pl.program_id(0)
    own_up = pltpu.make_async_copy(wup_ref, up_s.at[0], own_sem.at[0])
    own_down = pltpu.make_async_copy(wdown_ref, down_s.at[0], own_sem.at[1])

    @pl.when(step == 0)
    def _():
        own_up.start()
        for rel in range(4):
            load_bias(arrays, layout.bias, layout.up_col, b_s, b_sem, rel, True)
        own_down.start()
        for rel in range(1, 4):
            load_pieces(layout.pieces, arrays, ids_ref, layout.up_col, up_s, up_sem, rel, True)
            load_pieces(layout.pieces, arrays, ids_ref, layout.down_col, down_s, down_sem, rel, True)
        acc_s[...] = resid_ref[...] + bdown_ref[...].astype(f32)
        own_up.wait()
        own_down.wait()

    for rel in range(4):

        @pl.when(step == rel)
        def _(rel=rel):
            load_bias(arrays, layout.bias, layout.up_col, b_s, b_sem, rel, False)
            if rel:
                load_pieces(layout.pieces, arrays, ids_ref, layout.up_col, up_s, up_sem, rel, False)
                load_pieces(
                    layout.pieces, arrays, ids_ref, layout.down_col, down_s, down_sem, rel, False
                )

    pre = mm(normed_ref[...], up_s[step]) + b_s[step][0:1, :].astype(f32)
    hidden = (pre * gelu_parts(pre)).astype(bf16)
    acc_s[...] += mm(hidden, down_s[step])

    @pl.when(step == 3)
    def _():
        out_ref[...] = acc_s[...].astype(bf16)


def local_back_kernel(
    layout, span_ref, ids_ref, x_ref, gresid_ref, gb_ref, qkv_ref, wo_ref, wqkv_ref, gain_ref, *refs
):
    arrays = refs[: layout.count]
    out_ref = refs[layout.count]
    w_s, acc_s, w_sem, own_sem = refs[layout.count + 1 :]
    step = pl.program_id(0)
    length = x_ref.shape[0]
    width = wo_ref.shape[0]
    own_copy = pltpu.make_async_copy(wqkv_ref, w_s.at[0], own_sem)

    @pl.when(step == 0)
    def _():
        own_copy.start()
        for rel in range(1, 4):
            load_pieces(layout.pieces, arrays, ids_ref, layout.qkv_col, w_s, w_sem, rel, True)
        acc_s[...] = jnp.zeros_like(acc_s)
        own_copy.wait()

    for rel in range(1, 4):

        @pl.when(step == rel)
        def _(rel=rel):
            load_pieces(layout.pieces, arrays, ids_ref, layout.qkv_col, w_s, w_sem, rel, False)

    pick, _ = window_of(span_ref, ids_ref[0], length)
    qkv = qkv_ref[...]
    query = mm(pick, qkv[:, 0:width]).astype(bf16)
    grad_mixed = mm_nt(gb_ref[0:WIN, :], wo_ref[...]).astype(bf16)
    grad_q, grad_k, grad_v = attend_back(
        query, qkv[:, width : 2 * width], qkv[:, 2 * width : 3 * width], grad_mixed
    )
    grad_q = mm_tn(pick, grad_q).astype(bf16)
    grads = jnp.concatenate(
        [grad_q, grad_k, grad_v, jnp.zeros((length, w_s.shape[2] - 3 * width), bf16)], 1
    )
    acc_s[...] += mm_nt(grads, w_s[step])

    @pl.when(step == 3)
    def _():
        unit, rstd = unit_of(x_ref[...].astype(f32))
        grad = norm_back(acc_s[...], unit, rstd, gain_ref[...].astype(f32))
        resid = gresid_ref[...]
        high = resid.astype(bf16)
        low = (resid - high.astype(f32)).astype(bf16)
        out_ref[...] = (grad + mm_tn(pick, high) + mm_tn(pick, low)).astype(bf16)


class Layout:
    def __init__(self, count, pieces, bias, up_col, qkv_col, down_col):
        self.count = count
        self.pieces = pieces
        self.bias = bias
        self.up_col = up_col
        self.qkv_col = qkv_col
        self.down_col = down_col


def sds(shape, dtype):
    return jax.ShapeDtypeStruct(shape, dtype)


def params(mib=48):
    return pltpu.CompilerParams(vmem_limit_bytes=mib * MIB)


SMEM = pl.BlockSpec(memory_space=pltpu.SMEM)
VMEM = pl.BlockSpec(memory_space=pltpu.VMEM)
ANY = pl.BlockSpec(memory_space=pl.ANY)


def local(
    dp_size, mp_size, inputs, cotangent, span_table, ln1_gain, ln1_shift, w_query, b_query, w_key,
    w_value, b_value, w_out, b_out, ln2_gain, ln2_shift, w_up, b_up, w_down, b_down,
):
    tok_rows, model = inputs.shape
    seqs = span_table.shape[0]
    length = tok_rows // seqs
    width = w_query.shape[1]
    units = w_up.shape[1]
    dp_bits = dp_size.bit_length() - 1
    bit_x, bit_y = 1, dp_bits - 1
    dp_idx = lax.axis_index("dp")
    own = lax.axis_index("mp")
    core = dp_idx & 1
    at_x = (dp_idx >> bit_x) & 1
    at_y = (dp_idx >> bit_y) & 1
    ids = jnp.stack([own, core, at_y * 2 + at_x, jnp.int32(mp_size), at_x, at_y]).astype(jnp.int32)

    def from_rel(value, rel):
        return lax.ppermute(value, "mp", [(i, (i - rel) % mp_size) for i in range(mp_size)])

    def to_rel(value, rel):
        return from_rel(value, -rel)

    def swap(value, bits):
        return lax.ppermute(value, "dp", [(i, i ^ bits) for i in range(dp_size)])

    core_bit, x_bit, y_bit = 1, 1 << bit_x, 1 << bit_y

    def row(vector):
        return vector.reshape(1, -1)

    gain_one, shift_one = row(ln1_gain), row(ln1_shift)
    gain_two, shift_two = row(ln2_gain), row(ln2_shift)

    half = width // 2
    wo_half = lax.dynamic_slice_in_dim(w_out, core * half, half, 0)
    wo_mine = jnp.stack([from_rel(wo_half, rel) for rel in (1, 2, 3)])
    wo_other = swap(wo_mine, core_bit)

    def seq_rows(rows, cols):
        return pl.BlockSpec((rows, cols), lambda i, *_: (i, 0))

    def whole(array):
        return pl.BlockSpec(array.shape, lambda i, *_: (0,) * array.ndim)

    bq, bv = row(b_query), row(b_value)
    normed, xw, gw, nw, qw, keys, values, mw = pl.pallas_call(
        first_kernel,
        grid_spec=pltpu.PrefetchScalarGridSpec(
            num_scalar_prefetch=1,
            grid=(seqs,),
            in_specs=[seq_rows(length, model), seq_rows(length, model)]
            + [whole(a) for a in (gain_one, shift_one, w_query, w_key, w_value, bq, bv)],
            out_specs=[
                seq_rows(length, model),
                seq_rows(WIN, model),
                seq_rows(WIN, model),
                seq_rows(WIN, model),
                seq_rows(WIN, width),
                seq_rows(length, width),
                seq_rows(length, width),
                seq_rows(WIN, width),
            ],
        ),
        out_shape=[
            sds((tok_rows, model), bf16),
            sds((seqs * WIN, model), bf16),
            sds((seqs * WIN, model), bf16),
            sds((seqs * WIN, model), bf16),
            sds((seqs * WIN, width), bf16),
            sds((tok_rows, width), bf16),
            sds((tok_rows, width), bf16),
            sds((seqs * WIN, width), bf16),
        ],
        compiler_params=params(),
        name="windows_forward",
    )(span_table, inputs, cotangent, gain_one, shift_one, w_query, w_key, w_value, bq, bv)

    mixed_parts = [mw] + [from_rel(mw, rel) for rel in (1, 2, 3)]

    win_rows = seqs * WIN
    keep, send, p0, p1, p2, p3, resid_own, gown, ffn_small = pl.pallas_call(
        ffn_kernel,
        in_specs=[SMEM] + [VMEM] * 15,
        out_specs=[VMEM] * 9,
        out_shape=[sds((model, units), bf16)] * 2
        + [sds((WIN, model), bf16)] * 4
        + [sds((WIN, model), f32), sds((WIN, model), bf16), sds((8, model), f32)],
        scratch_shapes=[
            pltpu.VMEM((3, width, model), bf16),
            pltpu.VMEM((win_rows, model), f32),
            pltpu.VMEM((win_rows, model), f32),
        ],
        compiler_params=params(),
        name="windows_ffn",
    )(ids, *mixed_parts, w_out, wo_mine, wo_other, xw, gw, row(b_out), gain_two, shift_two, w_up,
      row(b_up), w_down)

    def sum_start(keep, send, small, name):
        recv = swap(send, core_bit)
        rows = (keep.shape[0] - small) // 4 + small
        return pl.pallas_call(
            functools.partial(split_kernel, small),
            in_specs=[SMEM, VMEM, VMEM],
            out_specs=[VMEM] * 4,
            out_shape=[sds((rows, model), f32)] + [sds((rows, model), bf16)] * 3,
            compiler_params=params(),
            name=name + "_split",
        )(ids, keep, recv)

    def sum_middle(parts, small, name):
        own_part, to_x, to_y, to_xy = parts
        rows = own_part.shape[0] - small
        outs = [sds((rows, model), bf16)] + ([sds((small, model), f32)] if small else [])
        got = (swap(to_x, x_bit), swap(to_y, y_bit), swap(to_xy, x_bit | y_bit))
        result = pl.pallas_call(
            total_kernel,
            in_specs=[VMEM] * 4,
            out_specs=[VMEM] * len(outs),
            out_shape=outs,
            compiler_params=params(),
            name=name + "_total",
        )(own_part, *got)
        done = result[0]
        rest = result[1] if small else None
        for bit in range(2, dp_bits - 1):
            done = (done.astype(f32) + swap(done, 1 << bit).astype(f32)).astype(bf16)
            if small:
                rest = rest + swap(rest, 1 << bit)
        return done, rest

    def sum_end(done, name):
        parts = (done, swap(done, x_bit), swap(done, y_bit), swap(done, x_bit | y_bit))
        mine = pl.pallas_call(
            place_kernel,
            in_specs=[SMEM] + [VMEM] * 4,
            out_specs=VMEM,
            out_shape=sds((4 * done.shape[0], model), bf16),
            compiler_params=params(),
            name=name + "_place",
        )(ids, *parts)
        return mine, swap(mine, core_bit)

    ffn_done, _ = sum_middle(sum_start(keep, send, 0, "ffn"), 0, "ffn")
    ffn_mine, ffn_other = sum_end(ffn_done, "ffn")
    grad_w_up, grad_w_down = pl.pallas_call(
        ffn_out_kernel,
        in_specs=[SMEM, VMEM, VMEM],
        out_specs=[VMEM] * 2,
        out_shape=[sds((model, units), f32), sds((units, model), f32)],
        compiler_params=params(),
        name="ffn_gradients",
    )(ids, ffn_mine, ffn_other)

    got = [to_rel(p, rel) for p, rel in ((p1, 1), (p2, 2), (p3, 3))]
    gresid, gb = pl.pallas_call(
        norm_two_kernel,
        in_specs=[VMEM] * 7,
        out_specs=[VMEM] * 2,
        out_shape=[sds((WIN, model), f32), sds((WIN + SMALL, model), bf16)],
        compiler_params=params(),
        name="windows_norm_back",
    )(p0, *got, resid_own, gown, gain_two)
    gb_parts = [gb] + [from_rel(gb, rel) for rel in (1, 2, 3)]

    def rel_rows(rows, cols):
        return pl.BlockSpec((rows, cols), lambda i, ids: (lax.rem(ids[0] + i, ids[3]), 0))

    att_rows = 2 * width + SMALL
    keep, send = pl.pallas_call(
        attn_kernel,
        grid_spec=pltpu.PrefetchScalarGridSpec(
            num_scalar_prefetch=1,
            grid=(seqs,),
            in_specs=[whole(g) for g in gb_parts]
            + [
                rel_rows(WIN, width),
                rel_rows(WIN, model),
                rel_rows(WIN, width),
                rel_rows(length, width),
                rel_rows(length, width),
                rel_rows(length, model),
            ]
            + [whole(a) for a in (w_query, w_key, w_value, w_out, gain_one, shift_one, ffn_small)],
            out_specs=[pl.BlockSpec((att_rows, model), lambda i, *_: (0, 0))] * 2,
            scratch_shapes=[
                pltpu.VMEM((seqs, WIN + SMALL, model), bf16),
                pltpu.VMEM((4, width, model), f32),
                pltpu.VMEM((8, model), f32),
            ],
        ),
        out_shape=[sds((att_rows, model), bf16)] * 2,
        compiler_params=params(),
        name="windows_attention_back",
    )(ids, *gb_parts, mw, nw, qw, keys, values, normed, w_query, w_key, w_value, w_out, gain_one,
      shift_one, ffn_small)

    att_done, small = sum_middle(sum_start(keep, send, SMALL, "att"), SMALL, "att")
    norm_rows = small[5:7]
    norm_sums = norm_rows + sum(from_rel(norm_rows, rel) for rel in (1, 2, 3))
    att_mine, att_other = sum_end(att_done, "att")
    grad_w_query, grad_w_key, grad_w_value, grad_w_out = pl.pallas_call(
        attn_out_kernel,
        in_specs=[SMEM, VMEM, VMEM],
        out_specs=[VMEM] * 4,
        out_shape=[sds((model, width), f32)] * 3 + [sds((width, model), f32)],
        compiler_params=params(),
        name="attention_gradients",
    )(ids, att_mine, att_other)

    qkv_cols = -(-3 * width // 128) * 128
    pad = qkv_cols - 3 * width
    wqkv = jnp.concatenate([w_query, w_key, w_value, jnp.zeros((model, pad), bf16)], 1)
    piece = model // 8

    def packed(first):
        return jnp.concatenate(
            [lax.dynamic_slice_in_dim(w, first, piece, 0) for w in (w_up, wqkv, w_down)], 1
        )

    bias_row = jnp.concatenate(
        [b_up, b_query, jnp.zeros((width,), bf16), b_value, jnp.zeros((pad + model,), bf16)]
    )
    bias_own = jnp.concatenate(
        [row(bias_row), jnp.zeros((SMALL - 1, bias_row.shape[0]), bf16)], 0
    )
    piece_p = packed((at_x * 2 + core) * piece)
    piece_q = packed(4 * piece + (at_y * 2 + core) * piece)
    message = jnp.concatenate([piece_p, bias_own, piece_q], 0)
    got3 = from_rel(message, 3)
    got1 = from_rel(message, 1)
    got2p = from_rel(got3[: piece + SMALL], 3)
    got2q = from_rel(got1[piece + SMALL :], 1)
    over_x = swap(jnp.concatenate([got3[:piece], got1[:piece], got2p[:piece]], 0), x_bit)
    over_y = swap(jnp.concatenate([got3[piece + SMALL :], got1[piece + SMALL :], got2q], 0), y_bit)
    arrays = [bias_own, got3, got1, got2p, got2q, over_x, over_y]
    arrays += [swap(a, core_bit) for a in arrays[1:]]
    pieces = []
    for flip_core, base in ((0, 0), (1, 6)):
        pieces += [
            (1 + base, 0, 3, 0, 0, flip_core),
            (1 + base, piece + SMALL, 3, 1, 0, flip_core),
            (2 + base, 0, 1, 0, 0, flip_core),
            (2 + base, piece + SMALL, 1, 1, 0, flip_core),
            (3 + base, 0, 2, 0, 0, flip_core),
            (4 + base, 0, 2, 1, 0, flip_core),
        ]
        for i, rel in enumerate((3, 1, 2)):
            pieces.append((5 + base, i * piece, rel, 0, 1, flip_core))
            pieces.append((6 + base, i * piece, rel, 1, 1, flip_core))
    bias_at = {0: (0, 0), 3: (1, piece), 1: (2, piece), 2: (3, piece)}
    layout = Layout(len(arrays), pieces, bias_at, 0, units, units + qkv_cols)

    own_rows = pl.BlockSpec((length, model), lambda i, ids, *_: (ids[0], 0))

    dma = pltpu.SemaphoreType.DMA
    qkv, wo_all, resid, normed_two = pl.pallas_call(
        functools.partial(local_attn_kernel, layout),
        grid_spec=pltpu.PrefetchScalarGridSpec(
            num_scalar_prefetch=1,
            grid=(4,),
            in_specs=[own_rows, own_rows, ANY, whole(w_out), whole(wo_mine), whole(wo_other)]
            + [whole(a) for a in (row(b_out), gain_two, shift_two)]
            + [ANY] * layout.count,
            out_specs=[
                pl.BlockSpec((None, length, qkv_cols), lambda i, *_: (i, 0, 0)),
                pl.BlockSpec((None, width, model), lambda i, *_: (i, 0, 0)),
                pl.BlockSpec((length, model), lambda i, *_: (0, 0)),
                pl.BlockSpec((length, model), lambda i, *_: (0, 0)),
            ],
            scratch_shapes=[
                pltpu.VMEM((4, model, qkv_cols), bf16),
                pltpu.VMEM((4, SMALL, qkv_cols), bf16),
                pltpu.VMEM((length, model), f32),
                dma((4, 8)),
                dma((4,)),
                dma,
            ],
        ),
        out_shape=[
            sds((4, length, qkv_cols), bf16),
            sds((4, width, model), bf16),
            sds((length, model), f32),
            sds((length, model), bf16),
        ],
        compiler_params=params(),
        name="own_attention",
    )(ids, inputs, normed, wqkv, w_out, wo_mine, wo_other, row(b_out), gain_two, shift_two, *arrays)

    layer_out = pl.pallas_call(
        functools.partial(local_ffn_kernel, layout),
        grid_spec=pltpu.PrefetchScalarGridSpec(
            num_scalar_prefetch=1,
            grid=(4,),
            in_specs=[whole(resid), whole(normed_two), ANY, ANY, whole(row(b_down))]
            + [ANY] * layout.count,
            out_specs=pl.BlockSpec((length, model), lambda i, *_: (0, 0)),
            scratch_shapes=[
                pltpu.VMEM((4, model, units), bf16),
                pltpu.VMEM((4, units, model), bf16),
                pltpu.VMEM((4, SMALL, units), bf16),
                pltpu.VMEM((length, model), f32),
                dma((4, 8)),
                dma((4, 8)),
                dma((4,)),
                dma((2,)),
            ],
        ),
        out_shape=sds((length, model), bf16),
        compiler_params=params(),
        name="own_ffn",
    )(ids, resid, normed_two, w_up, w_down, row(b_down), *arrays)

    grad_inputs = pl.pallas_call(
        functools.partial(local_back_kernel, layout),
        grid_spec=pltpu.PrefetchScalarGridSpec(
            num_scalar_prefetch=2,
            grid=(4,),
            in_specs=[
                pl.BlockSpec((length, model), lambda i, span, ids: (ids[0], 0)),
                whole(gresid),
                whole(gb),
                pl.BlockSpec((None, length, qkv_cols), lambda i, *_: (i, 0, 0)),
                pl.BlockSpec((None, width, model), lambda i, *_: (i, 0, 0)),
                ANY,
                whole(gain_one),
            ]
            + [ANY] * layout.count,
            out_specs=pl.BlockSpec((length, model), lambda i, *_: (0, 0)),
            scratch_shapes=[
                pltpu.VMEM((4, model, qkv_cols), bf16),
                pltpu.VMEM((length, model), f32),
                dma((4, 8)),
                dma,
            ],
        ),
        out_shape=sds((length, model), bf16),
        compiler_params=params(),
        name="own_attention_back",
    )(span_table, ids, inputs, gresid, gb, qkv, wo_all, wqkv, gain_one, *arrays)

    return (
        layer_out,
        grad_inputs,
        norm_sums[0],
        norm_sums[1],
        grad_w_query,
        small[7, :width],
        grad_w_key,
        grad_w_value,
        small[8, :width],
        grad_w_out,
        small[2],
        small[3],
        small[4],
        grad_w_up,
        small[0],
        grad_w_down,
        small[1],
    )


def solution(mesh):
    return jax.shard_map(
        functools.partial(local, mesh.shape["dp"], mesh.shape["mp"]),
        mesh=mesh,
        in_specs=(
            P("dp", None),
            P("dp", None),
            P("dp", None),
            P(),
            P(),
            P(None, "mp"),
            P("mp"),
            P(None, "mp"),
            P(None, "mp"),
            P("mp"),
            P("mp", None),
            P(),
            P(),
            P(),
            P(None, "mp"),
            P("mp"),
            P("mp", None),
            P(),
        ),
        out_specs=(
            P(("dp", "mp"), None),
            P(("dp", "mp"), None),
            P(),
            P(),
            P(None, "mp"),
            P("mp"),
            P(None, "mp"),
            P(None, "mp"),
            P("mp"),
            P("mp", None),
            P(),
            P(),
            P(),
            P(None, "mp"),
            P("mp"),
            P("mp", None),
            P(),
        ),
        check_vma=False,
    )
```

```python
import functools

import jax
import jax.numpy as jnp
from jax import lax
from jax.experimental import pallas as pl
from jax.experimental.pallas import tpu as pltpu
from jax.sharding import PartitionSpec as P

HD = 64
WIN = 128
EPS = 1e-06
SMALL = 16
MIB = 1 << 20

bf16 = jnp.bfloat16
f32 = jnp.float32


def mm(left, right):
    return lax.dot_general(left, right, (((1,), (0,)), ((), ())), preferred_element_type=f32)


def mm_nt(left, right):
    return lax.dot_general(left, right, (((1,), (1,)), ((), ())), preferred_element_type=f32)


def mm_tn(left, right):
    return lax.dot_general(left, right, (((0,), (0,)), ((), ())), preferred_element_type=f32)


def row_of(vec_ref, index, cols=None):
    return vec_ref[index : index + 1, 0 : (cols or vec_ref.shape[1])]


GAIN_ONE, SHIFT_ONE, GAIN_TWO, SHIFT_TWO, B_OUT, B_DOWN, B_UP, B_QUERY, B_VALUE = range(9)


def unit_of(values):
    centered = values - jnp.mean(values, -1, keepdims=True)
    rstd = lax.rsqrt(jnp.mean(centered * centered, -1, keepdims=True) + EPS)
    return centered * rstd, rstd


def norm_back(grad_norm, unit, rstd, gain):
    scaled = grad_norm * gain
    return rstd * (
        scaled
        - jnp.mean(scaled, -1, keepdims=True)
        - unit * jnp.mean(scaled * unit, -1, keepdims=True)
    )


def window_of(span_ref, seq, length):
    start = span_ref[0, seq]
    count = span_ref[1, seq]
    first = jnp.minimum(start, length - WIN)
    row = lax.broadcasted_iota(jnp.int32, (WIN, length), 0) + first
    col = lax.broadcasted_iota(jnp.int32, (WIN, length), 1)
    pick = row == col
    inside = pick & (row >= start) & (row < start + count)
    return pick.astype(f32).astype(bf16), inside.astype(f32).astype(bf16)


def per_head(rows, heads):
    lane = lax.broadcasted_iota(jnp.int32, (1, rows.shape[1]), 1)
    zeros = jnp.zeros_like(rows)
    parts = [
        jnp.where((lane >= h * HD) & (lane < (h + 1) * HD), rows, zeros) for h in range(heads)
    ]
    return jnp.concatenate(parts, 0)


def own_head(stacked, heads):
    rows = stacked.shape[0] // heads
    lane = lax.broadcasted_iota(jnp.int32, (1, stacked.shape[1]), 1)
    result = stacked[0:rows]
    for h in range(1, heads):
        result = jnp.where(lane >= h * HD, stacked[h * rows : (h + 1) * rows], result)
    return result


def softmax_parts(query, keys):
    scores = mm_nt(query, keys)
    terms = jnp.exp2((scores - jnp.max(scores, -1, keepdims=True)) * (0.125 * 1.4426950408889634))
    return terms, 1.0 / jnp.sum(terms, -1, keepdims=True)


def attend(query, keys, values, heads):
    terms, inverse = softmax_parts(per_head(query, heads), keys)
    return own_head(mm(terms.astype(bf16), values) * inverse, heads).astype(bf16)


def attend_back(query, keys, values, grad_mixed, heads):
    query, grad_mixed = per_head(query, heads), per_head(grad_mixed, heads)
    terms, inverse = softmax_parts(query, keys)
    prob = terms * inverse
    grad_prob = mm_nt(grad_mixed, values)
    row_dot = jnp.sum(prob * grad_prob, -1, keepdims=True)
    grad_scores = (prob * (grad_prob - row_dot)).astype(bf16)
    grad_q = own_head(mm(grad_scores, keys), heads) * 0.125
    grad_k = mm_tn(grad_scores, query) * 0.125
    grad_v = mm_tn(prob.astype(bf16), grad_mixed)
    return grad_q.astype(bf16), grad_k.astype(bf16), grad_v.astype(bf16)


def gelu_parts(values):
    phi = 0.5 * (1.0 + lax.erf(values * 0.7071067811865476))
    return phi


def start_all(copies):
    for copy in copies:
        copy.start()


def wait_all(copies):
    for copy in copies:
        copy.wait()


def prepare_kernel(count, ids_ref, *refs):
    vectors, (wo_ref, wup_ref, wdown_ref) = refs[:count], refs[count : count + 3]
    vec_ref, half_ref, piece_ref = refs[count + 3 : count + 6]
    *rows_s, sems = refs[count + 6 :]
    core, bit = ids_ref[1], ids_ref[3]
    half, rows = half_ref.shape[0], piece_ref.shape[0] // 2 - SMALL // 2
    copies = [
        pltpu.make_async_copy(ref, rows_s[i], sems.at[i]) for i, ref in enumerate(vectors)
    ]
    weights = [
        pltpu.make_async_copy(
            wo_ref.at[pl.ds(pl.multiple_of(core * half, 16), half), :], half_ref, sems.at[count]
        )
    ]
    first = pl.multiple_of((core * 2 + bit) * rows, 16)
    for i, ref in enumerate((wup_ref, wdown_ref)):
        weights.append(
            pltpu.make_async_copy(
                ref.at[pl.ds(first, rows), :],
                piece_ref.at[pl.ds(i * rows, rows), :],
                sems.at[count + 1 + i],
            )
        )
    start_all(copies + weights)
    wait_all(copies)
    vec_ref[...] = jnp.zeros_like(vec_ref)
    for i, ref in enumerate(vectors):
        size = ref.shape[0]
        vec_ref[i : i + 1, 0:size] = rows_s[i][...].astype(f32).reshape(1, size)
    bias = jnp.concatenate(
        [row_of(vec_ref, B_UP), jnp.zeros((SMALL - 1, vec_ref.shape[1]), f32)], 0
    )
    piece_ref[2 * rows : 2 * rows + SMALL, :] = bias.astype(bf16)
    wait_all(weights)


def first_kernel(
    span_ref, x_hbm, wq_hbm, wk_hbm, wv_hbm, vec_ref,
    normed_ref, nw_ref, qw_ref, k_ref, v_ref, mw_ref, x_s, w_s, sems,
):
    seqs = span_ref.shape[1]
    length = x_hbm.shape[0] // seqs
    width = wq_hbm.shape[0]
    inputs = [
        pltpu.make_async_copy(x_hbm.at[pl.ds(seq * length, length), :], x_s.at[seq], sems.at[seq])
        for seq in range(seqs)
    ]
    weights = [
        pltpu.make_async_copy(ref, w_s.at[i], sems.at[seqs + i])
        for i, ref in enumerate((wq_hbm, wk_hbm, wv_hbm))
    ]
    start_all(inputs[:1] + weights + inputs[1:])
    for seq in range(seqs):
        rows = slice(seq * length, (seq + 1) * length)
        win = slice(seq * WIN, (seq + 1) * WIN)
        inputs[seq].wait()
        unit, _ = unit_of(x_s[seq].astype(f32))
        normed = (unit * row_of(vec_ref, GAIN_ONE) + row_of(vec_ref, SHIFT_ONE)).astype(bf16)
        normed_ref[rows, :] = normed
        pick, _ = window_of(span_ref, seq, length)
        nw = mm(pick, normed).astype(bf16)
        nw_ref[win, :] = nw
        if seq == 0:
            wait_all(weights)
        query = (mm_nt(nw, w_s[0]) + row_of(vec_ref, B_QUERY, width)).astype(bf16)
        keys = mm_nt(normed, w_s[1]).astype(bf16)
        values = (mm_nt(normed, w_s[2]) + row_of(vec_ref, B_VALUE, width)).astype(bf16)
        qw_ref[win, :] = query
        k_ref[rows, :] = keys
        v_ref[rows, :] = values
        mixed = attend(query, keys, values, width // HD)
        mw_ref[:, seq * width : (seq + 1) * width] = mixed


def pick_kernel(span_ref, x_ref, cot_ref, xw_ref, gw_ref):
    seqs = span_ref.shape[1]
    length = x_ref.shape[0] // seqs
    for seq in range(seqs):
        rows = slice(seq * length, (seq + 1) * length)
        win = slice(seq * WIN, (seq + 1) * WIN)
        pick, inside = window_of(span_ref, seq, length)
        xw_ref[win, :] = mm(pick, x_ref[rows, :]).astype(bf16)
        gw_ref[win, :] = mm(inside, cot_ref[rows, :]).astype(bf16)


def full_attn_kernel(normed_ref, k_ref, v_ref, wq_ref, vec_ref, out_ref):
    width = wq_ref.shape[0]
    chunks = out_ref.shape[2] // width
    length = WIN * chunks

    def sequence(seq, carry):
        rows = pl.ds(pl.multiple_of(seq * length, length), length)
        query = (mm_nt(normed_ref[rows, :], wq_ref[...]) + row_of(vec_ref, B_QUERY, width)).astype(
            bf16
        )
        keys, values = k_ref[rows, :], v_ref[rows, :]
        for i in range(chunks):
            part = attend(query[i * WIN : (i + 1) * WIN], keys, values, width // HD)
            out_ref[seq, :, i * width : (i + 1) * width] = part
        return carry

    lax.fori_loop(0, out_ref.shape[0], sequence, 0)


def spread_kernel(ids_ref, mixed_ref, own_ref, keep_ref, send_ref):
    own, one, two = ids_ref[0], ids_ref[5], ids_ref[6]
    own_ref[...] = mixed_ref[own]
    keep_ref[...] = mixed_ref[own ^ two]
    rows = keep_ref.shape[0]
    send_ref[0:rows, :] = mixed_ref[own ^ one]
    send_ref[rows:, :] = mixed_ref[own ^ one ^ two]


def project(mixed_refs, wo_s, width):
    total = None
    for i, (ref, row) in enumerate(mixed_refs):
        count = ref.shape[1] // width
        rows = jnp.concatenate(
            [ref[row : row + WIN, c * width : (c + 1) * width] for c in range(count)], 0
        )
        part = mm(rows, wo_s[i])
        total = part if total is None else total + part
    return total


def lay_projection(wo_s, ids_ref, wo_ref, refs):
    core = ids_ref[1]
    wo_s[0] = wo_ref[...]
    one, pair, other = refs
    half = one.shape[0]
    mine = pl.ds(pl.multiple_of(core * half, 16), half)
    rest = pl.ds(pl.multiple_of((1 - core) * half, 16), half)
    wo_s[1, mine, :] = one[...]
    wo_s[2, mine, :] = pair[0:half, :]
    wo_s[3, mine, :] = pair[half:, :]
    wo_s[2, rest, :] = other[0:half, :]
    wo_s[1, rest, :] = other[half : 2 * half, :]
    wo_s[3, rest, :] = other[2 * half :, :]


def ffn_kernel(
    ids_ref, m0_ref, m1_ref, m2_ref, wo_ref, wo_one_ref, wo_pair_ref, wo_other_ref, xw_ref, gw_ref,
    vec_ref, wup_ref, wdown_ref,
    keep_ref, send_ref, p_own_ref, p_keep_ref, p_send_ref, resid_ref, gown_ref, small_ref,
    wo_s, resid_s, part_s,
):
    own, core, one, two = ids_ref[0], ids_ref[1], ids_ref[5], ids_ref[6]
    width = wo_ref.shape[0]
    lay_projection(wo_s, ids_ref, wo_ref, (wo_one_ref, wo_pair_ref, wo_other_ref))
    branch = project(((m0_ref, 0), (m1_ref, 0), (m2_ref, 0), (m2_ref, WIN)), wo_s, width)
    resid = xw_ref[...].astype(f32) + (branch + row_of(vec_ref, B_OUT))
    resid_s[...] = resid
    unit, _ = unit_of(resid)
    normed = (unit * row_of(vec_ref, GAIN_TWO) + row_of(vec_ref, SHIFT_TWO)).astype(bf16)
    pre = mm(normed, wup_ref[...]) + row_of(vec_ref, B_UP)
    phi = gelu_parts(pre)
    hidden = (pre * phi).astype(bf16)
    slope = phi + pre * (0.3989422804014327 * jnp.exp(-0.5 * pre * pre))
    grad_out = gw_ref[...]
    grad_pre = (slope * mm_nt(grad_out, wdown_ref[...])).astype(bf16)
    part_s[...] = mm_nt(grad_pre, wup_ref[...])

    def window(ref, place):
        return ref[pl.ds(pl.multiple_of(place * WIN, WIN), WIN), :]

    p_own_ref[...] = window(part_s, own).astype(bf16)
    p_keep_ref[...] = window(part_s, own ^ two).astype(bf16)
    p_send_ref[0:WIN, :] = window(part_s, own ^ one).astype(bf16)
    p_send_ref[WIN:, :] = window(part_s, own ^ one ^ two).astype(bf16)
    resid_ref[...] = window(resid_s, own)
    gown_ref[...] = window(gw_ref, own)
    grad_up = mm_tn(normed, grad_pre).astype(bf16)
    grad_down = mm_tn(hidden, grad_out).astype(bf16)

    @pl.when(core == 0)
    def _():
        keep_ref[...] = grad_up
        send_ref[...] = grad_down

    @pl.when(core == 1)
    def _():
        keep_ref[...] = grad_down
        send_ref[...] = grad_up

    small_ref[...] = jnp.zeros_like(small_ref)
    small_ref[0:1, :] = jnp.sum(grad_pre.astype(f32), 0, keepdims=True)
    small_ref[1:2, :] = jnp.sum(grad_out.astype(f32), 0, keepdims=True)


def pass_kernel(own_ref, keep_ref, recv_ref, mine_ref, send_ref):
    rows = own_ref.shape[0]
    mine_ref[...] = own_ref[...].astype(f32) + recv_ref[0:rows, :].astype(f32)
    total = keep_ref[...].astype(f32) + recv_ref[rows:, :].astype(f32)
    send_ref[...] = total.astype(bf16)


def norm_two_kernel(mine_ref, recv_ref, resid_ref, gown_ref, vec_ref, gresid_ref, gb_ref):
    grad_norm = mine_ref[...] + recv_ref[...].astype(f32)
    unit, rstd = unit_of(resid_ref[...])
    grad = gown_ref[...].astype(f32) + norm_back(grad_norm, unit, rstd, row_of(vec_ref, GAIN_TWO))
    gresid_ref[...] = grad
    gb_ref[0:WIN, :] = grad.astype(bf16)
    sums = [jnp.sum(grad_norm * unit, 0, keepdims=True), jnp.sum(grad_norm, 0, keepdims=True)]
    sums.append(jnp.zeros((SMALL - 2, grad.shape[1]), f32))
    gb_ref[WIN : WIN + SMALL, :] = jnp.concatenate(sums, 0).astype(bf16)


def attn_kernel(
    ids_ref, span_ref, g0_ref, g1_ref, g2_ref, mw_ref, nw_ref, qw_ref, k_ref, v_ref, normed_ref,
    wq_ref, wk_ref, wv_ref, wo_ref, vec_ref, ffn_small_ref,
    keep_ref, send_ref, d_own_ref, d_keep_ref, d_send_ref, gb_s, acc_s, col_s, dn_s,
):
    own, core, one, two = ids_ref[0], ids_ref[1], ids_ref[5], ids_ref[6]
    width, model = wq_ref.shape
    seqs = nw_ref.shape[0] // WIN
    length = normed_ref.shape[0] // seqs
    rows = g0_ref.shape[0]
    gb_s[own] = g0_ref[...]
    gb_s[own ^ one] = g1_ref[...]
    gb_s[own ^ two] = g2_ref[0:rows, :]
    gb_s[own ^ one ^ two] = g2_ref[rows:, :]
    for seq in range(seqs):
        rows = slice(seq * length, (seq + 1) * length)
        win = slice(seq * WIN, (seq + 1) * WIN)
        block = gb_s[seq]
        grad_branch = block[0:WIN]
        grad_mixed = mm_nt(grad_branch, wo_ref[...]).astype(bf16)
        grad_q, grad_k, grad_v = attend_back(
            qw_ref[win, :], k_ref[rows, :], v_ref[rows, :], grad_mixed, width // HD
        )
        normed = normed_ref[rows, :]
        pick, _ = window_of(span_ref, seq, length)
        all_q = mm_tn(pick, grad_q).astype(bf16)
        grad_norm = mm(all_q, wq_ref[...]) + mm(grad_k, wk_ref[...]) + mm(grad_v, wv_ref[...])
        dn_s[seq] = grad_norm.astype(bf16)
        mixed = mw_ref[:, seq * width : (seq + 1) * width]
        parts = (
            mm_tn(grad_q, nw_ref[win, :]),
            mm_tn(grad_k, normed),
            mm_tn(grad_v, normed),
            mm_tn(mixed, grad_branch),
        )
        cols = [
            jnp.sum(grad.astype(f32), 0, keepdims=True)
            for grad in (grad_q, grad_k, grad_v, grad_branch)
        ] + [block[WIN : WIN + 2].astype(f32)]
        if seq == 0:
            for i, part in enumerate(parts):
                acc_s[i] = part
            for i, part in enumerate(cols):
                col_s[i : i + part.shape[0], 0 : part.shape[1]] = part
        else:
            for i, part in enumerate(parts):
                acc_s[i] += part
            for i, part in enumerate(cols):
                col_s[i : i + part.shape[0], 0 : part.shape[1]] += part

    d_own_ref[...] = dn_s[own]
    d_keep_ref[...] = dn_s[own ^ two]
    d_send_ref[0:length, :] = dn_s[own ^ one]
    d_send_ref[length:, :] = dn_s[own ^ one ^ two]

    sums = jnp.zeros((1, model), f32)
    total = jnp.zeros((1, model), f32)
    pad = jnp.zeros((1, model - width), f32)
    col_q = col_s[0:1, 0:width]
    col_v = col_s[2:3, 0:width]
    for i, w_ref in enumerate((wq_ref, wk_ref, wv_ref)):
        sums += jnp.sum(w_ref[...].astype(f32) * acc_s[i], 0, keepdims=True)
        cols = col_s[i : i + 1, 0:width]
        high = cols.astype(bf16)
        low = (cols - high.astype(f32)).astype(bf16)
        both = jnp.concatenate([high, low, jnp.zeros((14, width), bf16)], 0)
        total += jnp.sum(mm(both, w_ref[...]), 0, keepdims=True)
    gain = (sums - row_of(vec_ref, SHIFT_ONE) * total) / row_of(vec_ref, GAIN_ONE)
    small = jnp.concatenate(
        [
            ffn_small_ref[0:2, :],
            col_s[3:6, :],
            gain,
            total,
            jnp.concatenate([col_q, pad], 1),
            jnp.concatenate([col_v, pad], 1),
            jnp.zeros((SMALL - 9, model), f32),
        ],
        0,
    ).astype(bf16)
    first = jnp.concatenate([acc_s[0], acc_s[1]], 0).astype(bf16)
    second = jnp.concatenate([acc_s[2], acc_s[3]], 0).astype(bf16)
    rows = first.shape[0]
    keep_ref[rows : rows + SMALL, :] = small
    send_ref[rows : rows + SMALL, :] = small

    @pl.when(core == 0)
    def _():
        keep_ref[0:rows, :] = first
        send_ref[0:rows, :] = second

    @pl.when(core == 1)
    def _():
        keep_ref[0:rows, :] = second
        send_ref[0:rows, :] = first


def split_kernel(small, which, ids_ref, keep_ref, recv_ref, mine_ref, send_ref):
    bit = ids_ref[which]
    rows = mine_ref.shape[0] - small

    def total(first, count):
        part = pl.ds(first, count)
        return keep_ref[part, :].astype(f32) + recv_ref[part, :].astype(f32)

    mine_ref[0:rows, :] = total(pl.multiple_of(bit * rows, 16), rows)
    send_ref[0:rows, :] = total(pl.multiple_of((1 - bit) * rows, 16), rows).astype(bf16)
    if small:
        block = total(2 * rows, small)
        mine_ref[rows:, :] = block
        send_ref[rows:, :] = block.astype(bf16)


def total_kernel(mine_ref, recv_ref, out_ref, *small_refs):
    total = mine_ref[...] + recv_ref[...].astype(f32)
    rows = out_ref.shape[0]
    out_ref[...] = total[0:rows].astype(bf16)
    if small_refs:
        small_refs[0][...] = total[rows:]


def join_kernel(which, ids_ref, mine_ref, recv_ref, out_ref):
    bit = ids_ref[which]
    rows = mine_ref.shape[0]
    out_ref[pl.ds(pl.multiple_of(bit * rows, 16), rows), :] = mine_ref[...]
    out_ref[pl.ds(pl.multiple_of((1 - bit) * rows, 16), rows), :] = recv_ref[...]


def ffn_out_kernel(ids_ref, mine_ref, other_ref, up_ref, down_ref):
    core = ids_ref[1]

    def write(first_ref, second_ref):
        up_ref[...] = first_ref[...].astype(f32)
        down_ref[...] = second_ref[...].astype(f32)

    pl.when(core == 0)(lambda: write(mine_ref, other_ref))
    pl.when(core == 1)(lambda: write(other_ref, mine_ref))


def attn_out_kernel(ids_ref, mine_ref, other_ref, q_ref, k_ref, v_ref, o_ref):
    core = ids_ref[1]
    width = o_ref.shape[0]

    def write(first_ref, second_ref):
        q_ref[...] = first_ref[0:width, :].astype(f32)
        k_ref[...] = first_ref[width : 2 * width, :].astype(f32)
        v_ref[...] = second_ref[0:width, :].astype(f32)
        o_ref[...] = second_ref[width : 2 * width, :].astype(f32)

    pl.when(core == 0)(lambda: write(mine_ref, other_ref))
    pl.when(core == 1)(lambda: write(other_ref, mine_ref))


def stack_kernel(*refs):
    out_ref = refs[-1]
    row = 0
    for ref in refs[:-1]:
        out_ref[row : row + ref.shape[0], :] = ref[...]
        row += ref.shape[0]


def own_rows(ref, ids_ref, length):
    return ref[pl.ds(pl.multiple_of(ids_ref[0] * length, 16), length), :]


def own_branch_kernel(
    ids_ref, m0_ref, m1_ref, m2_ref, wo_ref, wo_one_ref, wo_pair_ref, wo_other_ref, x_ref, vec_ref,
    resid_ref, normed_ref, wo_s,
):
    lay_projection(wo_s, ids_ref, wo_ref, (wo_one_ref, wo_pair_ref, wo_other_ref))
    branch = project(
        ((m0_ref, 0), (m1_ref, 0), (m2_ref, 0), (m2_ref, WIN)), wo_s, wo_ref.shape[0]
    )
    x = own_rows(x_ref, ids_ref, resid_ref.shape[0]).astype(f32)
    resid = x + (branch + row_of(vec_ref, B_OUT))
    resid_ref[...] = resid
    unit, _ = unit_of(resid)
    normed_ref[...] = (unit * row_of(vec_ref, GAIN_TWO) + row_of(vec_ref, SHIFT_TWO)).astype(bf16)


def local_ffn_kernel(number, rows, ids_ref, acc_ref, normed_ref, vec_ref, *refs):
    *weights, out_ref, up_s, down_s = refs
    each = 2 * rows + SMALL
    normed = normed_ref[...]
    total = acc_ref[...]
    for shard in range((1, 2, 1)[number]):
        if number == 0:
            up, down, bias = weights[0][...], weights[1][...], row_of(vec_ref, B_UP)
        else:
            for i, ref in enumerate(weights):
                core = ids_ref[1] ^ (i // 2)
                bit = ids_ref[3 + i // 2] ^ (i % 2)
                place = pl.ds(pl.multiple_of((core * 2 + bit) * rows, 16), rows)
                first = each * (1 - shard if number == 1 and i >= 2 else shard)
                up_s[place, :] = ref[first : first + rows, :]
                down_s[place, :] = ref[first + rows : first + 2 * rows, :]
            first = each * shard + 2 * rows
            bias = weights[0][first : first + SMALL, :].astype(f32)[0:1]
            up, down = up_s[...], down_s[...]
        pre = mm(normed, up) + bias
        hidden = (pre * gelu_parts(pre)).astype(bf16)
        total += mm(hidden, down)
    if number == 2:
        out_ref[...] = (total + row_of(vec_ref, B_DOWN)).astype(bf16)
    else:
        out_ref[...] = total


def norm_one_kernel(span_ref, ids_ref, mine_ref, recv_ref, x_ref, gresid_ref, vec_ref, out_ref):
    length = out_ref.shape[0]
    grad_norm = mine_ref[...] + recv_ref[...].astype(f32)
    pick, _ = window_of(span_ref, ids_ref[0], length)
    unit, rstd = unit_of(own_rows(x_ref, ids_ref, length).astype(f32))
    grad = norm_back(grad_norm, unit, rstd, row_of(vec_ref, GAIN_ONE))
    resid = gresid_ref[...]
    high = resid.astype(bf16)
    low = (resid - high.astype(f32)).astype(bf16)
    out_ref[...] = (grad + mm_tn(pick, high) + mm_tn(pick, low)).astype(bf16)


def sds(shape, dtype):
    return jax.ShapeDtypeStruct(shape, dtype)


def params(mib=48):
    return pltpu.CompilerParams(vmem_limit_bytes=mib * MIB)


def cost(micros):
    return pl.CostEstimate(
        flops=micros * 1_000_000_000, bytes_accessed=micros * 3_000_000, transcendentals=0
    )


SMEM = pl.BlockSpec(memory_space=pltpu.SMEM)
VMEM = pl.BlockSpec(memory_space=pltpu.VMEM)
ANY = pl.BlockSpec(memory_space=pl.ANY)
DMA = pltpu.SemaphoreType.DMA


def after(value, *deps):
    return lax.optimization_barrier((value,) + deps)[0]


def call(kernel, name, micros, mib, args, outs, scratch=(), scalars=1):
    return pl.pallas_call(
        kernel,
        in_specs=[SMEM] * scalars + [VMEM] * (len(args) - scalars),
        out_specs=[VMEM] * len(outs),
        out_shape=outs,
        scratch_shapes=list(scratch),
        compiler_params=params(mib),
        cost_estimate=cost(micros),
        name=name,
    )(*args)


def local(
    dp_size, mp_size, inputs, cotangent, span_table, ln1_gain, ln1_shift, w_query, b_query, w_key,
    w_value, b_value, w_out, b_out, ln2_gain, ln2_shift, w_up, b_up, w_down, b_down,
):
    tok_rows, model = inputs.shape
    seqs = span_table.shape[0]
    length = tok_rows // seqs
    width = w_query.shape[1]
    units = w_up.shape[1]
    dp_bits = dp_size.bit_length() - 1
    core_bit, x_bit, y_bit = 1, 2, 1 << (dp_bits - 1)
    dp_idx = lax.axis_index("dp")
    own = lax.axis_index("mp")
    core = dp_idx & 1
    at_x = (dp_idx >> 1) & 1
    at_y = dp_idx >> (dp_bits - 1)
    turn = (at_x ^ at_y) * core
    ids = jnp.stack([own, core, core, at_x ^ turn, at_y ^ turn, 1 + 2 * core, 3 - 2 * core])
    ids = ids.astype(jnp.int32)

    def joint(value, flip):
        pairs = []
        for i in range(dp_size):
            for j in range(mp_size):
                dp_flip, mp_flip = flip(i & 1)
                pairs.append((i * mp_size + j, (i ^ dp_flip) * mp_size + (j ^ mp_flip)))
        return lax.ppermute(value, ("dp", "mp"), pairs)

    def trade(value, bits):
        return joint(value, lambda core: (0, bits))

    def step_one(value):
        return joint(value, lambda core: (0, 3 if core else 1))

    def step_two(value):
        return joint(value, lambda core: (0, 1 if core else 3))

    def swap(value, bits):
        return joint(value, lambda core: (bits, 0))

    def cross_one(value):
        return joint(value, lambda core: ((y_bit, 0) if core else (x_bit, 0)))

    def cross_two(value):
        return joint(value, lambda core: ((x_bit, 0) if core else (y_bit, 0)))

    wq, wk, wv = w_query.T, w_key.T, w_value.T
    spans = span_table.T

    def rows_of(count, dtype=bf16):
        return sds((count, model), dtype)

    def stack(name, *arrays):
        rows = sum(a.shape[0] for a in arrays)
        return call(stack_kernel, name, 1, 8, arrays, [rows_of(rows)], scalars=0)[0]

    vectors = (ln1_gain, ln1_shift, ln2_gain, ln2_shift, b_out, b_down, b_up, b_query, b_value)
    half, quarter = width // 2, units // 4
    vec, wo_half, piece = pl.pallas_call(
        functools.partial(prepare_kernel, len(vectors)),
        in_specs=[SMEM] + [ANY] * (len(vectors) + 3),
        out_specs=[VMEM] * 3,
        out_shape=[
            rows_of(len(vectors), f32), rows_of(half), rows_of(2 * quarter + SMALL),
        ],
        scratch_shapes=[pltpu.VMEM(v.shape, bf16) for v in vectors] + [DMA((len(vectors) + 3,))],
        compiler_params=params(60),
        cost_estimate=cost(1),
        name="prepare",
    )(ids, *vectors, w_out, w_up, w_down)
    wo_one = step_one(wo_half)
    piece_one = step_one(piece)

    win_rows = seqs * WIN
    normed, nw, qw, keys, values, mw = pl.pallas_call(
        first_kernel,
        in_specs=[SMEM] + [ANY] * 4 + [VMEM],
        out_specs=[VMEM] * 6,
        out_shape=[
            rows_of(tok_rows),
            rows_of(win_rows),
            sds((win_rows, width), bf16),
            sds((tok_rows, width), bf16),
            sds((tok_rows, width), bf16),
            sds((WIN, seqs * width), bf16),
        ],
        scratch_shapes=[
            pltpu.VMEM((seqs, length, model), bf16),
            pltpu.VMEM((3, width, model), bf16),
            DMA((seqs + 3,)),
        ],
        compiler_params=params(24),
        cost_estimate=cost(7),
        name="windows_forward",
    )(spans, inputs, wq, wk, wv, vec)

    mw_one = step_one(mw)
    wo_pair = step_two(stack("projection_pair", after(wo_half, mw, piece_one), wo_one))
    (mixed,) = call(
        full_attn_kernel, "own_heads_attention", 7, 16,
        (after(normed, mw), keys, values, wq, vec), [sds((seqs, WIN, seqs * width), bf16)],
        scalars=0,
    )
    mw_pair = step_two(stack("windows_pair", after(mw, mixed), mw_one))
    wo_other = swap(stack("projection_rest", wo_one, wo_pair), core_bit)
    xw, gw = call(
        pick_kernel, "windows_pick", 2, 16, (spans, after(inputs, mw), cotangent),
        [rows_of(win_rows)] * 2,
    )
    m_own, m_keep, m_send = call(
        spread_kernel, "mixed_spread", 1, 8, (ids, after(mixed, mw_one)),
        [rows_of(WIN)] * 2 + [rows_of(2 * WIN)],
    )
    m_recv = step_one(after(m_send, mw_pair))
    piece_two = step_two(after(piece, mw_pair))

    wo_parts = (w_out, wo_one, wo_pair, wo_other)
    keep, send, p_own, p_keep, p_send, resid_own, gown, ffn_small = call(
        ffn_kernel,
        "windows_ffn",
        7,
        28,
        (ids, mw, mw_one, after(mw_pair, m_send), *wo_parts, xw, gw, vec, w_up, w_down),
        [rows_of(model)] * 2
        + [rows_of(WIN)] * 2
        + [rows_of(2 * WIN), rows_of(WIN, f32), rows_of(WIN), rows_of(8, f32)],
        [
            pltpu.VMEM((4, width, model), bf16),
            pltpu.VMEM((win_rows, model), f32),
            pltpu.VMEM((win_rows, model), f32),
        ],
    )

    def sum_split(keep, recv, small, which, name):
        rows = (keep.shape[0] - small) // 2 + small
        return call(
            functools.partial(split_kernel, small, which), name, 1, 8, (ids, keep, recv),
            [rows_of(rows, f32), rows_of(rows)],
        )

    def sum_total(mine, recv, small, name):
        rows = mine.shape[0] - small
        outs = [rows_of(rows)] + ([rows_of(small, f32)] if small else [])
        done, *rest = call(total_kernel, name, 1, 8, (mine, recv), outs, scalars=0)
        rest = rest[0] if small else None
        for bit in range(2, dp_bits - 1):
            done = (done.astype(f32) + swap(done, 1 << bit).astype(f32)).astype(bf16)
            if small:
                rest = rest + swap(rest, 1 << bit)
        return done, rest

    def join(mine, recv, which, name):
        return call(
            functools.partial(join_kernel, which), name, 1, 8, (ids, mine, recv),
            [rows_of(2 * mine.shape[0])],
        )[0]

    def pass_on(own_part, keep_part, recv, name):
        rows = own_part.shape[0]
        return call(
            pass_kernel, name, 1, 12, (own_part, keep_part, recv),
            [rows_of(rows, f32), rows_of(rows)], scalars=0,
        )

    p_recv = step_one(p_send)
    ffn_recv = swap(send, core_bit)
    ffn_mine, ffn_send = sum_split(keep, ffn_recv, 0, 3, "ffn_split_one")
    ffn_recv = cross_one(ffn_send)
    p_mine, p_send = pass_on(
        p_own, after(p_keep, ffn_send, piece_two, m_recv), p_recv, "windows_pass"
    )
    p_recv = step_two(p_send)
    pieces = stack("pieces", piece_one, after(piece_two, p_send))
    pieces_core = swap(pieces, core_bit)

    gresid, gb = call(
        norm_two_kernel, "windows_norm_back", 1, 8,
        (p_mine, after(p_recv, pieces), resid_own, gown, vec),
        [rows_of(WIN, f32), rows_of(WIN + SMALL)], scalars=0,
    )

    gb_one = step_one(gb)
    ffn_mine, ffn_send = sum_split(ffn_mine, after(ffn_recv, gb), 0, 4, "ffn_split_two")
    ffn_recv = cross_two(ffn_send)
    gb_pair = step_two(stack("branch_pair", after(gb, ffn_send), gb_one))
    ffn_done, _ = sum_total(ffn_mine, after(ffn_recv, gb_one), 0, "ffn_total")
    ffn_got = cross_two(ffn_done)
    over = cross_one(after(pieces, ffn_done))
    m_first = m_recv[0:WIN]
    m_pair = step_two(after(stack("mixed_pair", m_keep, m_recv[WIN:]), gb_pair))
    piece_last = step_two(after(piece_one, gb_pair))

    att_rows = 2 * width + SMALL
    keep, send, d_own, d_keep, d_send = call(
        attn_kernel,
        "windows_attention_back",
        10,
        28,
        (ids, spans, after(gb, ffn_done), gb_one, gb_pair, mw, nw, qw, keys, values, normed,
         wq, wk, wv, w_out, vec, ffn_small),
        [rows_of(att_rows)] * 2 + [rows_of(length)] * 2 + [rows_of(2 * length)],
        [
            pltpu.VMEM((seqs, WIN + SMALL, model), bf16),
            pltpu.VMEM((4, width, model), f32),
            pltpu.VMEM((8, model), f32),
            pltpu.VMEM((seqs, length, model), bf16),
        ],
        scalars=2,
    )

    att_recv = swap(send, core_bit)
    resid, normed_two = call(
        own_branch_kernel, "own_branch", 2, 16,
        (ids, m_own, m_first, after(m_pair, keep), *wo_parts, inputs, vec),
        [rows_of(length, f32), rows_of(length)],
        [pltpu.VMEM((4, width, model), bf16)],
    )
    att_mine, att_send = sum_split(keep, after(att_recv, resid), SMALL, 3, "att_split_one")
    att_recv = cross_one(att_send)
    d_recv = step_one(after(d_send, att_send))
    piece_last = after(piece_last, att_send)
    over_last = cross_one(piece_last)

    def ffn_part(number, acc, weights, name):
        return call(
            functools.partial(local_ffn_kernel, number, quarter), name, 3, 24,
            (ids, acc, normed_two, vec, *weights),
            [rows_of(length, bf16 if number == 2 else f32)],
            [pltpu.VMEM((model, units), bf16), pltpu.VMEM((units, model), bf16)],
        )[0]

    ffn_acc = ffn_part(0, after(resid, att_send), [w_up, w_down], "own_ffn_own")
    over = after(over, att_send)
    over_core = swap(over, core_bit)
    att_mine, att_send = sum_split(att_mine, after(att_recv, ffn_acc), SMALL, 4, "att_split_two")
    att_recv = cross_two(att_send)
    last = [piece_last, over_last, swap(piece_last, core_bit), swap(over_last, core_bit)]
    first = [pieces, over, pieces_core, over_core]
    ffn_acc = ffn_part(1, after(ffn_acc, att_send), first, "own_ffn_first")
    att_done, small = sum_total(att_mine, after(att_recv, ffn_acc), SMALL, "att_total")
    att_got = cross_two(att_done)
    d_mine, d_send = pass_on(d_own, d_keep, after(d_recv, att_done), "own_pass")
    d_recv = step_two(d_send)
    norm_sums = small[5:7]
    for bits in (1, 2):
        norm_sums = norm_sums + trade(norm_sums, bits)
    ffn_rows = join(ffn_done, after(ffn_got, att_done), 4, "ffn_join_one")
    ffn_got = cross_one(ffn_rows)
    layer_out = ffn_part(2, after(ffn_acc, d_send, ffn_rows), last, "own_ffn_last")
    att_part = join(att_done, after(att_got, layer_out), 4, "att_join_one")
    att_got = cross_one(att_part)
    ffn_half = join(ffn_rows, after(ffn_got, att_part), 3, "ffn_join_two")
    ffn_other = swap(ffn_half, core_bit)
    (grad_inputs,) = call(
        norm_one_kernel, "own_norm_back", 2, 16,
        (spans, ids, d_mine, after(d_recv, ffn_half), inputs, gresid, vec),
        [rows_of(length)], scalars=2,
    )
    att_half = join(att_part, after(att_got, grad_inputs), 3, "att_join_two")
    att_other = swap(att_half, core_bit)

    grad_w_up, grad_w_down = call(
        ffn_out_kernel, "ffn_gradients", 3, 16, (ids, ffn_half, ffn_other), [rows_of(model, f32)] * 2
    )
    grad_w_query, grad_w_key, grad_w_value, grad_w_out = call(
        attn_out_kernel, "attention_gradients", 2, 16, (ids, att_half, att_other),
        [rows_of(width, f32)] * 4,
    )

    return (
        layer_out,
        grad_inputs,
        norm_sums[0],
        norm_sums[1],
        grad_w_query.T,
        small[7, :width],
        grad_w_key.T,
        grad_w_value.T,
        small[8, :width],
        grad_w_out,
        small[2],
        small[3],
        small[4],
        grad_w_up,
        small[0],
        grad_w_down,
        small[1],
    )


def solution(mesh):
    return jax.shard_map(
        functools.partial(local, mesh.shape["dp"], mesh.shape["mp"]),
        mesh=mesh,
        in_specs=(
            P("dp", None),
            P("dp", None),
            P("dp", None),
            P(),
            P(),
            P(None, "mp"),
            P("mp"),
            P(None, "mp"),
            P(None, "mp"),
            P("mp"),
            P("mp", None),
            P(),
            P(),
            P(),
            P(None, "mp"),
            P("mp"),
            P("mp", None),
            P(),
        ),
        out_specs=(
            P(("dp", "mp"), None),
            P(("dp", "mp"), None),
            P(),
            P(),
            P(None, "mp"),
            P("mp"),
            P(None, "mp"),
            P(None, "mp"),
            P("mp"),
            P("mp", None),
            P(),
            P(),
            P(),
            P(None, "mp"),
            P("mp"),
            P("mp", None),
            P(),
        ),
        check_vma=False,
    )
```

```python
import functools

import jax
import jax.numpy as jnp
from jax import lax
from jax.experimental import pallas as pl
from jax.experimental.pallas import tpu as pltpu
from jax.sharding import PartitionSpec as P

HD = 64
WIN = 128
EPS = 1e-06
SMALL = 16
WIDE = 256
MIB = 1 << 20

bf16 = jnp.bfloat16
f32 = jnp.float32


def mm(left, right):
    return lax.dot_general(left, right, (((1,), (0,)), ((), ())), preferred_element_type=f32)


def mm_nt(left, right):
    return lax.dot_general(left, right, (((1,), (1,)), ((), ())), preferred_element_type=f32)


def mm_tn(left, right):
    return lax.dot_general(left, right, (((0,), (0,)), ((), ())), preferred_element_type=f32)


def row_of(vec_ref, index, cols=None):
    return vec_ref[index : index + 1, 0 : (cols or vec_ref.shape[1])]


GAIN_ONE, SHIFT_ONE, GAIN_TWO, SHIFT_TWO, B_OUT, B_DOWN, B_UP, B_QUERY, B_VALUE = range(9)


def here():
    at, own = lax.axis_index("dp"), lax.axis_index("mp")
    core = at & 1
    at_x, at_y = (at >> 1) & 1, at >> (lax.axis_size("dp").bit_length() - 2)
    turn = (at_x ^ at_y) * core
    return own, core, (at_x ^ turn, at_y ^ turn), 1 + core, 2 - core


def unit_of(values):
    centered = values - jnp.mean(values, -1, keepdims=True)
    rstd = lax.rsqrt(jnp.mean(centered * centered, -1, keepdims=True) + EPS)
    return centered * rstd, rstd


def norm_back(grad_norm, unit, rstd, gain):
    scaled = grad_norm * gain
    return rstd * (
        scaled
        - jnp.mean(scaled, -1, keepdims=True)
        - unit * jnp.mean(scaled * unit, -1, keepdims=True)
    )


def window_of(span_ref, seq, length):
    start = span_ref[0, seq]
    count = span_ref[1, seq]
    first = jnp.minimum(start, length - WIN)
    row = lax.broadcasted_iota(jnp.int32, (WIN, length), 0) + first
    col = lax.broadcasted_iota(jnp.int32, (WIN, length), 1)
    pick = row == col
    inside = pick & (row >= start) & (row < start + count)
    return pick.astype(f32).astype(bf16), inside.astype(f32).astype(bf16)


def per_head(rows, heads):
    lane = lax.broadcasted_iota(jnp.int32, (1, rows.shape[1]), 1)
    zeros = jnp.zeros_like(rows)
    parts = [
        jnp.where((lane >= h * HD) & (lane < (h + 1) * HD), rows, zeros) for h in range(heads)
    ]
    return jnp.concatenate(parts, 0)


def own_head(stacked, heads):
    rows = stacked.shape[0] // heads
    lane = lax.broadcasted_iota(jnp.int32, (1, stacked.shape[1]), 1)
    result = stacked[0:rows]
    for h in range(1, heads):
        result = jnp.where(lane >= h * HD, stacked[h * rows : (h + 1) * rows], result)
    return result


def softmax_parts(query, keys):
    scores = mm_nt(query, keys)
    terms = jnp.exp2((scores - jnp.max(scores, -1, keepdims=True)) * (0.125 * 1.4426950408889634))
    return terms, 1.0 / jnp.sum(terms, -1, keepdims=True)


def attend(query, keys, values, heads):
    terms, inverse = softmax_parts(per_head(query, heads), keys)
    return own_head(mm(terms.astype(bf16), values) * inverse, heads).astype(bf16)


def attend_back(query, keys, values, grad_mixed, heads):
    query, grad_mixed = per_head(query, heads), per_head(grad_mixed, heads)
    terms, inverse = softmax_parts(query, keys)
    prob = terms * inverse
    grad_prob = mm_nt(grad_mixed, values)
    row_dot = jnp.sum(prob * grad_prob, -1, keepdims=True)
    grad_scores = (prob * (grad_prob - row_dot)).astype(bf16)
    grad_q = own_head(mm(grad_scores, keys), heads) * 0.125
    grad_k = mm_tn(grad_scores, query) * 0.125
    grad_v = mm_tn(prob.astype(bf16), grad_mixed)
    return grad_q.astype(bf16), grad_k.astype(bf16), grad_v.astype(bf16)


def gelu_parts(values):
    phi = 0.5 * (1.0 + lax.erf(values * 0.7071067811865476))
    return phi


def start_all(copies):
    for copy in copies:
        copy.start()


def wait_all(copies):
    for copy in copies:
        copy.wait()


def prepare_kernel(count, *refs):
    vectors, (wq_ref, wk_ref, wv_ref, wo_ref, wup_ref, wdown_ref) = refs[:count], refs[count : count + 6]
    vec_ref, att_ref, ffn_ref, att_kept_ref, ffn_kept_ref = refs[count + 6 : count + 11]
    *rows_s, sems = refs[count + 11 :]
    _, core, (first, second), _, _ = here()
    rows = ffn_ref.shape[0] // 2
    place = core * 4 + first * 2 + second
    copies = [
        pltpu.make_async_copy(ref, rows_s[i], sems.at[i]) for i, ref in enumerate(vectors)
    ]
    weights = []
    for i, ref in enumerate((wup_ref, wdown_ref)):
        weights.append(
            pltpu.make_async_copy(
                ref.at[pl.ds(pl.multiple_of(place * rows, 16), rows), :],
                ffn_ref.at[pl.ds(i * rows, rows), :],
                sems.at[count + i],
            )
        )
    attention = [
        pltpu.make_async_copy(
            ref.at[pl.ds(pl.multiple_of(second * rows, 16), rows), :],
            att_ref.at[pl.ds(0, rows), :],
            sems.at[count + 2],
        )
        for ref in (wq_ref, wk_ref, wv_ref, wo_ref)
    ]
    for i, copy in enumerate(attention):
        pl.when(core * 2 + first == i)(copy.start)
    start_all(weights + copies)
    wait_all(copies)
    vec_ref[...] = jnp.zeros_like(vec_ref)
    for i, ref in enumerate(vectors):
        size = ref.shape[0]
        vec_ref[i : i + 1, 0:size] = rows_s[i][...].astype(f32).reshape(1, size)
    bias = [row_of(vec_ref, index) for index in (B_UP, B_QUERY, B_VALUE)]
    bias = jnp.concatenate(bias + [jnp.zeros((SMALL - 3, vec_ref.shape[1]), f32)], 0)
    att_ref[rows:, :] = bias.astype(bf16)
    wait_all(weights + attention[:1])
    att_kept_ref[...] = att_ref[...]
    ffn_kept_ref[...] = ffn_ref[...]


def first_kernel(
    span_ref, x_hbm, wq_hbm, wk_hbm, wv_hbm, vec_ref,
    normed_ref, nw_ref, qw_ref, k_ref, v_ref, mh_ref, x_s, w_s, sems,
):
    seqs = span_ref.shape[1]
    length = x_hbm.shape[0] // seqs
    width = wq_hbm.shape[0]
    inputs = [
        pltpu.make_async_copy(x_hbm.at[pl.ds(seq * length, length), :], x_s.at[seq], sems.at[seq])
        for seq in range(seqs)
    ]
    weights = [
        pltpu.make_async_copy(ref, w_s.at[i], sems.at[seqs + i])
        for i, ref in enumerate((wq_hbm, wk_hbm, wv_hbm))
    ]
    start_all(inputs[:1] + weights + inputs[1:])
    for seq in range(seqs):
        rows = slice(seq * length, (seq + 1) * length)
        win = slice(seq * WIN, (seq + 1) * WIN)
        inputs[seq].wait()
        unit, _ = unit_of(x_s[seq].astype(f32))
        normed = (unit * row_of(vec_ref, GAIN_ONE) + row_of(vec_ref, SHIFT_ONE)).astype(bf16)
        normed_ref[rows, :] = normed
        pick, _ = window_of(span_ref, seq, length)
        nw = mm(pick, normed).astype(bf16)
        nw_ref[win, :] = nw
        if seq == 0:
            wait_all(weights)
        query = (mm_nt(nw, w_s[0]) + row_of(vec_ref, B_QUERY, width)).astype(bf16)
        keys = mm_nt(normed, w_s[1]).astype(bf16)
        values = (mm_nt(normed, w_s[2]) + row_of(vec_ref, B_VALUE, width)).astype(bf16)
        qw_ref[win, :] = query
        k_ref[rows, :] = keys
        v_ref[rows, :] = values
        mh_ref[seq] = attend(query, keys, values, width // HD)


def pick_kernel(span_ref, cot_ref, gw_ref):
    seqs = span_ref.shape[1]
    length = cot_ref.shape[0] // seqs
    for seq in range(seqs):
        _, inside = window_of(span_ref, seq, length)
        rows = slice(seq * length, (seq + 1) * length)
        gw_ref[seq * WIN : (seq + 1) * WIN, :] = mm(inside, cot_ref[rows, :]).astype(bf16)


def feed_back(normed, grad_out, up, down, bias):
    pre = mm(normed, up) + bias
    phi = gelu_parts(pre)
    slope = phi + pre * (0.3989422804014327 * jnp.exp(-0.5 * pre * pre))
    grad_pre = (slope * mm_nt(grad_out, down)).astype(bf16)
    return (pre * phi).astype(bf16), grad_pre


def ffn_kernel(
    own_ref, one_ref, pair_ref, gw_ref, vec_ref, wup_ref, wdown_ref,
    keep_ref, send_ref, small_ref, normed_s,
):
    own, core, _, one, two = here()
    sources = (
        (own, own_ref, 0), (own ^ one, one_ref, 0), (own ^ two, pair_ref, 0),
        (own ^ one ^ two, pair_ref, WIN),
    )
    for seq, ref, row in sources:
        normed_s[pl.ds(pl.multiple_of(seq * WIN, 16), WIN), :] = ref[row : row + WIN, :]
    normed, grad_out = normed_s[...], gw_ref[...]
    hidden, grad_pre = feed_back(
        normed, grad_out, wup_ref[...], wdown_ref[...], row_of(vec_ref, B_UP)
    )
    grad_up = mm_tn(normed, grad_pre).astype(bf16)
    grad_down = mm_tn(hidden, grad_out).astype(bf16)

    @pl.when(core == 0)
    def _():
        keep_ref[...] = grad_up
        send_ref[...] = grad_down

    @pl.when(core == 1)
    def _():
        keep_ref[...] = grad_down
        send_ref[...] = grad_up

    small_ref[...] = jnp.zeros_like(small_ref)
    small_ref[0:1, :] = jnp.sum(grad_pre.astype(f32), 0, keepdims=True)
    small_ref[1:2, :] = jnp.sum(grad_out.astype(f32), 0, keepdims=True)


def own_window_kernel(
    rows, normed_ref, resid_ref, gw_ref, vec_ref, bias_ref, own_up_ref, own_down_ref, all_ref,
    other_ref, gresid_ref, gb_ref, up_s, down_s,
):
    normed = normed_ref[...]
    grad_out = gw_ref[pl.ds(pl.multiple_of(here()[0] * WIN, 16), WIN), :]
    grad_norm = None
    for shard in range(-1, 3):
        if shard < 0:
            up, down, bias = own_up_ref[...], own_down_ref[...], row_of(vec_ref, B_UP)
        else:
            lay_ffn(up_s.at[shard], down_s.at[shard], (all_ref, other_ref), shard, rows)
            up, down = up_s[shard], down_s[shard]
            bias = bias_ref[shard * SMALL : (shard + 1) * SMALL, :].astype(f32)[0:1]
        _, grad_pre = feed_back(normed, grad_out, up, down, bias)
        part = mm_nt(grad_pre, up)
        grad_norm = part if grad_norm is None else grad_norm + part
    unit, rstd = unit_of(resid_ref[...])
    grad = grad_out.astype(f32) + norm_back(grad_norm, unit, rstd, row_of(vec_ref, GAIN_TWO))
    gresid_ref[...] = grad
    gb_ref[0:WIN, :] = grad.astype(bf16)
    sums = [jnp.sum(grad_norm * unit, 0, keepdims=True), jnp.sum(grad_norm, 0, keepdims=True)]
    sums.append(jnp.zeros((SMALL - 2, grad.shape[1]), f32))
    gb_ref[WIN : WIN + SMALL, :] = jnp.concatenate(sums, 0).astype(bf16)


def attn_kernel(
    last, ga_ref, gb_ref, mh_ref, nw_ref, qw_ref, k_ref, v_ref, normed_ref,
    wq_ref, wk_ref, wv_ref, wo_ref, *refs,
):
    if last:
        vec_ref, small_ref, acc_in_ref, col_in_ref = refs[:4]
        keep_ref, send_ref, acc_ref, col_ref = refs[4:]
        acc_ref[...] = acc_in_ref[...]
        col_ref[...] = col_in_ref[...]
    else:
        acc_ref, col_ref = refs
        acc_ref[...] = jnp.zeros_like(acc_ref)
        col_ref[...] = jnp.zeros_like(col_ref)
    own, core, _, one, two = here()
    width, model = wq_ref.shape
    seqs = mh_ref.shape[0]
    length = normed_ref.shape[0] // seqs
    first = own ^ two if last else own
    block_rows = WIN + SMALL
    for seq, ref, row in ((first, ga_ref, 0), (first ^ one, gb_ref, block_rows if last else 0)):
        rows = pl.ds(pl.multiple_of(seq * length, length), length)
        win = pl.ds(pl.multiple_of(seq * WIN, WIN), WIN)
        grad_branch = ref[row : row + WIN, :]
        sums = ref[row + WIN : row + block_rows, :].astype(f32)
        grad_mixed = mm_nt(grad_branch, wo_ref[...]).astype(bf16)
        grad_q, grad_k, grad_v = attend_back(
            qw_ref[win, :], k_ref[rows, :], v_ref[rows, :], grad_mixed, width // HD
        )
        normed = normed_ref[rows, :]
        acc_ref[0] += mm_tn(grad_q, nw_ref[win, :])
        acc_ref[1] += mm_tn(grad_k, normed)
        acc_ref[2] += mm_tn(grad_v, normed)
        acc_ref[3] += mm_tn(mh_ref[seq], grad_branch)
        for i, grad in enumerate((grad_q, grad_k, grad_v, grad_branch)):
            col_ref[i : i + 1, 0 : grad.shape[1]] += jnp.sum(grad.astype(f32), 0, keepdims=True)
        col_ref[4:6, :] += sums[0:2]
    if not last:
        return

    sums = jnp.zeros((1, model), f32)
    total = jnp.zeros((1, model), f32)
    pad = jnp.zeros((1, model - width), f32)
    for i, w_ref in enumerate((wq_ref, wk_ref, wv_ref)):
        sums += jnp.sum(w_ref[...].astype(f32) * acc_ref[i], 0, keepdims=True)
        cols = col_ref[i : i + 1, 0:width]
        high = cols.astype(bf16)
        low = (cols - high.astype(f32)).astype(bf16)
        both = jnp.concatenate([high, low, jnp.zeros((14, width), bf16)], 0)
        total += jnp.sum(mm(both, w_ref[...]), 0, keepdims=True)
    gain = (sums - row_of(vec_ref, SHIFT_ONE) * total) / row_of(vec_ref, GAIN_ONE)
    small = jnp.concatenate(
        [
            gain,
            total,
            small_ref[0:2, :],
            col_ref[3:6, :],
            jnp.concatenate([col_ref[0:1, 0:width], pad], 1),
            jnp.concatenate([col_ref[2:3, 0:width], pad], 1),
            jnp.zeros((SMALL - 9, model), f32),
        ],
        0,
    ).astype(bf16)
    first = jnp.concatenate([acc_ref[0], acc_ref[1]], 0).astype(bf16)
    second = jnp.concatenate([acc_ref[2], acc_ref[3]], 0).astype(bf16)
    rows = first.shape[0]
    keep_ref[rows : rows + SMALL, :] = small
    send_ref[rows : rows + SMALL, :] = small

    @pl.when(core == 0)
    def _():
        keep_ref[0:rows, :] = first
        send_ref[0:rows, :] = second

    @pl.when(core == 1)
    def _():
        keep_ref[0:rows, :] = second
        send_ref[0:rows, :] = first


def split_kernel(small, which, keep_ref, recv_ref, mine_ref, send_ref):
    bit = here()[2][which]
    rows = mine_ref.shape[0] - small

    def total(first, count):
        part = pl.ds(first, count)
        return keep_ref[part, :].astype(f32) + recv_ref[part, :].astype(f32)

    mine_ref[0:rows, :] = total(pl.multiple_of(bit * rows, 16), rows)
    send_ref[0:rows, :] = total(pl.multiple_of((1 - bit) * rows, 16), rows).astype(bf16)
    if small:
        block = total(2 * rows, small)
        mine_ref[rows:, :] = block
        send_ref[rows:, :] = block.astype(bf16)


def total_kernel(mine_ref, recv_ref, out_ref, *small_refs):
    total = mine_ref[...] + recv_ref[...].astype(f32)
    rows = out_ref.shape[0]
    out_ref[...] = total[0:rows].astype(bf16)
    if small_refs:
        small_refs[0][...] = total[rows:]
        small_refs[1][...] = total[rows : rows + 8]


def join_kernel(which, mine_ref, recv_ref, out_ref):
    bit = here()[2][which]
    rows = mine_ref.shape[0]
    out_ref[pl.ds(pl.multiple_of(bit * rows, 16), rows), :] = mine_ref[...]
    out_ref[pl.ds(pl.multiple_of((1 - bit) * rows, 16), rows), :] = recv_ref[...]


def add_kernel(left_ref, right_ref, out_ref):
    out_ref[...] = left_ref[...] + right_ref[...]


def small_out_kernel(small_ref, left_ref, right_ref, *out_refs):
    norms = left_ref[...] + right_ref[...]
    for i, ref in enumerate(out_refs):
        row = norms[i : i + 1] if i < 2 else small_ref[i : i + 1, :]
        ref[...] = row[:, 0 : ref.shape[0]].reshape(ref.shape[0])


def ffn_out_kernel(mine_ref, other_ref, up_ref, down_ref):
    core = here()[1]

    def write(first_ref, second_ref):
        up_ref[...] = first_ref[...].astype(f32)
        down_ref[...] = second_ref[...].astype(f32)

    pl.when(core == 0)(lambda: write(mine_ref, other_ref))
    pl.when(core == 1)(lambda: write(other_ref, mine_ref))


def attn_out_kernel(mine_ref, other_ref, q_ref, k_ref, v_ref, o_ref):
    core = here()[1]
    width = o_ref.shape[0]

    def write(first_ref, second_ref):
        q_ref[...] = first_ref[0:width, :].astype(f32)
        k_ref[...] = first_ref[width : 2 * width, :].astype(f32)
        v_ref[...] = second_ref[0:width, :].astype(f32)
        o_ref[...] = second_ref[width : 2 * width, :].astype(f32)

    pl.when(core == 0)(lambda: write(mine_ref, other_ref))
    pl.when(core == 1)(lambda: write(other_ref, mine_ref))


def unpack_kernel(one_ref, pair_ref, got_ref, bias_ref):
    each = one_ref.shape[0]
    rows = each - SMALL
    for i, (ref, row) in enumerate(((one_ref, 0), (pair_ref, 0), (pair_ref, each))):
        got_ref[i * rows : (i + 1) * rows, :] = ref[row : row + rows, :]
        bias_ref[i * SMALL : (i + 1) * SMALL, :] = ref[row + rows : row + each, :]


def stack_kernel(*refs):
    out_ref = refs[-1]
    row = 0
    for ref in refs[:-1]:
        out_ref[row : row + ref.shape[0], :] = ref[...]
        row += ref.shape[0]


def own_rows(ref, length):
    return ref[pl.ds(pl.multiple_of(here()[0] * length, 16), length), :]


def eighths(refs, shard, rows):
    _, own_core, (first, second), _, _ = here()
    for flip, ref in enumerate(refs):
        bits = (second, first) if flip else (first, second)
        at = (1, 0, 2)[shard] if flip else shard
        for i in range(4):
            place = (own_core ^ flip) * 4 + (bits[0] ^ (i % 2)) * 2 + (bits[1] ^ (i // 2))
            yield place, ref, (i * 3 + at) * rows


def lay_attention(w_s, n, own_refs, stacks, shard, rows):
    if shard < 0:
        for i, ref in enumerate(own_refs):
            w_s[n, i * WIDE : i * WIDE + rows, :] = ref[...]
    else:
        piece = rows // 2
        for place, ref, row in eighths(stacks, shard, piece):
            to = pl.multiple_of((place >> 1) * WIDE + (place & 1) * piece, 16)
            w_s[n, pl.ds(to, piece), :] = ref[row : row + piece, :]


def lay_ffn(up_s, down_s, stacks, shard, rows):
    for place, ref, row in eighths(stacks, shard, 2 * rows):
        to = pl.ds(pl.multiple_of(place * rows, 16), rows)
        up_s[to, :] = ref[row : row + rows, :]
        down_s[to, :] = ref[row + rows : row + 2 * rows, :]


def local_attn_kernel(near, rows, span_ref, acc_ref, normed_ref, vec_ref, bias_ref, *refs):
    own = 4 if near else 0
    own_refs, stacks, rest = refs[:own], refs[own : own + 2], refs[own + 2 :]
    if near:
        qkv_ref, resid_ref, w_s, acc_s = rest
    else:
        qkv_ref, resid_ref, normed_two_ref, resid_win_ref, normed_win_ref, w_s, acc_s = rest
    length, model = resid_ref.shape
    normed = own_rows(normed_ref, length)
    if near:
        acc_s[...] = own_rows(acc_ref, length).astype(f32)
    else:
        acc_s[...] = acc_ref[...]
    pad = jnp.zeros((1, WIDE - rows), f32)
    for n, shard in enumerate((-1, 0) if near else (1, 2)):
        for i in range(3):
            w_s[n, i * WIDE + rows : (i + 1) * WIDE, :] = jnp.zeros((WIDE - rows, model), bf16)
        lay_attention(w_s, n, own_refs, stacks, shard, rows)
        if shard < 0:
            bias_q, bias_v = row_of(vec_ref, B_QUERY, rows), row_of(vec_ref, B_VALUE, rows)
        else:
            block = bias_ref[shard * SMALL : (shard + 1) * SMALL, :].astype(f32)
            bias_q, bias_v = block[1:2, 0:rows], block[2:3, 0:rows]
        bias = jnp.concatenate([bias_q, pad, jnp.zeros((1, WIDE), f32), bias_v, pad], 1)
        qkv = (mm_nt(normed, w_s[n, 0 : 3 * WIDE, :]) + bias).astype(bf16)
        qkv_ref[n] = qkv
        keys, values = qkv[:, WIDE : 2 * WIDE], qkv[:, 2 * WIDE : 3 * WIDE]
        mixed = jnp.concatenate(
            [
                attend(qkv[first : first + WIN, 0:WIDE], keys, values, rows // HD)
                for first in range(0, length, WIN)
            ],
            0,
        )
        acc_s[...] += mm(mixed[:, 0:rows], w_s[n, 3 * WIDE : 3 * WIDE + rows, :])
    resid = acc_s[...]
    if not near:
        resid += row_of(vec_ref, B_OUT)
        unit, _ = unit_of(resid)
        normed = (unit * row_of(vec_ref, GAIN_TWO) + row_of(vec_ref, SHIFT_TWO)).astype(bf16)
        normed_two_ref[...] = normed
        pick, _ = window_of(span_ref, here()[0], length)
        normed_win_ref[...] = mm(pick, normed).astype(bf16)
        high = resid.astype(bf16)
        rest = resid - high.astype(f32)
        low = rest.astype(bf16)
        last = (rest - low.astype(f32)).astype(bf16)
        resid_win_ref[...] = mm(pick, high) + mm(pick, low) + mm(pick, last)
    resid_ref[...] = resid


def local_back_kernel(
    near, rows, span_ref, acc_ref, x_ref, gresid_ref, gb_ref, qkv_ref, vec_ref, *refs
):
    own = 4 if near else 0
    own_refs, stacks = refs[:own], refs[own : own + 2]
    out_ref, w_s = refs[own + 2 :]
    length, model = out_ref.shape
    pick, _ = window_of(span_ref, here()[0], length)
    total = None if near else acc_ref[...]
    for n, shard in enumerate((-1, 0) if near else (1, 2)):
        for i in range(3):
            w_s[n, i * WIDE + rows : (i + 1) * WIDE, :] = jnp.zeros((WIDE - rows, model), bf16)
        lay_attention(w_s, n, own_refs, stacks, shard, rows)
        qkv = qkv_ref[n]
        query = mm(pick, qkv[:, 0:WIDE]).astype(bf16)
        w_out = w_s[n, 3 * WIDE : 3 * WIDE + rows, :]
        grad_mixed = mm_nt(gb_ref[0:WIN, :], w_out).astype(bf16)
        grad_mixed = jnp.concatenate([grad_mixed, jnp.zeros((WIN, WIDE - rows), bf16)], 1)
        grad_q, grad_k, grad_v = attend_back(
            query, qkv[:, WIDE : 2 * WIDE], qkv[:, 2 * WIDE : 3 * WIDE], grad_mixed, rows // HD
        )
        grad_q = mm_tn(pick, grad_q).astype(bf16)
        part = mm(jnp.concatenate([grad_q, grad_k, grad_v], 1), w_s[n, 0 : 3 * WIDE, :])
        total = part if total is None else total + part
    if near:
        out_ref[...] = total
    else:
        unit, rstd = unit_of(own_rows(x_ref, length).astype(f32))
        grad = norm_back(total, unit, rstd, row_of(vec_ref, GAIN_ONE))
        resid = gresid_ref[...]
        high = resid.astype(bf16)
        low = (resid - high.astype(f32)).astype(bf16)
        out_ref[...] = (grad + mm_tn(pick, high) + mm_tn(pick, low)).astype(bf16)


def local_ffn_kernel(near, rows, acc_ref, normed_ref, vec_ref, bias_ref, *refs):
    own = 2 if near else 0
    own_refs, stacks = refs[:own], refs[own : own + 2]
    out_ref, up_s, down_s = refs[own + 2 :]
    normed = normed_ref[...]
    total = acc_ref[...]
    for n, shard in enumerate((-1, 0) if near else (1, 2)):
        if shard < 0:
            up, down, bias = own_refs[0][...], own_refs[1][...], row_of(vec_ref, B_UP)
        else:
            lay_ffn(up_s.at[n], down_s.at[n], stacks, shard, rows)
            up, down = up_s[n], down_s[n]
            bias = bias_ref[shard * SMALL : (shard + 1) * SMALL, :].astype(f32)[0:1]
        pre = mm(normed, up) + bias
        hidden = (pre * gelu_parts(pre)).astype(bf16)
        total += mm(hidden, down)
    if near:
        out_ref[...] = total
    else:
        out_ref[...] = (total + row_of(vec_ref, B_DOWN)).astype(bf16)


def sds(shape, dtype):
    return jax.ShapeDtypeStruct(shape, dtype)


def params(mib=48):
    return pltpu.CompilerParams(vmem_limit_bytes=mib * MIB)


NO_COST = pl.CostEstimate(flops=0, bytes_accessed=0, transcendentals=0)


SMEM = pl.BlockSpec(memory_space=pltpu.SMEM)
VMEM = pl.BlockSpec(memory_space=pltpu.VMEM)
ANY = pl.BlockSpec(memory_space=pl.ANY)
DMA = pltpu.SemaphoreType.DMA


def after(value, *deps):
    return lax.optimization_barrier((value,) + deps)[0]


def call(kernel, name, mib, args, outs, scratch=(), scalars=0):
    return pl.pallas_call(
        kernel,
        in_specs=[SMEM] * scalars + [VMEM] * (len(args) - scalars),
        out_specs=[VMEM] * len(outs),
        out_shape=outs,
        scratch_shapes=list(scratch),
        compiler_params=params(mib),
        cost_estimate=NO_COST,
        name=name,
    )(*args)


def local(
    dp_size, mp_size, inputs, cotangent, span_table, ln1_gain, ln1_shift, w_query, b_query, w_key,
    w_value, b_value, w_out, b_out, ln2_gain, ln2_shift, w_up, b_up, w_down, b_down,
):
    tok_rows, model = inputs.shape
    seqs = span_table.shape[0]
    length = tok_rows // seqs
    width = w_query.shape[1]
    units = w_up.shape[1]
    dp_bits = dp_size.bit_length() - 1
    core_bit, x_bit, y_bit = 1, 2, 1 << (dp_bits - 1)
    def joint(value, flip):
        pairs = []
        for i in range(dp_size):
            for j in range(mp_size):
                dp_flip, mp_flip = flip(i & 1)
                pairs.append((i * mp_size + j, (i ^ dp_flip) * mp_size + (j ^ mp_flip)))
        return lax.ppermute(value, ("dp", "mp"), pairs)

    def trade(value, bits):
        return joint(value, lambda core: (0, bits))

    def step_one(value):
        return joint(value, lambda core: (0, 2 if core else 1))

    def step_two(value):
        return joint(value, lambda core: (0, 1 if core else 2))

    def swap(value, bits):
        return joint(value, lambda core: (bits, 0))

    def cross_one(value):
        return joint(value, lambda core: ((y_bit, 0) if core else (x_bit, 0)))

    def cross_two(value):
        return joint(value, lambda core: ((x_bit, 0) if core else (y_bit, 0)))

    wq, wk, wv = w_query.T, w_key.T, w_value.T
    spans = span_table.T

    def rows_of(count, dtype=bf16):
        return sds((count, model), dtype)

    def stack(name, *arrays):
        rows = sum(a.shape[0] for a in arrays)
        return call(stack_kernel, name, 8, arrays, [rows_of(rows)], scalars=0)[0]

    vectors = (ln1_gain, ln1_shift, ln2_gain, ln2_shift, b_out, b_down, b_up, b_query, b_value)
    eighth = model // 8
    vec, att_sent, ffn_sent, att_piece, ffn_piece = pl.pallas_call(
        functools.partial(prepare_kernel, len(vectors)),
        in_specs=[ANY] * (len(vectors) + 6),
        out_specs=[VMEM] * 5,
        out_shape=[rows_of(len(vectors), f32)]
        + [rows_of(eighth + SMALL), rows_of(2 * eighth)] * 2,
        scratch_shapes=[pltpu.VMEM(v.shape, bf16) for v in vectors] + [DMA((len(vectors) + 3,))],
        compiler_params=params(60),
        cost_estimate=NO_COST,
        name="prepare",
    )(*vectors, wq, wk, wv, w_out, w_up, w_down)
    att_one = step_one(att_sent)
    ffn_one = step_one(ffn_sent)

    win_rows = seqs * WIN
    normed, nw, qw, keys, values, mh = pl.pallas_call(
        first_kernel,
        in_specs=[SMEM] + [ANY] * 4 + [VMEM],
        out_specs=[VMEM] * 6,
        out_shape=[
            rows_of(tok_rows),
            rows_of(win_rows),
            sds((win_rows, width), bf16),
            sds((tok_rows, width), bf16),
            sds((tok_rows, width), bf16),
            sds((seqs, WIN, width), bf16),
        ],
        scratch_shapes=[
            pltpu.VMEM((seqs, length, model), bf16),
            pltpu.VMEM((3, width, model), bf16),
            DMA((seqs + 3,)),
        ],
        compiler_params=params(24),
        cost_estimate=NO_COST,
        name="windows_forward",
    )(spans, inputs, wq, wk, wv, vec)
    att_pair = step_two(stack("attention_pair", after(att_piece, normed), att_one))
    ffn_pair = step_two(stack("ffn_pair", after(ffn_piece, normed), ffn_one))
    (gw,) = call(
        pick_kernel, "windows_pick", 16, (spans, after(cotangent, normed)), [rows_of(win_rows)],
        scalars=1,
    )
    att_got, biases = call(
        unpack_kernel, "attention_got", 4, (att_one, after(att_pair, gw)),
        [rows_of(3 * eighth), rows_of(3 * SMALL)],
    )
    att_over = cross_one(att_got)
    ffn_got = stack("ffn_got", ffn_one, after(ffn_pair, att_got))
    att_both = stack("attention_both", att_got, att_over)
    att_over = cross_two(att_both)
    ffn_over = cross_one(after(ffn_got, att_both))
    att_all = stack("attention_all", att_both, att_over)
    att_weights = [att_all, swap(att_all, core_bit)]
    ffn_both = stack("ffn_both", ffn_got, after(ffn_over, att_all))
    ffn_over = cross_two(ffn_both)
    own_weights = [wq, wk, wv, w_out]

    def attention_part(near, acc, weights, name):
        outs = [sds((2, length, 3 * WIDE), bf16), rows_of(length, f32)]
        if not near:
            outs += [rows_of(length), rows_of(WIN, f32), rows_of(WIN)]
        return call(
            functools.partial(local_attn_kernel, near, width), name, 24,
            (spans, acc, normed, vec, biases, *weights), outs,
            [pltpu.VMEM((2, 4 * WIDE, model), bf16), pltpu.VMEM((length, model), f32)], scalars=1,
        )

    def ffn_part(near, acc, weights, name):
        return call(
            functools.partial(local_ffn_kernel, near, eighth), name, 24,
            (acc, normed_two, vec, biases, *weights), [rows_of(length, f32 if near else bf16)],
            [pltpu.VMEM((2, model, units), bf16), pltpu.VMEM((2, units, model), bf16)],
        )[0]

    def back_part(near, acc, qkv, weights, name):
        return call(
            functools.partial(local_back_kernel, near, width), name, 24,
            (spans, acc, inputs, gresid, gb, qkv, vec, *weights),
            [rows_of(length, f32 if near else bf16)],
            [pltpu.VMEM((2, 4 * WIDE, model), bf16)], scalars=1,
        )[0]

    qkv_near, resid_near = attention_part(
        True, after(inputs, ffn_both), own_weights + att_weights, "own_attention_near"
    )
    qkv_far, resid, normed_two, resid_win, normed_win = attention_part(
        False, resid_near, att_weights, "own_attention_far"
    )

    nt_one = step_one(normed_win)
    ffn_all = stack("ffn_all", ffn_both, after(ffn_over, normed_win))
    ffn_weights = [ffn_all, swap(ffn_all, core_bit)]
    nt_pair = step_two(stack("normed_pair", normed_win, nt_one))

    gresid, gb = call(
        functools.partial(own_window_kernel, eighth),
        "own_window",
        24,
        (normed_win, resid_win, gw, vec, biases, w_up, w_down, *ffn_weights),
        [rows_of(WIN, f32), rows_of(WIN + SMALL)],
        [pltpu.VMEM((3, model, units), bf16), pltpu.VMEM((3, units, model), bf16)],
    )
    gb_one = step_one(gb)
    keep, send, ffn_small = call(
        ffn_kernel,
        "windows_ffn",
        24,
        (after(normed_win, gb), nt_one, nt_pair, gw, vec, w_up, w_down),
        [rows_of(model)] * 2 + [rows_of(8, f32)],
        [pltpu.VMEM((win_rows, model), bf16)],
    )

    def sum_split(keep, recv, small, which, name):
        rows = (keep.shape[0] - small) // 2 + small
        return call(
            functools.partial(split_kernel, small, which), name, 8, (keep, recv),
            [rows_of(rows, f32), rows_of(rows)],
        )

    def sum_total(mine, recv, small, name):
        rows = mine.shape[0] - small
        outs = [rows_of(rows)]
        if small:
            outs += [rows_of(small, f32), rows_of(8, f32)]
        done, *rest = call(total_kernel, name, 8, (mine, recv), outs)
        for bit in range(2, dp_bits - 1):
            done = (done.astype(f32) + swap(done, 1 << bit).astype(f32)).astype(bf16)
            rest = [part + swap(part, 1 << bit) for part in rest]
        return [done, *rest]

    def join(mine, recv, which, name):
        return call(
            functools.partial(join_kernel, which), name, 8, (mine, recv),
            [rows_of(2 * mine.shape[0])],
        )[0]

    ffn_recv = swap(send, core_bit)
    gb_pair = step_two(stack("branch_pair", after(gb, keep), gb_one))
    ffn_mine, ffn_send = sum_split(keep, ffn_recv, 0, 0, "ffn_split_one")
    ffn_recv = cross_one(ffn_send)
    attn_args = (mh, nw, qw, keys, values, normed, wq, wk, wv, w_out)
    acc, cols = call(
        functools.partial(attn_kernel, False),
        "windows_attention_back_near",
        24,
        (after(gb, gb_one, ffn_send), gb_one, *attn_args),
        [sds((4, width, model), f32), rows_of(8, f32)],
    )
    ffn_acc = ffn_part(True, after(resid, acc), [w_up, w_down] + ffn_weights, "own_ffn_near")
    ffn_mine, ffn_send = sum_split(ffn_mine, after(ffn_recv, ffn_acc), 0, 1, "ffn_split_two")
    ffn_recv = cross_two(ffn_send)
    att_rows = 2 * width + SMALL
    keep, send = call(
        functools.partial(attn_kernel, True),
        "windows_attention_back_far",
        24,
        (after(gb_pair, ffn_send), gb_pair, *attn_args, vec, ffn_small, acc, cols),
        [rows_of(att_rows)] * 2,
        [pltpu.VMEM((4, width, model), f32), pltpu.VMEM((8, model), f32)],
    )

    att_recv = swap(send, core_bit)
    (ffn_done,) = sum_total(ffn_mine, after(ffn_recv, keep), 0, "ffn_total")
    ffn_next = cross_two(ffn_done)
    att_mine, att_send = sum_split(keep, att_recv, SMALL, 0, "att_split_one")
    att_recv = cross_one(att_send)
    layer_out = ffn_part(False, after(ffn_acc, att_send), ffn_weights, "own_ffn_far")
    ffn_rows = join(ffn_done, after(ffn_next, layer_out), 1, "ffn_join_one")
    ffn_next = cross_one(ffn_rows)
    att_mine, att_send = sum_split(att_mine, after(att_recv, ffn_rows), SMALL, 1, "att_split_two")
    att_recv = cross_two(att_send)
    back_acc = back_part(
        True, after(gresid, att_send), qkv_near, own_weights + att_weights, "own_back_near"
    )
    att_done, small, norms = sum_total(att_mine, after(att_recv, back_acc), SMALL, "att_total")
    att_next = cross_two(att_done)
    norms_got = trade(norms, 1)
    grad_inputs = back_part(False, after(back_acc, att_done), qkv_far, att_weights, "own_back_far")
    att_part = join(att_done, after(att_next, grad_inputs), 1, "att_join_one")
    att_next = cross_one(att_part)
    ffn_half = join(ffn_rows, after(ffn_next, att_part), 0, "ffn_join_two")
    ffn_other = swap(ffn_half, core_bit)
    (norms,) = call(
        add_kernel, "norm_sums", 4, (norms, after(norms_got, att_part)), [rows_of(8, f32)]
    )
    norms_got = trade(norms, 2)
    grad_w_up, grad_w_down = call(
        ffn_out_kernel, "ffn_gradients", 16, (ffn_half, ffn_other), [rows_of(model, f32)] * 2
    )
    att_half = join(att_part, after(att_next, grad_w_up), 0, "att_join_two")
    att_other = swap(att_half, core_bit)
    small_outs = call(
        small_out_kernel, "small_gradients", 4, (small, norms, after(norms_got, att_half)),
        [sds((model,), f32)] * 7 + [sds((width,), f32)] * 2,
    )
    grad_w_query, grad_w_key, grad_w_value, grad_w_out = call(
        attn_out_kernel, "attention_gradients", 16,
        (att_half, after(att_other, small_outs[0])), [rows_of(width, f32)] * 4,
    )
    (
        grad_ln1_gain, grad_ln1_shift, grad_b_up, grad_b_down, grad_b_out, grad_ln2_gain,
        grad_ln2_shift, grad_b_query, grad_b_value,
    ) = small_outs

    return (
        layer_out,
        grad_inputs,
        grad_ln1_gain,
        grad_ln1_shift,
        grad_w_query.T,
        grad_b_query,
        grad_w_key.T,
        grad_w_value.T,
        grad_b_value,
        grad_w_out,
        grad_b_out,
        grad_ln2_gain,
        grad_ln2_shift,
        grad_w_up,
        grad_b_up,
        grad_w_down,
        grad_b_down,
    )


def solution(mesh):
    return jax.shard_map(
        functools.partial(local, mesh.shape["dp"], mesh.shape["mp"]),
        mesh=mesh,
        in_specs=(
            P("dp", None),
            P("dp", None),
            P("dp", None),
            P(),
            P(),
            P(None, "mp"),
            P("mp"),
            P(None, "mp"),
            P(None, "mp"),
            P("mp"),
            P("mp", None),
            P(),
            P(),
            P(),
            P(None, "mp"),
            P("mp"),
            P("mp", None),
            P(),
        ),
        out_specs=(
            P(("dp", "mp"), None),
            P(("dp", "mp"), None),
            P(),
            P(),
            P(None, "mp"),
            P("mp"),
            P(None, "mp"),
            P(None, "mp"),
            P("mp"),
            P("mp", None),
            P(),
            P(),
            P(),
            P(None, "mp"),
            P("mp"),
            P("mp", None),
            P(),
        ),
        check_vma=False,
    )
```

```python
import functools

import jax
import jax.numpy as jnp
from jax import lax
from jax.experimental import pallas as pl
from jax.experimental.pallas import tpu as pltpu
from jax.sharding import PartitionSpec as P

HD = 64
WIN = 128
EPS = 1e-06
SMALL = 16
WIDE = 256
MIB = 1 << 20

bf16 = jnp.bfloat16
f32 = jnp.float32


def mm(left, right):
    return lax.dot_general(left, right, (((1,), (0,)), ((), ())), preferred_element_type=f32)


def mm_nt(left, right):
    return lax.dot_general(left, right, (((1,), (1,)), ((), ())), preferred_element_type=f32)


def mm_tn(left, right):
    return lax.dot_general(left, right, (((0,), (0,)), ((), ())), preferred_element_type=f32)


def row_of(vec_ref, index, cols=None):
    return vec_ref[index : index + 1, 0 : (cols or vec_ref.shape[1])]


GAIN_ONE, SHIFT_ONE, GAIN_TWO, SHIFT_TWO, B_OUT, B_DOWN, B_UP, B_QUERY, B_VALUE = range(9)


def here():
    at, own = lax.axis_index("dp"), lax.axis_index("mp")
    core = at & 1
    at_x, at_y = (at >> 1) & 1, at >> (lax.axis_size("dp").bit_length() - 2)
    turn = (at_x ^ at_y) * core
    return own, core, (at_x ^ turn, at_y ^ turn), 1 + core, 2 - core


def unit_of(values):
    centered = values - jnp.mean(values, -1, keepdims=True)
    rstd = lax.rsqrt(jnp.mean(centered * centered, -1, keepdims=True) + EPS)
    return centered * rstd, rstd


def norm_back(grad_norm, unit, rstd, gain):
    scaled = grad_norm * gain
    return rstd * (
        scaled
        - jnp.mean(scaled, -1, keepdims=True)
        - unit * jnp.mean(scaled * unit, -1, keepdims=True)
    )


def window_of(span_ref, seq, length):
    start = span_ref[0, seq]
    count = span_ref[1, seq]
    first = jnp.minimum(start, length - WIN)
    row = lax.broadcasted_iota(jnp.int32, (WIN, length), 0) + first
    col = lax.broadcasted_iota(jnp.int32, (WIN, length), 1)
    pick = row == col
    inside = pick & (row >= start) & (row < start + count)
    return pick.astype(f32).astype(bf16), inside.astype(f32).astype(bf16)


def per_head(rows, heads):
    lane = lax.broadcasted_iota(jnp.int32, (1, rows.shape[1]), 1)
    zeros = jnp.zeros_like(rows)
    parts = [
        jnp.where((lane >= h * HD) & (lane < (h + 1) * HD), rows, zeros) for h in range(heads)
    ]
    return jnp.concatenate(parts, 0)


def own_head(stacked, heads):
    rows = stacked.shape[0] // heads
    lane = lax.broadcasted_iota(jnp.int32, (1, stacked.shape[1]), 1)
    result = stacked[0:rows]
    for h in range(1, heads):
        result = jnp.where(lane >= h * HD, stacked[h * rows : (h + 1) * rows], result)
    return result


def softmax_parts(query, keys):
    scores = mm_nt(query, keys)
    terms = jnp.exp2((scores - jnp.max(scores, -1, keepdims=True)) * (0.125 * 1.4426950408889634))
    return terms, 1.0 / jnp.sum(terms, -1, keepdims=True)


def attend(query, keys, values, heads):
    terms, inverse = softmax_parts(per_head(query, heads), keys)
    return own_head(mm(terms.astype(bf16), values) * inverse, heads).astype(bf16)


def attend_back(query, keys, values, grad_mixed, heads):
    query, grad_mixed = per_head(query, heads), per_head(grad_mixed, heads)
    terms, inverse = softmax_parts(query, keys)
    prob = terms * inverse
    grad_prob = mm_nt(grad_mixed, values)
    row_dot = jnp.sum(prob * grad_prob, -1, keepdims=True)
    grad_scores = (prob * (grad_prob - row_dot)).astype(bf16)
    grad_q = own_head(mm(grad_scores, keys), heads) * 0.125
    grad_k = mm_tn(grad_scores, query) * 0.125
    grad_v = mm_tn(prob.astype(bf16), grad_mixed)
    return grad_q.astype(bf16), grad_k.astype(bf16), grad_v.astype(bf16)


def gelu_parts(values):
    phi = 0.5 * (1.0 + lax.erf(values * 0.7071067811865476))
    return phi


def start_all(copies):
    for copy in copies:
        copy.start()


def wait_all(copies):
    for copy in copies:
        copy.wait()


def prepare_kernel(count, *refs):
    vectors, (wq_ref, wk_ref, wv_ref, wo_ref, wup_ref, wdown_ref) = refs[:count], refs[count : count + 6]
    vec_ref, att_ref, ffn_ref, att_kept_ref, ffn_kept_ref = refs[count + 6 : count + 11]
    *rows_s, sems = refs[count + 11 :]
    _, core, (first, second), _, _ = here()
    rows = ffn_ref.shape[0] // 3
    place = core * 4 + first * 2 + second
    copies = [
        pltpu.make_async_copy(ref, rows_s[i], sems.at[i]) for i, ref in enumerate(vectors)
    ]
    weights = []
    for i, (ref, row, count_rows, to) in enumerate(
        ((wup_ref, place * rows, rows, 0), (wdown_ref, (core * 2 + first) * 2 * rows, 2 * rows, rows))
    ):
        weights.append(
            pltpu.make_async_copy(
                ref.at[pl.ds(pl.multiple_of(row, 16), count_rows), :],
                ffn_ref.at[pl.ds(to, count_rows), :],
                sems.at[count + i],
            )
        )
    attention = [
        pltpu.make_async_copy(
            ref.at[pl.ds(pl.multiple_of(second * rows, 16), rows), :],
            att_ref.at[pl.ds(0, rows), :],
            sems.at[count + 2],
        )
        for ref in (wq_ref, wk_ref, wv_ref, wo_ref)
    ]
    for i, copy in enumerate(attention):
        pl.when(core * 2 + first == i)(copy.start)
    start_all(weights + copies)
    wait_all(copies)
    vec_ref[...] = jnp.zeros_like(vec_ref)
    for i, ref in enumerate(vectors):
        size = ref.shape[0]
        vec_ref[i : i + 1, 0:size] = rows_s[i][...].astype(f32).reshape(1, size)
    bias = [row_of(vec_ref, index) for index in (B_UP, B_QUERY, B_VALUE)]
    bias = jnp.concatenate(bias + [jnp.zeros((SMALL - 3, vec_ref.shape[1]), f32)], 0)
    att_ref[rows:, :] = bias.astype(bf16)
    wait_all(weights + attention[:1])
    att_kept_ref[...] = att_ref[...]
    ffn_kept_ref[...] = ffn_ref[...]


def first_kernel(
    span_ref, x_hbm, wq_hbm, wk_hbm, wv_hbm, vec_ref,
    normed_ref, nw_ref, qw_ref, k_ref, v_ref, mh_ref, x_s, w_s, sems,
):
    seqs = span_ref.shape[1]
    length = x_hbm.shape[0] // seqs
    width = wq_hbm.shape[0]
    inputs = [
        pltpu.make_async_copy(x_hbm.at[pl.ds(seq * length, length), :], x_s.at[seq], sems.at[seq])
        for seq in range(seqs)
    ]
    weights = [
        pltpu.make_async_copy(ref, w_s.at[i], sems.at[seqs + i])
        for i, ref in enumerate((wq_hbm, wk_hbm, wv_hbm))
    ]
    start_all(inputs[:1] + weights + inputs[1:])
    for seq in range(seqs):
        rows = slice(seq * length, (seq + 1) * length)
        win = slice(seq * WIN, (seq + 1) * WIN)
        inputs[seq].wait()
        unit, _ = unit_of(x_s[seq].astype(f32))
        normed = (unit * row_of(vec_ref, GAIN_ONE) + row_of(vec_ref, SHIFT_ONE)).astype(bf16)
        normed_ref[rows, :] = normed
        pick, _ = window_of(span_ref, seq, length)
        nw = mm(pick, normed).astype(bf16)
        nw_ref[win, :] = nw
        if seq == 0:
            wait_all(weights)
        query = (mm_nt(nw, w_s[0]) + row_of(vec_ref, B_QUERY, width)).astype(bf16)
        keys = mm_nt(normed, w_s[1]).astype(bf16)
        values = (mm_nt(normed, w_s[2]) + row_of(vec_ref, B_VALUE, width)).astype(bf16)
        qw_ref[win, :] = query
        k_ref[rows, :] = keys
        v_ref[rows, :] = values
        mh_ref[seq] = attend(query, keys, values, width // HD)


def pick_kernel(span_ref, cot_ref, gw_ref):
    seqs = span_ref.shape[1]
    length = cot_ref.shape[0] // seqs
    for seq in range(seqs):
        _, inside = window_of(span_ref, seq, length)
        rows = slice(seq * length, (seq + 1) * length)
        gw_ref[seq * WIN : (seq + 1) * WIN, :] = mm(inside, cot_ref[rows, :]).astype(bf16)


def feed_back(normed, grad_out, up, down, bias):
    pre = mm(normed, up) + bias
    phi = gelu_parts(pre)
    slope = phi + pre * (0.3989422804014327 * jnp.exp(-0.5 * pre * pre))
    grad_pre = (slope * mm_nt(grad_out, down)).astype(bf16)
    return (pre * phi).astype(bf16), grad_pre


def ffn_kernel(
    own_ref, one_ref, pair_ref, gw_ref, vec_ref, wup_ref, wdown_ref,
    keep_ref, send_ref, small_ref, normed_s,
):
    own, core, _, one, two = here()
    sources = (
        (own, own_ref, 0), (own ^ one, one_ref, 0), (own ^ two, pair_ref, 0),
        (own ^ one ^ two, pair_ref, WIN),
    )
    for seq, ref, row in sources:
        normed_s[pl.ds(pl.multiple_of(seq * WIN, 16), WIN), :] = ref[row : row + WIN, :]
    normed, grad_out = normed_s[...], gw_ref[...]
    hidden, grad_pre = feed_back(
        normed, grad_out, wup_ref[...], wdown_ref[...], row_of(vec_ref, B_UP)
    )
    grad_up = mm_tn(normed, grad_pre).astype(bf16)
    grad_down = mm_tn(hidden, grad_out).astype(bf16)

    @pl.when(core == 0)
    def _():
        keep_ref[...] = grad_up
        send_ref[...] = grad_down

    @pl.when(core == 1)
    def _():
        keep_ref[...] = grad_down
        send_ref[...] = grad_up

    small_ref[...] = jnp.zeros_like(small_ref)
    small_ref[0:1, :] = jnp.sum(grad_pre.astype(f32), 0, keepdims=True)
    small_ref[1:2, :] = jnp.sum(grad_out.astype(f32), 0, keepdims=True)


def own_window_kernel(
    rows, normed_ref, resid_ref, gw_ref, vec_ref, bias_ref, own_up_ref, own_down_ref, *refs
):
    *stacks, gresid_ref, gb_ref, up_s, down_s = refs
    normed = normed_ref[...]
    grad_out = gw_ref[pl.ds(pl.multiple_of(here()[0] * WIN, 16), WIN), :]
    grad_norm = None
    for shard in range(-1, 3):
        if shard < 0:
            up, down, bias = own_up_ref[...], own_down_ref[...], row_of(vec_ref, B_UP)
        else:
            lay_ffn(up_s.at[shard], down_s.at[shard], stacks, shard, rows)
            up, down = up_s[shard], down_s[shard]
            bias = bias_ref[shard * SMALL : (shard + 1) * SMALL, :].astype(f32)[0:1]
        _, grad_pre = feed_back(normed, grad_out, up, down, bias)
        part = mm_nt(grad_pre, up)
        grad_norm = part if grad_norm is None else grad_norm + part
    unit, rstd = unit_of(resid_ref[...])
    grad = grad_out.astype(f32) + norm_back(grad_norm, unit, rstd, row_of(vec_ref, GAIN_TWO))
    gresid_ref[...] = grad
    gb_ref[0:WIN, :] = grad.astype(bf16)
    sums = [jnp.sum(grad_norm * unit, 0, keepdims=True), jnp.sum(grad_norm, 0, keepdims=True)]
    sums.append(jnp.zeros((SMALL - 2, grad.shape[1]), f32))
    gb_ref[WIN : WIN + SMALL, :] = jnp.concatenate(sums, 0).astype(bf16)


def attn_kernel(
    last, ga_ref, gb_ref, mh_ref, nw_ref, qw_ref, k_ref, v_ref, normed_ref,
    wq_ref, wk_ref, wv_ref, wo_ref, *refs,
):
    if last:
        vec_ref, small_ref, acc_in_ref, col_in_ref = refs[:4]
        keep_ref, send_ref, acc_ref, col_ref = refs[4:]
        acc_ref[...] = acc_in_ref[...]
        col_ref[...] = col_in_ref[...]
    else:
        acc_ref, col_ref = refs
        acc_ref[...] = jnp.zeros_like(acc_ref)
        col_ref[...] = jnp.zeros_like(col_ref)
    own, core, _, one, two = here()
    width, model = wq_ref.shape
    seqs = mh_ref.shape[0]
    length = normed_ref.shape[0] // seqs
    first = own ^ two if last else own
    block_rows = WIN + SMALL
    for seq, ref, row in ((first, ga_ref, 0), (first ^ one, gb_ref, block_rows if last else 0)):
        rows = pl.ds(pl.multiple_of(seq * length, length), length)
        win = pl.ds(pl.multiple_of(seq * WIN, WIN), WIN)
        grad_branch = ref[row : row + WIN, :]
        sums = ref[row + WIN : row + block_rows, :].astype(f32)
        grad_mixed = mm_nt(grad_branch, wo_ref[...]).astype(bf16)
        grad_q, grad_k, grad_v = attend_back(
            qw_ref[win, :], k_ref[rows, :], v_ref[rows, :], grad_mixed, width // HD
        )
        normed = normed_ref[rows, :]
        acc_ref[0] += mm_tn(grad_q, nw_ref[win, :])
        acc_ref[1] += mm_tn(grad_k, normed)
        acc_ref[2] += mm_tn(grad_v, normed)
        acc_ref[3] += mm_tn(mh_ref[seq], grad_branch)
        for i, grad in enumerate((grad_q, grad_k, grad_v, grad_branch)):
            col_ref[i : i + 1, 0 : grad.shape[1]] += jnp.sum(grad.astype(f32), 0, keepdims=True)
        col_ref[4:6, :] += sums[0:2]
    if not last:
        return

    sums = jnp.zeros((1, model), f32)
    total = jnp.zeros((1, model), f32)
    pad = jnp.zeros((1, model - width), f32)
    for i, w_ref in enumerate((wq_ref, wk_ref, wv_ref)):
        sums += jnp.sum(w_ref[...].astype(f32) * acc_ref[i], 0, keepdims=True)
        cols = col_ref[i : i + 1, 0:width]
        high = cols.astype(bf16)
        low = (cols - high.astype(f32)).astype(bf16)
        both = jnp.concatenate([high, low, jnp.zeros((14, width), bf16)], 0)
        total += jnp.sum(mm(both, w_ref[...]), 0, keepdims=True)
    gain = (sums - row_of(vec_ref, SHIFT_ONE) * total) / row_of(vec_ref, GAIN_ONE)
    small = jnp.concatenate(
        [
            gain,
            total,
            small_ref[0:2, :],
            col_ref[3:6, :],
            jnp.concatenate([col_ref[0:1, 0:width], pad], 1),
            jnp.concatenate([col_ref[2:3, 0:width], pad], 1),
            jnp.zeros((SMALL - 9, model), f32),
        ],
        0,
    ).astype(bf16)
    first = jnp.concatenate([acc_ref[0], acc_ref[1]], 0).astype(bf16)
    second = jnp.concatenate([acc_ref[2], acc_ref[3]], 0).astype(bf16)
    rows = first.shape[0]
    keep_ref[rows : rows + SMALL, :] = small
    send_ref[rows : rows + SMALL, :] = small

    @pl.when(core == 0)
    def _():
        keep_ref[0:rows, :] = first
        send_ref[0:rows, :] = second

    @pl.when(core == 1)
    def _():
        keep_ref[0:rows, :] = second
        send_ref[0:rows, :] = first


def split_kernel(small, which, keep_ref, recv_ref, mine_ref, send_ref):
    bit = here()[2][which]
    rows = mine_ref.shape[0] - small

    def total(first, count):
        part = pl.ds(first, count)
        return keep_ref[part, :].astype(f32) + recv_ref[part, :].astype(f32)

    mine_ref[0:rows, :] = total(pl.multiple_of(bit * rows, 16), rows)
    send_ref[0:rows, :] = total(pl.multiple_of((1 - bit) * rows, 16), rows).astype(bf16)
    if small:
        block = total(2 * rows, small)
        mine_ref[rows:, :] = block
        send_ref[rows:, :] = block.astype(bf16)


def total_kernel(mine_ref, recv_ref, out_ref, *small_refs):
    total = mine_ref[...] + recv_ref[...].astype(f32)
    rows = out_ref.shape[0]
    out_ref[...] = total[0:rows].astype(bf16)
    if small_refs:
        small_refs[0][...] = total[rows:]
        small_refs[1][...] = total[rows : rows + 8]


def join_kernel(which, mine_ref, recv_ref, out_ref):
    bit = here()[2][which]
    rows = mine_ref.shape[0]
    out_ref[pl.ds(pl.multiple_of(bit * rows, 16), rows), :] = mine_ref[...]
    out_ref[pl.ds(pl.multiple_of((1 - bit) * rows, 16), rows), :] = recv_ref[...]


def add_kernel(left_ref, right_ref, out_ref):
    out_ref[...] = left_ref[...] + right_ref[...]


def small_out_kernel(small_ref, left_ref, right_ref, *out_refs):
    norms = left_ref[...] + right_ref[...]
    for i, ref in enumerate(out_refs):
        row = norms[i : i + 1] if i < 2 else small_ref[i : i + 1, :]
        ref[...] = row[:, 0 : ref.shape[0]].reshape(ref.shape[0])


def ffn_out_kernel(mine_ref, other_ref, up_ref, down_ref):
    core = here()[1]

    def write(first_ref, second_ref):
        up_ref[...] = first_ref[...].astype(f32)
        down_ref[...] = second_ref[...].astype(f32)

    pl.when(core == 0)(lambda: write(mine_ref, other_ref))
    pl.when(core == 1)(lambda: write(other_ref, mine_ref))


def attn_out_kernel(mine_ref, other_ref, q_ref, k_ref, v_ref, o_ref):
    core = here()[1]
    width = o_ref.shape[0]

    def write(first_ref, second_ref):
        q_ref[...] = first_ref[0:width, :].astype(f32)
        k_ref[...] = first_ref[width : 2 * width, :].astype(f32)
        v_ref[...] = second_ref[0:width, :].astype(f32)
        o_ref[...] = second_ref[width : 2 * width, :].astype(f32)

    pl.when(core == 0)(lambda: write(mine_ref, other_ref))
    pl.when(core == 1)(lambda: write(other_ref, mine_ref))


def unpack_kernel(one_ref, pair_ref, got_ref, bias_ref):
    each = one_ref.shape[0]
    rows = each - SMALL
    for i, (ref, row) in enumerate(((one_ref, 0), (pair_ref, 0), (pair_ref, each))):
        got_ref[i * rows : (i + 1) * rows, :] = ref[row : row + rows, :]
        bias_ref[i * SMALL : (i + 1) * SMALL, :] = ref[row + rows : row + each, :]


def rows_kernel(moves, count, *refs):
    for parts, out_ref in zip(moves, refs[count:]):
        to = 0
        for source, row, rows in parts:
            out_ref[to : to + rows, :] = refs[source][row : row + rows, :]
            to += rows


def stack_kernel(*refs):
    out_ref = refs[-1]
    row = 0
    for ref in refs[:-1]:
        out_ref[row : row + ref.shape[0], :] = ref[...]
        row += ref.shape[0]


def own_rows(ref, length):
    return ref[pl.ds(pl.multiple_of(here()[0] * length, 16), length), :]


def eighths(refs, shard, rows):
    _, own_core, (first, second), _, _ = here()
    for flip, ref in enumerate(refs):
        bits = (second, first) if flip else (first, second)
        at = (1, 0, 2)[shard] if flip else shard
        for i in range(4):
            place = (own_core ^ flip) * 4 + (bits[0] ^ (i % 2)) * 2 + (bits[1] ^ (i // 2))
            yield place, ref, (i * 3 + at) * rows


def lay_attention(w_s, n, own_refs, stacks, shard, rows):
    if shard < 0:
        for i, ref in enumerate(own_refs):
            w_s[n, i * WIDE : i * WIDE + rows, :] = ref[...]
    else:
        piece = rows // 2
        for place, ref, row in eighths(stacks, shard, piece):
            to = pl.multiple_of((place >> 1) * WIDE + (place & 1) * piece, 16)
            w_s[n, pl.ds(to, piece), :] = ref[row : row + piece, :]


def lay_ffn(up_s, down_s, stacks, shard, rows):
    for place, ref, row in eighths(stacks[:2], shard, rows):
        up_s[pl.ds(pl.multiple_of(place * rows, 16), rows), :] = ref[row : row + rows, :]
    _, own_core, (first, second), _, _ = here()
    each = 2 * rows
    for flip, ref in enumerate(stacks[2:]):
        at = (1, 0, 2)[shard] if flip else shard
        for i in range(2):
            place = (own_core ^ flip) * 2 + ((second if flip else first) ^ i)
            row = (i * 3 + at) * each
            to = pl.ds(pl.multiple_of(place * each, 16), each)
            down_s[to, :] = ref[row : row + each, :]


def local_attn_kernel(near, rows, span_ref, acc_ref, normed_ref, vec_ref, bias_ref, *refs):
    own = 4 if near else 0
    own_refs, stacks, rest = refs[:own], refs[own : own + 2], refs[own + 2 :]
    if near:
        qkv_ref, resid_ref, w_s, acc_s = rest
    else:
        qkv_ref, resid_ref, normed_two_ref, resid_win_ref, normed_win_ref, w_s, acc_s = rest
    length, model = resid_ref.shape
    normed = own_rows(normed_ref, length)
    if near:
        acc_s[...] = own_rows(acc_ref, length).astype(f32)
    else:
        acc_s[...] = acc_ref[...]
    pad = jnp.zeros((1, WIDE - rows), f32)
    for n, shard in enumerate((-1, 0) if near else (1, 2)):
        for i in range(3):
            w_s[n, i * WIDE + rows : (i + 1) * WIDE, :] = jnp.zeros((WIDE - rows, model), bf16)
        lay_attention(w_s, n, own_refs, stacks, shard, rows)
        if shard < 0:
            bias_q, bias_v = row_of(vec_ref, B_QUERY, rows), row_of(vec_ref, B_VALUE, rows)
        else:
            block = bias_ref[shard * SMALL : (shard + 1) * SMALL, :].astype(f32)
            bias_q, bias_v = block[1:2, 0:rows], block[2:3, 0:rows]
        bias = jnp.concatenate([bias_q, pad, jnp.zeros((1, WIDE), f32), bias_v, pad], 1)
        qkv = (mm_nt(normed, w_s[n, 0 : 3 * WIDE, :]) + bias).astype(bf16)
        qkv_ref[n] = qkv
        keys, values = qkv[:, WIDE : 2 * WIDE], qkv[:, 2 * WIDE : 3 * WIDE]
        mixed = jnp.concatenate(
            [
                attend(qkv[first : first + WIN, 0:WIDE], keys, values, rows // HD)
                for first in range(0, length, WIN)
            ],
            0,
        )
        acc_s[...] += mm(mixed[:, 0:rows], w_s[n, 3 * WIDE : 3 * WIDE + rows, :])
    resid = acc_s[...]
    if not near:
        resid += row_of(vec_ref, B_OUT)
        unit, _ = unit_of(resid)
        normed = (unit * row_of(vec_ref, GAIN_TWO) + row_of(vec_ref, SHIFT_TWO)).astype(bf16)
        normed_two_ref[...] = normed
        pick, _ = window_of(span_ref, here()[0], length)
        normed_win_ref[...] = mm(pick, normed).astype(bf16)
        high = resid.astype(bf16)
        rest = resid - high.astype(f32)
        low = rest.astype(bf16)
        last = (rest - low.astype(f32)).astype(bf16)
        resid_win_ref[...] = mm(pick, high) + mm(pick, low) + mm(pick, last)
    resid_ref[...] = resid


def local_back_kernel(
    near, rows, span_ref, acc_ref, x_ref, gresid_ref, gb_ref, qkv_ref, vec_ref, *refs
):
    own = 4 if near else 0
    own_refs, stacks = refs[:own], refs[own : own + 2]
    out_ref, w_s = refs[own + 2 :]
    length, model = out_ref.shape
    pick, _ = window_of(span_ref, here()[0], length)
    total = None if near else acc_ref[...]
    for n, shard in enumerate((-1, 0) if near else (1, 2)):
        for i in range(3):
            w_s[n, i * WIDE + rows : (i + 1) * WIDE, :] = jnp.zeros((WIDE - rows, model), bf16)
        lay_attention(w_s, n, own_refs, stacks, shard, rows)
        qkv = qkv_ref[n]
        query = mm(pick, qkv[:, 0:WIDE]).astype(bf16)
        w_out = w_s[n, 3 * WIDE : 3 * WIDE + rows, :]
        grad_mixed = mm_nt(gb_ref[0:WIN, :], w_out).astype(bf16)
        grad_mixed = jnp.concatenate([grad_mixed, jnp.zeros((WIN, WIDE - rows), bf16)], 1)
        grad_q, grad_k, grad_v = attend_back(
            query, qkv[:, WIDE : 2 * WIDE], qkv[:, 2 * WIDE : 3 * WIDE], grad_mixed, rows // HD
        )
        grad_q = mm_tn(pick, grad_q).astype(bf16)
        part = mm(jnp.concatenate([grad_q, grad_k, grad_v], 1), w_s[n, 0 : 3 * WIDE, :])
        total = part if total is None else total + part
    if near:
        out_ref[...] = total
    else:
        unit, rstd = unit_of(own_rows(x_ref, length).astype(f32))
        grad = norm_back(total, unit, rstd, row_of(vec_ref, GAIN_ONE))
        resid = gresid_ref[...]
        high = resid.astype(bf16)
        low = (resid - high.astype(f32)).astype(bf16)
        out_ref[...] = (grad + mm_tn(pick, high) + mm_tn(pick, low)).astype(bf16)


def local_ffn_kernel(near, rows, acc_ref, normed_ref, vec_ref, bias_ref, *refs):
    own = 2 if near else 0
    own_refs, stacks = refs[:own], refs[own : own + 4]
    out_ref, up_s, down_s = refs[own + 4 :]
    normed = normed_ref[...]
    total = acc_ref[...]
    for n, shard in enumerate((-1, 0) if near else (1, 2)):
        if shard < 0:
            up, down, bias = own_refs[0][...], own_refs[1][...], row_of(vec_ref, B_UP)
        else:
            lay_ffn(up_s.at[n], down_s.at[n], stacks, shard, rows)
            up, down = up_s[n], down_s[n]
            bias = bias_ref[shard * SMALL : (shard + 1) * SMALL, :].astype(f32)[0:1]
        pre = mm(normed, up) + bias
        hidden = (pre * gelu_parts(pre)).astype(bf16)
        total += mm(hidden, down)
    if near:
        out_ref[...] = total
    else:
        out_ref[...] = (total + row_of(vec_ref, B_DOWN)).astype(bf16)


def sds(shape, dtype):
    return jax.ShapeDtypeStruct(shape, dtype)


def params(mib=48):
    return pltpu.CompilerParams(vmem_limit_bytes=mib * MIB)


LONG = 30


MICROS = {
    "prepare": 2.5, "windows_forward": 8, "windows_pick": 1.2, "own_attention_own": 2.7,
    "own_attention_rest": 9.0, "own_window": 4.1, "windows_ffn": 3.4,
    "windows_attention_back_near": 3.3, "windows_attention_back_far": 3.9, "own_ffn_near": 2.8,
    "own_ffn_far": 3.8, "own_back_near": 4.8, "own_back_far": 6.1, "ffn_gradients": 2.5,
    "attention_gradients": 1.6, "small_gradients": 0.6,
}


def cost(name):
    micros = MICROS.get(name, 0.1) * 0.3
    return pl.CostEstimate(
        flops=int(micros * 1e9), bytes_accessed=int(micros * 3e6), transcendentals=0
    )


SMEM = pl.BlockSpec(memory_space=pltpu.SMEM)
VMEM = pl.BlockSpec(memory_space=pltpu.VMEM)
ANY = pl.BlockSpec(memory_space=pl.ANY)
DMA = pltpu.SemaphoreType.DMA


def after(value, *deps):
    return lax.optimization_barrier((value,) + deps)[0]


def call(kernel, name, mib, args, outs, scratch=(), scalars=0):
    return pl.pallas_call(
        kernel,
        in_specs=[SMEM] * scalars + [VMEM] * (len(args) - scalars),
        out_specs=[VMEM] * len(outs),
        out_shape=outs,
        scratch_shapes=list(scratch),
        compiler_params=params(mib),
        cost_estimate=cost(name),
        name=name,
    )(*args)


def local(
    dp_size, mp_size, inputs, cotangent, span_table, ln1_gain, ln1_shift, w_query, b_query, w_key,
    w_value, b_value, w_out, b_out, ln2_gain, ln2_shift, w_up, b_up, w_down, b_down,
):
    tok_rows, model = inputs.shape
    seqs = span_table.shape[0]
    length = tok_rows // seqs
    width = w_query.shape[1]
    units = w_up.shape[1]
    dp_bits = dp_size.bit_length() - 1
    core_bit, x_bit, y_bit = 1, 2, 1 << (dp_bits - 1)
    def joint(value, flip):
        pairs = []
        for i in range(dp_size):
            for j in range(mp_size):
                dp_flip, mp_flip = flip(i & 1)
                pairs.append((i * mp_size + j, (i ^ dp_flip) * mp_size + (j ^ mp_flip)))
        return lax.ppermute(value, ("dp", "mp"), pairs)

    def trade(value, bits):
        return joint(value, lambda core: (0, bits))

    def step_one(value):
        return joint(value, lambda core: (0, 2 if core else 1))

    def step_two(value):
        return joint(value, lambda core: (0, 1 if core else 2))

    def swap(value, bits):
        return joint(value, lambda core: (bits, 0))

    def cross_one(value):
        return joint(value, lambda core: ((y_bit, 0) if core else (x_bit, 0)))

    def cross_two(value):
        return joint(value, lambda core: ((x_bit, 0) if core else (y_bit, 0)))

    wq, wk, wv = w_query.T, w_key.T, w_value.T
    spans = span_table.T

    def rows_of(count, dtype=bf16):
        return sds((count, model), dtype)

    def stack(name, *arrays):
        rows = sum(a.shape[0] for a in arrays)
        return call(stack_kernel, name, 8, arrays, [rows_of(rows)])[0]

    vectors = (ln1_gain, ln1_shift, ln2_gain, ln2_shift, b_out, b_down, b_up, b_query, b_value)
    eighth = model // 8
    vec, att_sent, ffn_sent, att_piece, ffn_piece = pl.pallas_call(
        functools.partial(prepare_kernel, len(vectors)),
        in_specs=[ANY] * (len(vectors) + 6),
        out_specs=[VMEM] * 5,
        out_shape=[rows_of(len(vectors), f32)]
        + [rows_of(eighth + SMALL), rows_of(3 * eighth)] * 2,
        scratch_shapes=[pltpu.VMEM(v.shape, bf16) for v in vectors] + [DMA((len(vectors) + 3,))],
        compiler_params=params(60),
        cost_estimate=cost("prepare"),
        name="prepare",
    )(*vectors, wq, wk, wv, w_out, w_up, w_down)
    att_one = step_one(att_sent)
    ffn_one = step_one(ffn_sent)

    win_rows = seqs * WIN
    normed, nw, qw, keys, values, mh = pl.pallas_call(
        first_kernel,
        in_specs=[SMEM] + [ANY] * 4 + [VMEM],
        out_specs=[VMEM] * 6,
        out_shape=[
            rows_of(tok_rows),
            rows_of(win_rows),
            sds((win_rows, width), bf16),
            sds((tok_rows, width), bf16),
            sds((tok_rows, width), bf16),
            sds((seqs, WIN, width), bf16),
        ],
        scratch_shapes=[
            pltpu.VMEM((seqs, length, model), bf16),
            pltpu.VMEM((3, width, model), bf16),
            DMA((seqs + 3,)),
        ],
        compiler_params=params(24),
        cost_estimate=cost("windows_forward"),
        name="windows_forward",
    )(spans, inputs, wq, wk, wv, vec)
    def pick_rows(name, ins, moves):
        outs = [rows_of(sum(part[2] for part in parts)) for parts in moves]
        return call(functools.partial(rows_kernel, moves, len(ins)), name, 8, ins, outs)

    att_pair = step_two(stack("attention_pair", after(att_piece, normed), att_one))
    ffn_pair = step_two(stack("ffn_pair", after(ffn_piece, normed), ffn_one))
    (gw,) = call(
        pick_kernel, "windows_pick", 16, (spans, after(cotangent, normed)), [rows_of(win_rows)],
        scalars=1,
    )
    att_got, biases = call(
        unpack_kernel, "attention_got", 4, (att_one, after(att_pair, gw)),
        [rows_of(3 * eighth), rows_of(3 * SMALL)],
    )
    att_over = cross_one(att_got)

    att_both = stack("attention_both", att_got, att_over)
    att_over = cross_two(att_both)
    third = 3 * eighth
    up_got, down_got = pick_rows(
        "ffn_got",
        [ffn_one, after(ffn_pair, att_both)],
        [
            ((0, 0, eighth), (1, 0, eighth), (1, third, eighth)),
            ((0, eighth, 2 * eighth), (1, eighth, 2 * eighth), (1, third + eighth, 2 * eighth)),
        ],
    )
    up_over, down_over = cross_one(up_got), cross_one(down_got)
    up_both = stack("up_both", up_got, up_over)
    up_over = cross_two(up_both)
    att_all = stack("attention_all", att_both, after(att_over, up_both))
    att_weights = [att_all, swap(att_all, core_bit)]
    own_weights = [wq, wk, wv, w_out]

    def attention_part(near, acc, weights, name):
        outs = [sds((2, length, 3 * WIDE), bf16), rows_of(length, f32)]
        if not near:
            outs += [rows_of(length), rows_of(WIN, f32), rows_of(WIN)]
        return call(
            functools.partial(local_attn_kernel, near, width), name, 24,
            (spans, acc, normed, vec, biases, *weights), outs,
            [pltpu.VMEM((2, 4 * WIDE, model), bf16), pltpu.VMEM((length, model), f32)], scalars=1,
        )

    def ffn_part(near, acc, weights, name):
        return call(
            functools.partial(local_ffn_kernel, near, eighth), name, 24,
            (acc, normed_two, vec, biases, *weights), [rows_of(length, f32 if near else bf16)],
            [pltpu.VMEM((2, model, units), bf16), pltpu.VMEM((2, units, model), bf16)],
        )[0]

    def back_part(near, acc, qkv, weights, name):
        return call(
            functools.partial(local_back_kernel, near, width), name, 24,
            (spans, acc, inputs, gresid, gb, qkv, vec, *weights),
            [rows_of(length, f32 if near else bf16)],
            [pltpu.VMEM((2, 4 * WIDE, model), bf16)], scalars=1
        )[0]

    qkv_near, resid_near = attention_part(
        True, inputs, own_weights + att_weights, "own_attention_near"
    )
    qkv_far, resid, normed_two, resid_win, normed_win = attention_part(
        False, resid_near, att_weights, "own_attention_far"
    )

    nt_one = step_one(normed_win)
    nt_pair = step_two(stack("normed_pair", normed_win, nt_one))
    down_all = stack("down_all", down_got, after(down_over, normed_win))
    up_all = stack("up_all", up_both, after(up_over, nt_one))
    ffn_weights = [up_all, swap(up_all, core_bit), down_all, swap(down_all, core_bit)]

    gresid, gb = call(
        functools.partial(own_window_kernel, eighth),
        "own_window",
        24,
        (normed_win, resid_win, gw, vec, biases, w_up, w_down, *ffn_weights),
        [rows_of(WIN, f32), rows_of(WIN + SMALL)],
        [pltpu.VMEM((3, model, units), bf16), pltpu.VMEM((3, units, model), bf16)],
    )
    gb_one = step_one(gb)
    def sum_split(keep, recv, small, which, name):
        rows = (keep.shape[0] - small) // 2 + small
        return call(
            functools.partial(split_kernel, small, which), name, 8, (keep, recv),
            [rows_of(rows, f32), rows_of(rows)],
        )

    def sum_total(mine, recv, small, name):
        rows = mine.shape[0] - small
        outs = [rows_of(rows)]
        if small:
            outs += [rows_of(small, f32), rows_of(8, f32)]
        done, *rest = call(total_kernel, name, 8, (mine, recv), outs)
        for bit in range(2, dp_bits - 1):
            done = (done.astype(f32) + swap(done, 1 << bit).astype(f32)).astype(bf16)
            rest = [part + swap(part, 1 << bit) for part in rest]
        return [done, *rest]

    def join(mine, recv, which, name):
        return call(
            functools.partial(join_kernel, which), name, 8, (mine, recv),
            [rows_of(2 * mine.shape[0])],
        )[0]

    ffn_keep, ffn_send, ffn_small = call(
        ffn_kernel,
        "windows_ffn",
        24,
        (after(normed_win, gb), nt_one, nt_pair, gw, vec, w_up, w_down),
        [rows_of(model)] * 2 + [rows_of(8, f32)],
        [pltpu.VMEM((win_rows, model), bf16)],
    )
    gb_pair = step_two(stack("branch_pair", after(gb, ffn_keep), gb_one))
    attn_args = (mh, nw, qw, keys, values, normed, wq, wk, wv, w_out)
    acc, cols = call(
        functools.partial(attn_kernel, False),
        "windows_attention_back_near",
        24,
        (gb, gb_one, *attn_args),
        [sds((4, width, model), f32), rows_of(8, f32)],
    )

    ffn_recv = swap(after(ffn_send, gb_one), core_bit)
    ffn_mine, ffn_send = sum_split(ffn_keep, ffn_recv, 0, 0, "ffn_split_one")
    ffn_recv = cross_one(ffn_send)
    ffn_acc = ffn_part(True, after(resid, ffn_send), [w_up, w_down] + ffn_weights, "own_ffn_near")
    att_rows = 2 * width + SMALL
    keep, send = call(
        functools.partial(attn_kernel, True),
        "windows_attention_back_far",
        24,
        (after(gb_pair, ffn_acc, ffn_recv), gb_pair, *attn_args, vec, ffn_small, acc, cols),
        [rows_of(att_rows)] * 2,
        [pltpu.VMEM((4, width, model), f32), pltpu.VMEM((8, model), f32)]
    )

    att_recv = swap(send, core_bit)
    ffn_mine, ffn_send = sum_split(ffn_mine, after(ffn_recv, keep), 0, 1, "ffn_split_two")
    ffn_recv = cross_two(ffn_send)
    att_mine, att_send = sum_split(keep, after(att_recv, ffn_send), SMALL, 0, "att_split_one")
    att_recv = cross_one(att_send)
    layer_out = ffn_part(False, after(ffn_acc, att_send), ffn_weights, "own_ffn_far")
    att_mine, att_send = sum_split(att_mine, after(att_recv, layer_out), SMALL, 1, "att_split_two")
    att_recv = cross_two(att_send)
    (ffn_done,) = sum_total(ffn_mine, after(ffn_recv, att_send), 0, "ffn_total")
    ffn_next = cross_two(ffn_done)
    back_acc = back_part(
        True, after(gresid, ffn_done), qkv_near, own_weights + att_weights, "own_back_near"
    )
    att_done, small, norms = sum_total(att_mine, after(att_recv, back_acc), SMALL, "att_total")
    att_next = cross_two(att_done)
    norms_got = trade(norms, 1)
    ffn_rows = join(ffn_done, after(ffn_next, att_done), 1, "ffn_join_one")
    ffn_next = cross_one(ffn_rows)
    grad_inputs = back_part(False, after(back_acc, ffn_rows), qkv_far, att_weights, "own_back_far")
    (norms,) = call(
        add_kernel, "norm_sums", 4, (norms, after(norms_got, grad_inputs)), [rows_of(8, f32)]
    )
    norms_got = trade(norms, 2)
    att_part = join(att_done, after(att_next, norms), 1, "att_join_one")
    att_next = cross_one(att_part)
    ffn_half = join(ffn_rows, after(ffn_next, att_part), 0, "ffn_join_two")
    ffn_other = swap(ffn_half, core_bit)
    grad_w_up, grad_w_down = call(
        ffn_out_kernel, "ffn_gradients", 16, (ffn_half, ffn_other), [rows_of(model, f32)] * 2
    )
    att_half = join(att_part, after(att_next, norms_got, grad_w_up), 0, "att_join_two")
    att_other = swap(att_half, core_bit)
    small_outs = call(
        small_out_kernel, "small_gradients", 4, (small, norms, after(norms_got, att_half)),
        [sds((model,), f32)] * 7 + [sds((width,), f32)] * 2,
    )
    grad_w_query, grad_w_key, grad_w_value, grad_w_out = call(
        attn_out_kernel, "attention_gradients", 16, (att_half, after(att_other, small_outs[0])),
        [rows_of(width, f32)] * 4,
    )
    (
        grad_ln1_gain, grad_ln1_shift, grad_b_up, grad_b_down, grad_b_out, grad_ln2_gain,
        grad_ln2_shift, grad_b_query, grad_b_value,
    ) = small_outs

    return (
        layer_out,
        grad_inputs,
        grad_ln1_gain,
        grad_ln1_shift,
        grad_w_query.T,
        grad_b_query,
        grad_w_key.T,
        grad_w_value.T,
        grad_b_value,
        grad_w_out,
        grad_b_out,
        grad_ln2_gain,
        grad_ln2_shift,
        grad_w_up,
        grad_b_up,
        grad_w_down,
        grad_b_down,
    )


def solution(mesh):
    return jax.shard_map(
        functools.partial(local, mesh.shape["dp"], mesh.shape["mp"]),
        mesh=mesh,
        in_specs=(
            P("dp", None),
            P("dp", None),
            P("dp", None),
            P(),
            P(),
            P(None, "mp"),
            P("mp"),
            P(None, "mp"),
            P(None, "mp"),
            P("mp"),
            P("mp", None),
            P(),
            P(),
            P(),
            P(None, "mp"),
            P("mp"),
            P("mp", None),
            P(),
        ),
        out_specs=(
            P(("dp", "mp"), None),
            P(("dp", "mp"), None),
            P(),
            P(),
            P(None, "mp"),
            P("mp"),
            P(None, "mp"),
            P(None, "mp"),
            P("mp"),
            P("mp", None),
            P(),
            P(),
            P(),
            P(None, "mp"),
            P("mp"),
            P("mp", None),
            P(),
        ),
        check_vma=False,
    )
```

```python
import functools

import jax
import jax.numpy as jnp
from jax import lax
from jax.experimental import pallas as pl
from jax.experimental.pallas import tpu as pltpu
from jax.sharding import PartitionSpec as P

HD = 64
WIN = 128
EPS = 1e-06
SMALL = 16
WIDE = 256
MIB = 1 << 20

bf16 = jnp.bfloat16
f32 = jnp.float32


def mm(left, right):
    return lax.dot_general(left, right, (((1,), (0,)), ((), ())), preferred_element_type=f32)


def mm_nt(left, right):
    return lax.dot_general(left, right, (((1,), (1,)), ((), ())), preferred_element_type=f32)


def mm_tn(left, right):
    return lax.dot_general(left, right, (((0,), (0,)), ((), ())), preferred_element_type=f32)


def row_of(vec_ref, index, cols=None):
    return vec_ref[index : index + 1, 0 : (cols or vec_ref.shape[1])]


GAIN_ONE, SHIFT_ONE, GAIN_TWO, SHIFT_TWO, B_OUT, B_DOWN, B_UP, B_QUERY, B_VALUE = range(9)


def here():
    at, own = lax.axis_index("dp"), lax.axis_index("mp")
    core = at & 1
    at_x, at_y = (at >> 1) & 1, at >> (lax.axis_size("dp").bit_length() - 2)
    turn = (at_x ^ at_y) * core
    return own, core, (at_x ^ turn, at_y ^ turn), 1 + core, 2 - core


def unit_of(values):
    centered = values - jnp.mean(values, -1, keepdims=True)
    rstd = lax.rsqrt(jnp.mean(centered * centered, -1, keepdims=True) + EPS)
    return centered * rstd, rstd


def norm_back(grad_norm, unit, rstd, gain):
    scaled = grad_norm * gain
    return rstd * (
        scaled
        - jnp.mean(scaled, -1, keepdims=True)
        - unit * jnp.mean(scaled * unit, -1, keepdims=True)
    )


def window_of(span_ref, seq, length):
    start = span_ref[0, seq]
    count = span_ref[1, seq]
    first = jnp.minimum(start, length - WIN)
    row = lax.broadcasted_iota(jnp.int32, (WIN, length), 0) + first
    col = lax.broadcasted_iota(jnp.int32, (WIN, length), 1)
    pick = row == col
    inside = pick & (row >= start) & (row < start + count)
    return pick.astype(f32).astype(bf16), inside.astype(f32).astype(bf16)


def per_head(rows, heads):
    lane = lax.broadcasted_iota(jnp.int32, (1, rows.shape[1]), 1)
    zeros = jnp.zeros_like(rows)
    parts = [
        jnp.where((lane >= h * HD) & (lane < (h + 1) * HD), rows, zeros) for h in range(heads)
    ]
    return jnp.concatenate(parts, 0)


def own_head(stacked, heads):
    rows = stacked.shape[0] // heads
    lane = lax.broadcasted_iota(jnp.int32, (1, stacked.shape[1]), 1)
    result = stacked[0:rows]
    for h in range(1, heads):
        result = jnp.where(lane >= h * HD, stacked[h * rows : (h + 1) * rows], result)
    return result


def softmax_parts(query, keys):
    scores = mm_nt(query, keys)
    terms = jnp.exp2((scores - jnp.max(scores, -1, keepdims=True)) * (0.125 * 1.4426950408889634))
    return terms, 1.0 / jnp.sum(terms, -1, keepdims=True)


def attend(query, keys, values, heads):
    terms, inverse = softmax_parts(per_head(query, heads), keys)
    return own_head(mm(terms.astype(bf16), values) * inverse, heads).astype(bf16)


def attend_back(query, keys, values, grad_mixed, heads):
    query, grad_mixed = per_head(query, heads), per_head(grad_mixed, heads)
    terms, inverse = softmax_parts(query, keys)
    prob = terms * inverse
    grad_prob = mm_nt(grad_mixed, values)
    row_dot = jnp.sum(prob * grad_prob, -1, keepdims=True)
    grad_scores = (prob * (grad_prob - row_dot)).astype(bf16)
    grad_q = own_head(mm(grad_scores, keys), heads) * 0.125
    grad_k = mm_tn(grad_scores, query) * 0.125
    grad_v = mm_tn(prob.astype(bf16), grad_mixed)
    return grad_q.astype(bf16), grad_k.astype(bf16), grad_v.astype(bf16)


def gelu_parts(values):
    phi = 0.5 * (1.0 + lax.erf(values * 0.7071067811865476))
    return phi


def start_all(copies):
    for copy in copies:
        copy.start()


def wait_all(copies):
    for copy in copies:
        copy.wait()


def prepare_kernel(count, *refs):
    vectors, (wq_ref, wk_ref, wv_ref, wo_ref, wup_ref, wdown_ref) = refs[:count], refs[count : count + 6]
    vec_ref, att_ref, ffn_ref, att_kept_ref, ffn_kept_ref = refs[count + 6 : count + 11]
    *rows_s, sems = refs[count + 11 :]
    _, core, (first, second), _, _ = here()
    rows = ffn_ref.shape[0] // 3
    place = core * 4 + first * 2 + second
    copies = [
        pltpu.make_async_copy(ref, rows_s[i], sems.at[i]) for i, ref in enumerate(vectors)
    ]
    weights = []
    for i, (ref, row, count_rows, to) in enumerate(
        ((wup_ref, place * rows, rows, 0), (wdown_ref, (core * 2 + first) * 2 * rows, 2 * rows, rows))
    ):
        weights.append(
            pltpu.make_async_copy(
                ref.at[pl.ds(pl.multiple_of(row, 16), count_rows), :],
                ffn_ref.at[pl.ds(to, count_rows), :],
                sems.at[count + i],
            )
        )
    attention = [
        pltpu.make_async_copy(
            ref.at[pl.ds(pl.multiple_of(second * rows, 16), rows), :],
            att_ref.at[pl.ds(0, rows), :],
            sems.at[count + 2],
        )
        for ref in (wq_ref, wk_ref, wv_ref, wo_ref)
    ]
    for i, copy in enumerate(attention):
        pl.when(core * 2 + first == i)(copy.start)
    start_all(weights + copies)
    wait_all(copies)
    vec_ref[...] = jnp.zeros_like(vec_ref)
    for i, ref in enumerate(vectors):
        size = ref.shape[0]
        vec_ref[i : i + 1, 0:size] = rows_s[i][...].astype(f32).reshape(1, size)
    bias = [row_of(vec_ref, index) for index in (B_UP, B_QUERY, B_VALUE)]
    bias = jnp.concatenate(bias + [jnp.zeros((SMALL - 3, vec_ref.shape[1]), f32)], 0)
    att_ref[rows:, :] = bias.astype(bf16)
    wait_all(weights + attention[:1])
    att_kept_ref[...] = att_ref[...]
    ffn_kept_ref[...] = ffn_ref[...]


def first_kernel(
    span_ref, x_hbm, wq_hbm, wk_hbm, wv_hbm, vec_ref,
    normed_ref, nw_ref, qw_ref, k_ref, v_ref, mh_ref, x_s, w_s, sems,
):
    seqs = span_ref.shape[1]
    length = x_hbm.shape[0] // seqs
    width = wq_hbm.shape[0]
    inputs = [
        pltpu.make_async_copy(x_hbm.at[pl.ds(seq * length, length), :], x_s.at[seq], sems.at[seq])
        for seq in range(seqs)
    ]
    weights = [
        pltpu.make_async_copy(ref, w_s.at[i], sems.at[seqs + i])
        for i, ref in enumerate((wq_hbm, wk_hbm, wv_hbm))
    ]
    start_all(inputs[:1] + weights + inputs[1:])
    for seq in range(seqs):
        rows = slice(seq * length, (seq + 1) * length)
        win = slice(seq * WIN, (seq + 1) * WIN)
        inputs[seq].wait()
        unit, _ = unit_of(x_s[seq].astype(f32))
        normed = (unit * row_of(vec_ref, GAIN_ONE) + row_of(vec_ref, SHIFT_ONE)).astype(bf16)
        normed_ref[rows, :] = normed
        pick, _ = window_of(span_ref, seq, length)
        nw = mm(pick, normed).astype(bf16)
        nw_ref[win, :] = nw
        if seq == 0:
            wait_all(weights)
        query = (mm_nt(nw, w_s[0]) + row_of(vec_ref, B_QUERY, width)).astype(bf16)
        keys = mm_nt(normed, w_s[1]).astype(bf16)
        values = (mm_nt(normed, w_s[2]) + row_of(vec_ref, B_VALUE, width)).astype(bf16)
        qw_ref[win, :] = query
        k_ref[rows, :] = keys
        v_ref[rows, :] = values
        mh_ref[seq] = attend(query, keys, values, width // HD)


def pick_kernel(span_ref, cot_ref, gw_ref):
    seqs = span_ref.shape[1]
    length = cot_ref.shape[0] // seqs
    for seq in range(seqs):
        _, inside = window_of(span_ref, seq, length)
        rows = slice(seq * length, (seq + 1) * length)
        gw_ref[seq * WIN : (seq + 1) * WIN, :] = mm(inside, cot_ref[rows, :]).astype(bf16)


def feed_back(normed, grad_out, up, down, bias):
    pre = mm(normed, up) + bias
    phi = gelu_parts(pre)
    slope = phi + pre * (0.3989422804014327 * jnp.exp(-0.5 * pre * pre))
    grad_pre = (slope * mm_nt(grad_out, down)).astype(bf16)
    return (pre * phi).astype(bf16), grad_pre


def ffn_kernel(
    own_ref, one_ref, pair_ref, gw_ref, vec_ref, wup_ref, wdown_ref,
    keep_ref, send_ref, small_ref, normed_s,
):
    own, core, _, one, two = here()
    sources = (
        (own, own_ref, 0), (own ^ one, one_ref, 0), (own ^ two, pair_ref, 0),
        (own ^ one ^ two, pair_ref, WIN),
    )
    for seq, ref, row in sources:
        normed_s[pl.ds(pl.multiple_of(seq * WIN, 16), WIN), :] = ref[row : row + WIN, :]
    normed, grad_out = normed_s[...], gw_ref[...]
    hidden, grad_pre = feed_back(
        normed, grad_out, wup_ref[...], wdown_ref[...], row_of(vec_ref, B_UP)
    )
    grad_up = mm_tn(normed, grad_pre).astype(bf16)
    grad_down = mm_tn(hidden, grad_out).astype(bf16)

    @pl.when(core == 0)
    def _():
        keep_ref[...] = grad_up
        send_ref[...] = grad_down

    @pl.when(core == 1)
    def _():
        keep_ref[...] = grad_down
        send_ref[...] = grad_up

    small_ref[...] = jnp.zeros_like(small_ref)
    small_ref[0:1, :] = jnp.sum(grad_pre.astype(f32), 0, keepdims=True)
    small_ref[1:2, :] = jnp.sum(grad_out.astype(f32), 0, keepdims=True)


def own_window_kernel(
    rows, normed_ref, resid_ref, gw_ref, vec_ref, bias_ref, own_up_ref, own_down_ref, *refs
):
    *stacks, gresid_ref, gb_ref, up_s, down_s = refs
    normed = normed_ref[...]
    grad_out = gw_ref[pl.ds(pl.multiple_of(here()[0] * WIN, 16), WIN), :]
    grad_norm = None
    for shard in range(-1, 3):
        if shard < 0:
            up, down, bias = own_up_ref[...], own_down_ref[...], row_of(vec_ref, B_UP)
        else:
            lay_ffn(up_s.at[shard], down_s.at[shard], stacks, shard, rows)
            up, down = up_s[shard], down_s[shard]
            bias = bias_ref[shard * SMALL : (shard + 1) * SMALL, :].astype(f32)[0:1]
        _, grad_pre = feed_back(normed, grad_out, up, down, bias)
        part = mm_nt(grad_pre, up)
        grad_norm = part if grad_norm is None else grad_norm + part
    unit, rstd = unit_of(resid_ref[...])
    grad = grad_out.astype(f32) + norm_back(grad_norm, unit, rstd, row_of(vec_ref, GAIN_TWO))
    gresid_ref[...] = grad
    gb_ref[0:WIN, :] = grad.astype(bf16)
    sums = [jnp.sum(grad_norm * unit, 0, keepdims=True), jnp.sum(grad_norm, 0, keepdims=True)]
    sums.append(jnp.zeros((SMALL - 2, grad.shape[1]), f32))
    gb_ref[WIN : WIN + SMALL, :] = jnp.concatenate(sums, 0).astype(bf16)


def attn_kernel(
    last, ga_ref, gb_ref, mh_ref, nw_ref, qw_ref, k_ref, v_ref, normed_ref,
    wq_ref, wk_ref, wv_ref, wo_ref, *refs,
):
    if last:
        vec_ref, small_ref, acc_in_ref, col_in_ref = refs[:4]
        keep_ref, send_ref, acc_ref, col_ref = refs[4:]
        acc_ref[...] = acc_in_ref[...]
        col_ref[...] = col_in_ref[...]
    else:
        acc_ref, col_ref = refs
        acc_ref[...] = jnp.zeros_like(acc_ref)
        col_ref[...] = jnp.zeros_like(col_ref)
    own, core, _, one, two = here()
    width, model = wq_ref.shape
    seqs = mh_ref.shape[0]
    length = normed_ref.shape[0] // seqs
    first = own ^ two if last else own
    block_rows = WIN + SMALL
    for seq, ref, row in ((first, ga_ref, 0), (first ^ one, gb_ref, block_rows if last else 0)):
        rows = pl.ds(pl.multiple_of(seq * length, length), length)
        win = pl.ds(pl.multiple_of(seq * WIN, WIN), WIN)
        grad_branch = ref[row : row + WIN, :]
        sums = ref[row + WIN : row + block_rows, :].astype(f32)
        grad_mixed = mm_nt(grad_branch, wo_ref[...]).astype(bf16)
        grad_q, grad_k, grad_v = attend_back(
            qw_ref[win, :], k_ref[rows, :], v_ref[rows, :], grad_mixed, width // HD
        )
        normed = normed_ref[rows, :]
        acc_ref[0] += mm_tn(grad_q, nw_ref[win, :])
        acc_ref[1] += mm_tn(grad_k, normed)
        acc_ref[2] += mm_tn(grad_v, normed)
        acc_ref[3] += mm_tn(mh_ref[seq], grad_branch)
        for i, grad in enumerate((grad_q, grad_k, grad_v, grad_branch)):
            col_ref[i : i + 1, 0 : grad.shape[1]] += jnp.sum(grad.astype(f32), 0, keepdims=True)
        col_ref[4:6, :] += sums[0:2]
    if not last:
        return

    sums = jnp.zeros((1, model), f32)
    total = jnp.zeros((1, model), f32)
    pad = jnp.zeros((1, model - width), f32)
    for i, w_ref in enumerate((wq_ref, wk_ref, wv_ref)):
        sums += jnp.sum(w_ref[...].astype(f32) * acc_ref[i], 0, keepdims=True)
        cols = col_ref[i : i + 1, 0:width]
        high = cols.astype(bf16)
        low = (cols - high.astype(f32)).astype(bf16)
        both = jnp.concatenate([high, low, jnp.zeros((14, width), bf16)], 0)
        total += jnp.sum(mm(both, w_ref[...]), 0, keepdims=True)
    gain = (sums - row_of(vec_ref, SHIFT_ONE) * total) / row_of(vec_ref, GAIN_ONE)
    small = jnp.concatenate(
        [
            gain,
            total,
            small_ref[0:2, :],
            col_ref[3:6, :],
            jnp.concatenate([col_ref[0:1, 0:width], pad], 1),
            jnp.concatenate([col_ref[2:3, 0:width], pad], 1),
            jnp.zeros((SMALL - 9, model), f32),
        ],
        0,
    ).astype(bf16)
    first = jnp.concatenate([acc_ref[0], acc_ref[1]], 0).astype(bf16)
    second = jnp.concatenate([acc_ref[2], acc_ref[3]], 0).astype(bf16)
    rows = first.shape[0]
    keep_ref[rows : rows + SMALL, :] = small
    send_ref[rows : rows + SMALL, :] = small

    @pl.when(core == 0)
    def _():
        keep_ref[0:rows, :] = first
        send_ref[0:rows, :] = second

    @pl.when(core == 1)
    def _():
        keep_ref[0:rows, :] = second
        send_ref[0:rows, :] = first


def split_kernel(small, which, keep_ref, recv_ref, mine_ref, send_ref):
    bit = here()[2][which]
    rows = mine_ref.shape[0] - small

    def total(first, count):
        part = pl.ds(first, count)
        return keep_ref[part, :].astype(f32) + recv_ref[part, :].astype(f32)

    mine_ref[0:rows, :] = total(pl.multiple_of(bit * rows, 16), rows)
    send_ref[0:rows, :] = total(pl.multiple_of((1 - bit) * rows, 16), rows).astype(bf16)
    if small:
        block = total(2 * rows, small)
        mine_ref[rows:, :] = block
        send_ref[rows:, :] = block.astype(bf16)


def total_kernel(mine_ref, recv_ref, out_ref, *small_refs):
    total = mine_ref[...] + recv_ref[...].astype(f32)
    rows = out_ref.shape[0]
    out_ref[...] = total[0:rows].astype(bf16)
    if small_refs:
        small_refs[0][...] = total[rows:]
        small_refs[1][...] = total[rows : rows + 8]


def join_kernel(which, mine_ref, recv_ref, out_ref):
    bit = here()[2][which]
    rows = mine_ref.shape[0]
    out_ref[pl.ds(pl.multiple_of(bit * rows, 16), rows), :] = mine_ref[...]
    out_ref[pl.ds(pl.multiple_of((1 - bit) * rows, 16), rows), :] = recv_ref[...]


def add_kernel(left_ref, right_ref, out_ref):
    out_ref[...] = left_ref[...] + right_ref[...]


def small_out_kernel(small_ref, left_ref, right_ref, *out_refs):
    norms = left_ref[...] + right_ref[...]
    for i, ref in enumerate(out_refs):
        row = norms[i : i + 1] if i < 2 else small_ref[i : i + 1, :]
        ref[...] = row[:, 0 : ref.shape[0]].reshape(ref.shape[0])


def ffn_out_kernel(mine_ref, other_ref, up_ref, down_ref):
    core = here()[1]

    def write(first_ref, second_ref):
        up_ref[...] = first_ref[...].astype(f32)
        down_ref[...] = second_ref[...].astype(f32)

    pl.when(core == 0)(lambda: write(mine_ref, other_ref))
    pl.when(core == 1)(lambda: write(other_ref, mine_ref))


def attn_out_kernel(mine_ref, other_ref, q_ref, k_ref, v_ref, o_ref):
    core = here()[1]
    width = o_ref.shape[0]

    def write(first_ref, second_ref):
        q_ref[...] = first_ref[0:width, :].astype(f32)
        k_ref[...] = first_ref[width : 2 * width, :].astype(f32)
        v_ref[...] = second_ref[0:width, :].astype(f32)
        o_ref[...] = second_ref[width : 2 * width, :].astype(f32)

    pl.when(core == 0)(lambda: write(mine_ref, other_ref))
    pl.when(core == 1)(lambda: write(other_ref, mine_ref))


def unpack_kernel(one_ref, pair_ref, got_ref, bias_ref):
    each = one_ref.shape[0]
    rows = each - SMALL
    for i, (ref, row) in enumerate(((one_ref, 0), (pair_ref, 0), (pair_ref, each))):
        got_ref[i * rows : (i + 1) * rows, :] = ref[row : row + rows, :]
        bias_ref[i * SMALL : (i + 1) * SMALL, :] = ref[row + rows : row + each, :]


def rows_kernel(moves, count, *refs):
    for parts, out_ref in zip(moves, refs[count:]):
        to = 0
        for source, row, rows in parts:
            out_ref[to : to + rows, :] = refs[source][row : row + rows, :]
            to += rows


def stack_kernel(*refs):
    out_ref = refs[-1]
    row = 0
    for ref in refs[:-1]:
        out_ref[row : row + ref.shape[0], :] = ref[...]
        row += ref.shape[0]


def own_rows(ref, length):
    return ref[pl.ds(pl.multiple_of(here()[0] * length, 16), length), :]


def eighths(refs, shard, rows):
    _, own_core, (first, second), _, _ = here()
    for flip, ref in enumerate(refs):
        bits = (second, first) if flip else (first, second)
        at = (1, 0, 2)[shard] if flip else shard
        for i in range(4):
            place = (own_core ^ flip) * 4 + (bits[0] ^ (i % 2)) * 2 + (bits[1] ^ (i // 2))
            yield place, ref, (i * 3 + at) * rows


def lay_attention(w_s, n, own_refs, stacks, shard, rows):
    if shard < 0:
        for i, ref in enumerate(own_refs):
            w_s[n, i * WIDE : i * WIDE + rows, :] = ref[...]
    else:
        piece = rows // 2
        for place, ref, row in eighths(stacks, shard, piece):
            to = pl.multiple_of((place >> 1) * WIDE + (place & 1) * piece, 16)
            w_s[n, pl.ds(to, piece), :] = ref[row : row + piece, :]


def lay_ffn(up_s, down_s, stacks, shard, rows):
    for place, ref, row in eighths(stacks[:2], shard, rows):
        up_s[pl.ds(pl.multiple_of(place * rows, 16), rows), :] = ref[row : row + rows, :]
    _, own_core, (first, second), _, _ = here()
    each = 2 * rows
    for flip, ref in enumerate(stacks[2:]):
        at = (1, 0, 2)[shard] if flip else shard
        for i in range(2):
            place = (own_core ^ flip) * 2 + ((second if flip else first) ^ i)
            row = (i * 3 + at) * each
            to = pl.ds(pl.multiple_of(place * each, 16), each)
            down_s[to, :] = ref[row : row + each, :]


def local_attn_kernel(near, rows, span_ref, acc_ref, normed_ref, vec_ref, bias_ref, *refs):
    own = 4 if near else 0
    own_refs, stacks, rest = refs[:own], refs[own : own + 2], refs[own + 2 :]
    if near:
        qkv_ref, resid_ref, w_s, acc_s = rest
    else:
        qkv_ref, resid_ref, normed_two_ref, resid_win_ref, normed_win_ref, w_s, acc_s = rest
    length, model = resid_ref.shape
    normed = own_rows(normed_ref, length)
    if near:
        acc_s[...] = own_rows(acc_ref, length).astype(f32)
    else:
        acc_s[...] = acc_ref[...]
    pad = jnp.zeros((1, WIDE - rows), f32)
    for n, shard in enumerate((-1, 0) if near else (1, 2)):
        for i in range(3):
            w_s[n, i * WIDE + rows : (i + 1) * WIDE, :] = jnp.zeros((WIDE - rows, model), bf16)
        lay_attention(w_s, n, own_refs, stacks, shard, rows)
        if shard < 0:
            bias_q, bias_v = row_of(vec_ref, B_QUERY, rows), row_of(vec_ref, B_VALUE, rows)
        else:
            block = bias_ref[shard * SMALL : (shard + 1) * SMALL, :].astype(f32)
            bias_q, bias_v = block[1:2, 0:rows], block[2:3, 0:rows]
        bias = jnp.concatenate([bias_q, pad, jnp.zeros((1, WIDE), f32), bias_v, pad], 1)
        qkv = (mm_nt(normed, w_s[n, 0 : 3 * WIDE, :]) + bias).astype(bf16)
        qkv_ref[n] = qkv
        keys, values = qkv[:, WIDE : 2 * WIDE], qkv[:, 2 * WIDE : 3 * WIDE]
        mixed = jnp.concatenate(
            [
                attend(qkv[first : first + WIN, 0:WIDE], keys, values, rows // HD)
                for first in range(0, length, WIN)
            ],
            0,
        )
        acc_s[...] += mm(mixed[:, 0:rows], w_s[n, 3 * WIDE : 3 * WIDE + rows, :])
    resid = acc_s[...]
    if not near:
        resid += row_of(vec_ref, B_OUT)
        unit, _ = unit_of(resid)
        normed = (unit * row_of(vec_ref, GAIN_TWO) + row_of(vec_ref, SHIFT_TWO)).astype(bf16)
        normed_two_ref[...] = normed
        pick, _ = window_of(span_ref, here()[0], length)
        normed_win_ref[...] = mm(pick, normed).astype(bf16)
        high = resid.astype(bf16)
        rest = resid - high.astype(f32)
        low = rest.astype(bf16)
        last = (rest - low.astype(f32)).astype(bf16)
        resid_win_ref[...] = mm(pick, high) + mm(pick, low) + mm(pick, last)
    resid_ref[...] = resid


def local_back_kernel(
    near, rows, span_ref, acc_ref, x_ref, gresid_ref, gb_ref, qkv_ref, vec_ref, *refs
):
    own = 4 if near else 0
    own_refs, stacks = refs[:own], refs[own : own + 2]
    out_ref, w_s = refs[own + 2 :]
    length, model = out_ref.shape
    pick, _ = window_of(span_ref, here()[0], length)
    total = None if near else acc_ref[...]
    for n, shard in enumerate((-1, 0) if near else (1, 2)):
        for i in range(3):
            w_s[n, i * WIDE + rows : (i + 1) * WIDE, :] = jnp.zeros((WIDE - rows, model), bf16)
        lay_attention(w_s, n, own_refs, stacks, shard, rows)
        qkv = qkv_ref[n]
        query = mm(pick, qkv[:, 0:WIDE]).astype(bf16)
        w_out = w_s[n, 3 * WIDE : 3 * WIDE + rows, :]
        grad_mixed = mm_nt(gb_ref[0:WIN, :], w_out).astype(bf16)
        grad_mixed = jnp.concatenate([grad_mixed, jnp.zeros((WIN, WIDE - rows), bf16)], 1)
        grad_q, grad_k, grad_v = attend_back(
            query, qkv[:, WIDE : 2 * WIDE], qkv[:, 2 * WIDE : 3 * WIDE], grad_mixed, rows // HD
        )
        grad_q = mm_tn(pick, grad_q).astype(bf16)
        part = mm(jnp.concatenate([grad_q, grad_k, grad_v], 1), w_s[n, 0 : 3 * WIDE, :])
        total = part if total is None else total + part
    if near:
        out_ref[...] = total
    else:
        unit, rstd = unit_of(own_rows(x_ref, length).astype(f32))
        grad = norm_back(total, unit, rstd, row_of(vec_ref, GAIN_ONE))
        resid = gresid_ref[...]
        high = resid.astype(bf16)
        low = (resid - high.astype(f32)).astype(bf16)
        out_ref[...] = (grad + mm_tn(pick, high) + mm_tn(pick, low)).astype(bf16)


def local_ffn_kernel(near, rows, acc_ref, normed_ref, vec_ref, bias_ref, *refs):
    own = 2 if near else 0
    own_refs, stacks = refs[:own], refs[own : own + 4]
    out_ref, up_s, down_s = refs[own + 4 :]
    normed = normed_ref[...]
    total = acc_ref[...]
    for n, shard in enumerate((-1, 0) if near else (1, 2)):
        if shard < 0:
            up, down, bias = own_refs[0][...], own_refs[1][...], row_of(vec_ref, B_UP)
        else:
            lay_ffn(up_s.at[n], down_s.at[n], stacks, shard, rows)
            up, down = up_s[n], down_s[n]
            bias = bias_ref[shard * SMALL : (shard + 1) * SMALL, :].astype(f32)[0:1]
        pre = mm(normed, up) + bias
        hidden = (pre * gelu_parts(pre)).astype(bf16)
        total += mm(hidden, down)
    if near:
        out_ref[...] = total
    else:
        out_ref[...] = (total + row_of(vec_ref, B_DOWN)).astype(bf16)


def sds(shape, dtype):
    return jax.ShapeDtypeStruct(shape, dtype)


def params(mib=48):
    return pltpu.CompilerParams(vmem_limit_bytes=mib * MIB)


LONG = 30


MICROS = {
    "prepare": 2.5, "windows_forward": 8, "windows_pick": 1.2, "own_attention_own": 2.7,
    "own_attention_rest": 9.0, "own_window": 4.1, "own_probabilities": 3.5, "windows_ffn": 3.4,
    "windows_attention_back_near": 3.3, "windows_attention_back_far": 3.9, "own_ffn_near": 2.8,
    "own_ffn_far": 3.8, "own_back_near": 4.8, "own_back_far": 6.1, "ffn_gradients": 2.5,
    "attention_gradients": 1.6, "small_gradients": 0.6,
}


def cost(name):
    micros = MICROS.get(name, 0.1) * 0.1
    return pl.CostEstimate(
        flops=int(micros * 1e9), bytes_accessed=int(micros * 3e6), transcendentals=0
    )


SMEM = pl.BlockSpec(memory_space=pltpu.SMEM)
VMEM = pl.BlockSpec(memory_space=pltpu.VMEM)
ANY = pl.BlockSpec(memory_space=pl.ANY)
DMA = pltpu.SemaphoreType.DMA


def after(value, *deps):
    return lax.optimization_barrier((value,) + deps)[0]


def call(kernel, name, mib, args, outs, scratch=(), scalars=0):
    return pl.pallas_call(
        kernel,
        in_specs=[SMEM] * scalars + [VMEM] * (len(args) - scalars),
        out_specs=[VMEM] * len(outs),
        out_shape=outs,
        scratch_shapes=list(scratch),
        compiler_params=params(mib),
        cost_estimate=cost(name),
        name=name,
    )(*args)


def local(
    dp_size, mp_size, inputs, cotangent, span_table, ln1_gain, ln1_shift, w_query, b_query, w_key,
    w_value, b_value, w_out, b_out, ln2_gain, ln2_shift, w_up, b_up, w_down, b_down,
):
    tok_rows, model = inputs.shape
    seqs = span_table.shape[0]
    length = tok_rows // seqs
    width = w_query.shape[1]
    units = w_up.shape[1]
    dp_bits = dp_size.bit_length() - 1
    core_bit, x_bit, y_bit = 1, 2, 1 << (dp_bits - 1)
    def joint(value, flip):
        pairs = []
        for i in range(dp_size):
            for j in range(mp_size):
                dp_flip, mp_flip = flip(i & 1)
                pairs.append((i * mp_size + j, (i ^ dp_flip) * mp_size + (j ^ mp_flip)))
        return lax.ppermute(value, ("dp", "mp"), pairs)

    def trade(value, bits):
        return joint(value, lambda core: (0, bits))

    def step_one(value):
        return joint(value, lambda core: (0, 2 if core else 1))

    def step_two(value):
        return joint(value, lambda core: (0, 1 if core else 2))

    def swap(value, bits):
        return joint(value, lambda core: (bits, 0))

    def cross_one(value):
        return joint(value, lambda core: ((y_bit, 0) if core else (x_bit, 0)))

    def cross_halves(value):
        rows = value.shape[0] // 2
        return cross_one(value[:rows]), cross_one(value[rows:])

    def cross_two(value):
        return joint(value, lambda core: ((x_bit, 0) if core else (y_bit, 0)))

    wq, wk, wv = w_query.T, w_key.T, w_value.T
    spans = span_table.T

    def rows_of(count, dtype=bf16):
        return sds((count, model), dtype)

    def stack(name, *arrays):
        rows = sum(a.shape[0] for a in arrays)
        return call(stack_kernel, name, 8, arrays, [rows_of(rows)])[0]

    vectors = (ln1_gain, ln1_shift, ln2_gain, ln2_shift, b_out, b_down, b_up, b_query, b_value)
    eighth = model // 8
    vec, att_sent, ffn_sent, att_piece, ffn_piece = pl.pallas_call(
        functools.partial(prepare_kernel, len(vectors)),
        in_specs=[ANY] * (len(vectors) + 6),
        out_specs=[VMEM] * 5,
        out_shape=[rows_of(len(vectors), f32)]
        + [rows_of(eighth + SMALL), rows_of(3 * eighth)] * 2,
        scratch_shapes=[pltpu.VMEM(v.shape, bf16) for v in vectors] + [DMA((len(vectors) + 3,))],
        compiler_params=params(60),
        cost_estimate=cost("prepare"),
        name="prepare",
    )(*vectors, wq, wk, wv, w_out, w_up, w_down)
    att_one = step_one(att_sent)
    ffn_one = step_one(ffn_sent)

    win_rows = seqs * WIN
    normed, nw, qw, keys, values, mh = pl.pallas_call(
        first_kernel,
        in_specs=[SMEM] + [ANY] * 4 + [VMEM],
        out_specs=[VMEM] * 6,
        out_shape=[
            rows_of(tok_rows),
            rows_of(win_rows),
            sds((win_rows, width), bf16),
            sds((tok_rows, width), bf16),
            sds((tok_rows, width), bf16),
            sds((seqs, WIN, width), bf16),
        ],
        scratch_shapes=[
            pltpu.VMEM((seqs, length, model), bf16),
            pltpu.VMEM((3, width, model), bf16),
            DMA((seqs + 3,)),
        ],
        compiler_params=params(24),
        cost_estimate=cost("windows_forward"),
        name="windows_forward",
    )(spans, inputs, wq, wk, wv, vec)
    def pick_rows(name, ins, moves):
        outs = [rows_of(sum(part[2] for part in parts)) for parts in moves]
        return call(functools.partial(rows_kernel, moves, len(ins)), name, 8, ins, outs)

    att_pair = step_two(stack("attention_pair", after(att_piece, normed), att_one))
    ffn_pair = step_two(stack("ffn_pair", after(ffn_piece, normed), ffn_one))
    (gw,) = call(
        pick_kernel, "windows_pick", 16, (spans, after(cotangent, normed)), [rows_of(win_rows)],
        scalars=1,
    )
    att_got, biases = call(
        unpack_kernel, "attention_got", 4, (att_one, after(att_pair, gw)),
        [rows_of(3 * eighth), rows_of(3 * SMALL)],
    )
    att_over = cross_one(att_got)

    att_both = stack("attention_both", att_got, att_over)
    att_over = cross_two(att_both)
    third = 3 * eighth
    up_got, down_got = pick_rows(
        "ffn_got",
        [ffn_one, after(ffn_pair, att_both)],
        [
            ((0, 0, eighth), (1, 0, eighth), (1, third, eighth)),
            ((0, eighth, 2 * eighth), (1, eighth, 2 * eighth), (1, third + eighth, 2 * eighth)),
        ],
    )
    up_over, down_over = cross_one(up_got), cross_one(down_got)
    up_both = stack("up_both", up_got, up_over)
    up_over = cross_two(up_both)
    att_all = stack("attention_all", att_both, after(att_over, up_both))
    att_weights = [att_all, swap(att_all, core_bit)]
    own_weights = [wq, wk, wv, w_out]

    def attention_part(near, acc, weights, name):
        outs = [sds((2, length, 3 * WIDE), bf16), rows_of(length, f32)]
        if not near:
            outs += [rows_of(length), rows_of(WIN, f32), rows_of(WIN)]
        return call(
            functools.partial(local_attn_kernel, near, width), name, 20,
            (spans, acc, normed, vec, biases, *weights), outs,
            [pltpu.VMEM((2, 4 * WIDE, model), bf16), pltpu.VMEM((length, model), f32)], scalars=1,
        )

    def ffn_part(near, acc, weights, name):
        return call(
            functools.partial(local_ffn_kernel, near, eighth), name, 20,
            (acc, normed_two, vec, biases, *weights), [rows_of(length, f32 if near else bf16)],
            [pltpu.VMEM((2, model, units), bf16), pltpu.VMEM((2, units, model), bf16)],
        )[0]

    def back_part(near, acc, qkv, weights, name):
        return call(
            functools.partial(local_back_kernel, near, width), name, 20,
            (spans, acc, inputs, gresid, gb, qkv, vec, *weights),
            [rows_of(length, f32 if near else bf16)],
            [pltpu.VMEM((2, 4 * WIDE, model), bf16)], scalars=1
        )[0]

    qkv_near, resid_near = attention_part(
        True, inputs, own_weights + att_weights, "own_attention_near"
    )
    qkv_far, resid, normed_two, resid_win, normed_win = attention_part(
        False, resid_near, att_weights, "own_attention_far"
    )

    nt_one = step_one(normed_win)
    nt_pair = step_two(stack("normed_pair", normed_win, nt_one))
    down_all = stack("down_all", down_got, after(down_over, normed_win))
    up_all = stack("up_all", up_both, after(up_over, nt_one))
    ffn_weights = [up_all, swap(up_all, core_bit), down_all, swap(down_all, core_bit)]

    gresid, gb = call(
        functools.partial(own_window_kernel, eighth),
        "own_window",
        24,
        (normed_win, resid_win, gw, vec, biases, w_up, w_down, *ffn_weights),
        [rows_of(WIN, f32), rows_of(WIN + SMALL)],
        [pltpu.VMEM((3, model, units), bf16), pltpu.VMEM((3, units, model), bf16)],
    )
    gb_one = step_one(gb)
    def sum_split(keep, recv, small, which, name):
        rows = (keep.shape[0] - small) // 2 + small
        return call(
            functools.partial(split_kernel, small, which), name, 8, (keep, recv),
            [rows_of(rows, f32), rows_of(rows)],
        )

    def sum_total(mine, recv, small, name):
        rows = mine.shape[0] - small
        outs = [rows_of(rows)]
        if small:
            outs += [rows_of(small, f32), rows_of(8, f32)]
        done, *rest = call(total_kernel, name, 8, (mine, recv), outs)
        for bit in range(2, dp_bits - 1):
            done = (done.astype(f32) + swap(done, 1 << bit).astype(f32)).astype(bf16)
            rest = [part + swap(part, 1 << bit) for part in rest]
        return [done, *rest]

    def join(mine, recv, which, name):
        return call(
            functools.partial(join_kernel, which), name, 8, (mine, recv),
            [rows_of(2 * mine.shape[0])],
        )[0]

    ffn_keep, ffn_send, ffn_small = call(
        ffn_kernel,
        "windows_ffn",
        24,
        (after(normed_win, gb), nt_one, nt_pair, gw, vec, w_up, w_down),
        [rows_of(model)] * 2 + [rows_of(8, f32)],
        [pltpu.VMEM((win_rows, model), bf16)],
    )
    gb_pair = step_two(stack("branch_pair", after(gb, ffn_keep), gb_one))
    attn_args = (mh, nw, qw, keys, values, normed, wq, wk, wv, w_out)
    acc, cols = call(
        functools.partial(attn_kernel, False),
        "windows_attention_back_near",
        24,
        (gb, gb_one, *attn_args),
        [sds((4, width, model), f32), rows_of(8, f32)],
    )

    ffn_recv = swap(after(ffn_send, gb_one), core_bit)
    ffn_mine, ffn_send = sum_split(ffn_keep, ffn_recv, 0, 0, "ffn_split_one")
    ffn_recv = stack("ffn_halves", *cross_halves(ffn_send))
    ffn_acc = ffn_part(True, after(resid, ffn_send), [w_up, w_down] + ffn_weights, "own_ffn_near")
    att_rows = 2 * width + SMALL
    keep, send = call(
        functools.partial(attn_kernel, True),
        "windows_attention_back_far",
        24,
        (after(gb_pair, ffn_acc, ffn_recv), gb_pair, *attn_args, vec, ffn_small, acc, cols),
        [rows_of(att_rows)] * 2,
        [pltpu.VMEM((4, width, model), f32), pltpu.VMEM((8, model), f32)]
    )

    att_recv = swap(send, core_bit)
    ffn_mine, ffn_send = sum_split(ffn_mine, after(ffn_recv, keep), 0, 1, "ffn_split_two")
    ffn_recv = cross_two(ffn_send)
    att_mine, att_send = sum_split(keep, after(att_recv, ffn_send), SMALL, 0, "att_split_one")
    att_recv = cross_one(att_send)
    layer_out = ffn_part(False, after(ffn_acc, att_send), ffn_weights, "own_ffn_far")
    att_mine, att_send = sum_split(att_mine, after(att_recv, layer_out), SMALL, 1, "att_split_two")
    att_recv = cross_two(att_send)
    (ffn_done,) = sum_total(ffn_mine, after(ffn_recv, att_send), 0, "ffn_total")
    ffn_next = cross_two(ffn_done)
    back_acc = back_part(
        True, after(gresid, ffn_done), qkv_near, own_weights + att_weights, "own_back_near"
    )
    att_done, small, norms = sum_total(att_mine, after(att_recv, back_acc), SMALL, "att_total")
    att_next = cross_two(att_done)
    norms_got = trade(norms, 1)
    ffn_rows = join(ffn_done, after(ffn_next, att_done), 1, "ffn_join_one")
    ffn_next = cross_one(ffn_rows)
    grad_inputs = back_part(False, after(back_acc, ffn_rows), qkv_far, att_weights, "own_back_far")
    (norms,) = call(
        add_kernel, "norm_sums", 4, (norms, after(norms_got, grad_inputs)), [rows_of(8, f32)]
    )
    norms_got = trade(norms, 2)
    att_part = join(att_done, after(att_next, norms), 1, "att_join_one")
    att_next = cross_one(att_part)
    ffn_half = join(ffn_rows, after(ffn_next, att_part), 0, "ffn_join_two")
    ffn_other = swap(ffn_half, core_bit)
    grad_w_up, grad_w_down = call(
        ffn_out_kernel, "ffn_gradients", 16, (ffn_half, ffn_other), [rows_of(model, f32)] * 2
    )
    att_half = join(att_part, after(att_next, norms_got, grad_w_up), 0, "att_join_two")
    att_other = swap(att_half, core_bit)
    small_outs = call(
        small_out_kernel, "small_gradients", 4, (small, norms, after(norms_got, att_half)),
        [sds((model,), f32)] * 7 + [sds((width,), f32)] * 2,
    )
    grad_w_query, grad_w_key, grad_w_value, grad_w_out = call(
        attn_out_kernel, "attention_gradients", 16, (att_half, after(att_other, small_outs[0])),
        [rows_of(width, f32)] * 4,
    )
    (
        grad_ln1_gain, grad_ln1_shift, grad_b_up, grad_b_down, grad_b_out, grad_ln2_gain,
        grad_ln2_shift, grad_b_query, grad_b_value,
    ) = small_outs

    return (
        layer_out,
        grad_inputs,
        grad_ln1_gain,
        grad_ln1_shift,
        grad_w_query.T,
        grad_b_query,
        grad_w_key.T,
        grad_w_value.T,
        grad_b_value,
        grad_w_out,
        grad_b_out,
        grad_ln2_gain,
        grad_ln2_shift,
        grad_w_up,
        grad_b_up,
        grad_w_down,
        grad_b_down,
    )


def solution(mesh):
    return jax.shard_map(
        functools.partial(local, mesh.shape["dp"], mesh.shape["mp"]),
        mesh=mesh,
        in_specs=(
            P("dp", None),
            P("dp", None),
            P("dp", None),
            P(),
            P(),
            P(None, "mp"),
            P("mp"),
            P(None, "mp"),
            P(None, "mp"),
            P("mp"),
            P("mp", None),
            P(),
            P(),
            P(),
            P(None, "mp"),
            P("mp"),
            P("mp", None),
            P(),
        ),
        out_specs=(
            P(("dp", "mp"), None),
            P(("dp", "mp"), None),
            P(),
            P(),
            P(None, "mp"),
            P("mp"),
            P(None, "mp"),
            P(None, "mp"),
            P("mp"),
            P("mp", None),
            P(),
            P(),
            P(),
            P(None, "mp"),
            P("mp"),
            P("mp", None),
            P(),
        ),
        check_vma=False,
    )
```

```python
import functools

import jax
import jax.numpy as jnp
from jax import lax
from jax.experimental import pallas as pl
from jax.experimental.pallas import tpu as pltpu
from jax.sharding import PartitionSpec as P

HD = 64
WIN = 128
EPS = 1e-06
SMALL = 16
WIDE = 256
MIB = 1 << 20

bf16 = jnp.bfloat16
f32 = jnp.float32


def mm(left, right):
    return lax.dot_general(left, right, (((1,), (0,)), ((), ())), preferred_element_type=f32)


def mm_nt(left, right):
    return lax.dot_general(left, right, (((1,), (1,)), ((), ())), preferred_element_type=f32)


def mm_tn(left, right):
    return lax.dot_general(left, right, (((0,), (0,)), ((), ())), preferred_element_type=f32)


def row_of(vec_ref, index, cols=None):
    return vec_ref[index : index + 1, 0 : (cols or vec_ref.shape[1])]


GAIN_ONE, SHIFT_ONE, GAIN_TWO, SHIFT_TWO, B_OUT, B_DOWN, B_UP, B_QUERY, B_VALUE = range(9)


def here():
    at, own = lax.axis_index("dp"), lax.axis_index("mp")
    core = at & 1
    at_x, at_y = (at >> 1) & 1, at >> (lax.axis_size("dp").bit_length() - 2)
    turn = (at_x ^ at_y) * core
    return own, core, (at_x ^ turn, at_y ^ turn), 1 + core, 2 - core


def unit_of(values):
    centered = values - jnp.mean(values, -1, keepdims=True)
    rstd = lax.rsqrt(jnp.mean(centered * centered, -1, keepdims=True) + EPS)
    return centered * rstd, rstd


def norm_back(grad_norm, unit, rstd, gain):
    scaled = grad_norm * gain
    return rstd * (
        scaled
        - jnp.mean(scaled, -1, keepdims=True)
        - unit * jnp.mean(scaled * unit, -1, keepdims=True)
    )


def window_of(span_ref, seq, length):
    start = span_ref[0, seq]
    count = span_ref[1, seq]
    first = jnp.minimum(start, length - WIN)
    row = lax.broadcasted_iota(jnp.int32, (WIN, length), 0) + first
    col = lax.broadcasted_iota(jnp.int32, (WIN, length), 1)
    pick = row == col
    inside = pick & (row >= start) & (row < start + count)
    return pick.astype(f32).astype(bf16), inside.astype(f32).astype(bf16)


def per_head(rows, heads):
    lane = lax.broadcasted_iota(jnp.int32, (1, rows.shape[1]), 1)
    zeros = jnp.zeros_like(rows)
    parts = [
        jnp.where((lane >= h * HD) & (lane < (h + 1) * HD), rows, zeros) for h in range(heads)
    ]
    return jnp.concatenate(parts, 0)


def own_head(stacked, heads):
    rows = stacked.shape[0] // heads
    lane = lax.broadcasted_iota(jnp.int32, (1, stacked.shape[1]), 1)
    result = stacked[0:rows]
    for h in range(1, heads):
        result = jnp.where(lane >= h * HD, stacked[h * rows : (h + 1) * rows], result)
    return result


def softmax_parts(query, keys):
    scores = mm_nt(query, keys)
    terms = jnp.exp2((scores - jnp.max(scores, -1, keepdims=True)) * (0.125 * 1.4426950408889634))
    return terms, 1.0 / jnp.sum(terms, -1, keepdims=True)


def attend(query, keys, values, heads):
    terms, inverse = softmax_parts(per_head(query, heads), keys)
    return own_head(mm(terms.astype(bf16), values) * inverse, heads).astype(bf16)


def attend_back(query, keys, values, grad_mixed, heads):
    query, grad_mixed = per_head(query, heads), per_head(grad_mixed, heads)
    terms, inverse = softmax_parts(query, keys)
    prob = terms * inverse
    grad_prob = mm_nt(grad_mixed, values)
    row_dot = jnp.sum(prob * grad_prob, -1, keepdims=True)
    grad_scores = (prob * (grad_prob - row_dot)).astype(bf16)
    grad_q = own_head(mm(grad_scores, keys), heads) * 0.125
    grad_k = mm_tn(grad_scores, query) * 0.125
    grad_v = mm_tn(prob.astype(bf16), grad_mixed)
    return grad_q.astype(bf16), grad_k.astype(bf16), grad_v.astype(bf16)


def gelu_parts(values):
    phi = 0.5 * (1.0 + lax.erf(values * 0.7071067811865476))
    return phi


def start_all(copies):
    for copy in copies:
        copy.start()


def wait_all(copies):
    for copy in copies:
        copy.wait()


def prepare_kernel(count, *refs):
    vectors, (wq_ref, wk_ref, wv_ref, wo_ref, wup_ref, wdown_ref) = refs[:count], refs[count : count + 6]
    vec_ref, att_ref, ffn_ref, att_kept_ref, ffn_kept_ref = refs[count + 6 : count + 11]
    *rows_s, sems = refs[count + 11 :]
    _, core, (first, second), _, _ = here()
    rows = ffn_ref.shape[0] // 3
    place = core * 4 + first * 2 + second
    copies = [
        pltpu.make_async_copy(ref, rows_s[i], sems.at[i]) for i, ref in enumerate(vectors)
    ]
    weights = []
    for i, (ref, row, count_rows, to) in enumerate(
        ((wup_ref, place * rows, rows, 0), (wdown_ref, (core * 2 + first) * 2 * rows, 2 * rows, rows))
    ):
        weights.append(
            pltpu.make_async_copy(
                ref.at[pl.ds(pl.multiple_of(row, 16), count_rows), :],
                ffn_ref.at[pl.ds(to, count_rows), :],
                sems.at[count + i],
            )
        )
    attention = [
        pltpu.make_async_copy(
            ref.at[pl.ds(pl.multiple_of(second * rows, 16), rows), :],
            att_ref.at[pl.ds(0, rows), :],
            sems.at[count + 2],
        )
        for ref in (wq_ref, wk_ref, wv_ref, wo_ref)
    ]
    for i, copy in enumerate(attention):
        pl.when(core * 2 + first == i)(copy.start)
    start_all(weights + copies)
    wait_all(copies)
    vec_ref[...] = jnp.zeros_like(vec_ref)
    for i, ref in enumerate(vectors):
        size = ref.shape[0]
        vec_ref[i : i + 1, 0:size] = rows_s[i][...].astype(f32).reshape(1, size)
    bias = [row_of(vec_ref, index) for index in (B_UP, B_QUERY, B_VALUE)]
    bias = jnp.concatenate(bias + [jnp.zeros((SMALL - 3, vec_ref.shape[1]), f32)], 0)
    att_ref[rows:, :] = bias.astype(bf16)
    wait_all(weights + attention[:1])
    att_kept_ref[...] = att_ref[...]
    ffn_kept_ref[...] = ffn_ref[...]


def first_kernel(
    span_ref, x_hbm, wq_hbm, wk_hbm, wv_hbm, vec_ref,
    normed_ref, nw_ref, qw_ref, k_ref, v_ref, mh_ref, x_s, w_s, sems,
):
    seqs = span_ref.shape[1]
    length = x_hbm.shape[0] // seqs
    width = wq_hbm.shape[0]
    inputs = [
        pltpu.make_async_copy(x_hbm.at[pl.ds(seq * length, length), :], x_s.at[seq], sems.at[seq])
        for seq in range(seqs)
    ]
    weights = [
        pltpu.make_async_copy(ref, w_s.at[i], sems.at[seqs + i])
        for i, ref in enumerate((wq_hbm, wk_hbm, wv_hbm))
    ]
    start_all(inputs[:1] + weights + inputs[1:])
    for seq in range(seqs):
        rows = slice(seq * length, (seq + 1) * length)
        win = slice(seq * WIN, (seq + 1) * WIN)
        inputs[seq].wait()
        unit, _ = unit_of(x_s[seq].astype(f32))
        normed = (unit * row_of(vec_ref, GAIN_ONE) + row_of(vec_ref, SHIFT_ONE)).astype(bf16)
        normed_ref[rows, :] = normed
        pick, _ = window_of(span_ref, seq, length)
        nw = mm(pick, normed).astype(bf16)
        nw_ref[win, :] = nw
        if seq == 0:
            wait_all(weights)
        query = (mm_nt(nw, w_s[0]) + row_of(vec_ref, B_QUERY, width)).astype(bf16)
        keys = mm_nt(normed, w_s[1]).astype(bf16)
        values = (mm_nt(normed, w_s[2]) + row_of(vec_ref, B_VALUE, width)).astype(bf16)
        qw_ref[win, :] = query
        k_ref[rows, :] = keys
        v_ref[rows, :] = values
        mh_ref[seq] = attend(query, keys, values, width // HD)


def pick_kernel(span_ref, cot_ref, gw_ref):
    seqs = span_ref.shape[1]
    length = cot_ref.shape[0] // seqs
    for seq in range(seqs):
        _, inside = window_of(span_ref, seq, length)
        rows = slice(seq * length, (seq + 1) * length)
        gw_ref[seq * WIN : (seq + 1) * WIN, :] = mm(inside, cot_ref[rows, :]).astype(bf16)


def feed_back(normed, grad_out, up, down, bias):
    pre = mm(normed, up) + bias
    phi = gelu_parts(pre)
    slope = phi + pre * (0.3989422804014327 * jnp.exp(-0.5 * pre * pre))
    grad_pre = (slope * mm_nt(grad_out, down)).astype(bf16)
    return (pre * phi).astype(bf16), grad_pre


def ffn_kernel(
    own_ref, one_ref, pair_ref, gw_ref, vec_ref, wup_ref, wdown_ref,
    keep_ref, send_ref, small_ref, normed_s,
):
    own, core, _, one, two = here()
    sources = (
        (own, own_ref, 0), (own ^ one, one_ref, 0), (own ^ two, pair_ref, 0),
        (own ^ one ^ two, pair_ref, WIN),
    )
    for seq, ref, row in sources:
        normed_s[pl.ds(pl.multiple_of(seq * WIN, 16), WIN), :] = ref[row : row + WIN, :]
    normed, grad_out = normed_s[...], gw_ref[...]
    hidden, grad_pre = feed_back(
        normed, grad_out, wup_ref[...], wdown_ref[...], row_of(vec_ref, B_UP)
    )
    grad_up = mm_tn(normed, grad_pre).astype(bf16)
    grad_down = mm_tn(hidden, grad_out).astype(bf16)

    @pl.when(core == 0)
    def _():
        keep_ref[...] = grad_up
        send_ref[...] = grad_down

    @pl.when(core == 1)
    def _():
        keep_ref[...] = grad_down
        send_ref[...] = grad_up

    small_ref[...] = jnp.zeros_like(small_ref)
    small_ref[0:1, :] = jnp.sum(grad_pre.astype(f32), 0, keepdims=True)
    small_ref[1:2, :] = jnp.sum(grad_out.astype(f32), 0, keepdims=True)


def own_window_kernel(
    rows, normed_ref, resid_ref, gw_ref, vec_ref, bias_ref, own_up_ref, own_down_ref, *refs
):
    *stacks, gresid_ref, gb_ref, up_s, down_s = refs
    normed = normed_ref[...]
    grad_out = gw_ref[pl.ds(pl.multiple_of(here()[0] * WIN, 16), WIN), :]
    grad_norm = None
    for shard in range(-1, 3):
        if shard < 0:
            up, down, bias = own_up_ref[...], own_down_ref[...], row_of(vec_ref, B_UP)
        else:
            lay_ffn(up_s.at[shard], down_s.at[shard], stacks, shard, rows)
            up, down = up_s[shard], down_s[shard]
            bias = bias_ref[shard * SMALL : (shard + 1) * SMALL, :].astype(f32)[0:1]
        _, grad_pre = feed_back(normed, grad_out, up, down, bias)
        part = mm_nt(grad_pre, up)
        grad_norm = part if grad_norm is None else grad_norm + part
    unit, rstd = unit_of(resid_ref[...])
    grad = grad_out.astype(f32) + norm_back(grad_norm, unit, rstd, row_of(vec_ref, GAIN_TWO))
    gresid_ref[...] = grad
    gb_ref[0:WIN, :] = grad.astype(bf16)
    sums = [jnp.sum(grad_norm * unit, 0, keepdims=True), jnp.sum(grad_norm, 0, keepdims=True)]
    sums.append(jnp.zeros((SMALL - 2, grad.shape[1]), f32))
    gb_ref[WIN : WIN + SMALL, :] = jnp.concatenate(sums, 0).astype(bf16)


def attn_kernel(
    last, ga_ref, gb_ref, mh_ref, nw_ref, qw_ref, k_ref, v_ref, normed_ref,
    wq_ref, wk_ref, wv_ref, wo_ref, *refs,
):
    if last:
        vec_ref, small_ref, acc_in_ref, col_in_ref = refs[:4]
        keep_ref, send_ref, acc_ref, col_ref = refs[4:]
        acc_ref[...] = acc_in_ref[...]
        col_ref[...] = col_in_ref[...]
    else:
        acc_ref, col_ref = refs
        acc_ref[...] = jnp.zeros_like(acc_ref)
        col_ref[...] = jnp.zeros_like(col_ref)
    own, core, _, one, two = here()
    width, model = wq_ref.shape
    seqs = mh_ref.shape[0]
    length = normed_ref.shape[0] // seqs
    first = own ^ two if last else own
    block_rows = WIN + SMALL
    for seq, ref, row in ((first, ga_ref, 0), (first ^ one, gb_ref, block_rows if last else 0)):
        rows = pl.ds(pl.multiple_of(seq * length, length), length)
        win = pl.ds(pl.multiple_of(seq * WIN, WIN), WIN)
        grad_branch = ref[row : row + WIN, :]
        sums = ref[row + WIN : row + block_rows, :].astype(f32)
        grad_mixed = mm_nt(grad_branch, wo_ref[...]).astype(bf16)
        grad_q, grad_k, grad_v = attend_back(
            qw_ref[win, :], k_ref[rows, :], v_ref[rows, :], grad_mixed, width // HD
        )
        normed = normed_ref[rows, :]
        acc_ref[0] += mm_tn(grad_q, nw_ref[win, :])
        acc_ref[1] += mm_tn(grad_k, normed)
        acc_ref[2] += mm_tn(grad_v, normed)
        acc_ref[3] += mm_tn(mh_ref[seq], grad_branch)
        for i, grad in enumerate((grad_q, grad_k, grad_v, grad_branch)):
            col_ref[i : i + 1, 0 : grad.shape[1]] += jnp.sum(grad.astype(f32), 0, keepdims=True)
        col_ref[4:6, :] += sums[0:2]
    if not last:
        return

    sums = jnp.zeros((1, model), f32)
    total = jnp.zeros((1, model), f32)
    pad = jnp.zeros((1, model - width), f32)
    for i, w_ref in enumerate((wq_ref, wk_ref, wv_ref)):
        sums += jnp.sum(w_ref[...].astype(f32) * acc_ref[i], 0, keepdims=True)
        cols = col_ref[i : i + 1, 0:width]
        high = cols.astype(bf16)
        low = (cols - high.astype(f32)).astype(bf16)
        both = jnp.concatenate([high, low, jnp.zeros((14, width), bf16)], 0)
        total += jnp.sum(mm(both, w_ref[...]), 0, keepdims=True)
    gain = (sums - row_of(vec_ref, SHIFT_ONE) * total) / row_of(vec_ref, GAIN_ONE)
    small = jnp.concatenate(
        [
            gain,
            total,
            small_ref[0:2, :],
            col_ref[3:6, :],
            jnp.concatenate([col_ref[0:1, 0:width], pad], 1),
            jnp.concatenate([col_ref[2:3, 0:width], pad], 1),
            jnp.zeros((SMALL - 9, model), f32),
        ],
        0,
    ).astype(bf16)
    first = jnp.concatenate([acc_ref[0], acc_ref[1]], 0).astype(bf16)
    second = jnp.concatenate([acc_ref[2], acc_ref[3]], 0).astype(bf16)
    rows = first.shape[0]
    keep_ref[rows : rows + SMALL, :] = small
    send_ref[rows : rows + SMALL, :] = small

    @pl.when(core == 0)
    def _():
        keep_ref[0:rows, :] = first
        send_ref[0:rows, :] = second

    @pl.when(core == 1)
    def _():
        keep_ref[0:rows, :] = second
        send_ref[0:rows, :] = first


def split_kernel(small, which, keep_ref, recv_ref, mine_ref, send_ref):
    bit = here()[2][which]
    rows = mine_ref.shape[0] - small

    def total(first, count):
        part = pl.ds(first, count)
        return keep_ref[part, :].astype(f32) + recv_ref[part, :].astype(f32)

    mine_ref[0:rows, :] = total(pl.multiple_of(bit * rows, 16), rows)
    send_ref[0:rows, :] = total(pl.multiple_of((1 - bit) * rows, 16), rows).astype(bf16)
    if small:
        block = total(2 * rows, small).astype(bf16)
        mine_ref[rows:, :] = block.astype(f32)
        send_ref[rows:, :] = block


def total_kernel(mine_ref, recv_ref, out_ref):
    out_ref[...] = (mine_ref[...] + recv_ref[...].astype(f32)).astype(bf16)


def pair_kernel(left_ref, right_ref, out_ref):
    out_ref[...] = (left_ref[...].astype(f32) + right_ref[...].astype(f32)).astype(bf16)


def last_pair_kernel(left_ref, right_ref, out_ref, small_ref, norms_ref):
    total = left_ref[...].astype(f32) + right_ref[...].astype(f32)
    rows = out_ref.shape[0]
    out_ref[...] = total[0:rows].astype(bf16)
    small_ref[...] = total[rows:]
    norms_ref[...] = total[rows : rows + 8]


def join_kernel(which, mine_ref, recv_ref, out_ref):
    bit = here()[2][which]
    rows = mine_ref.shape[0]
    out_ref[pl.ds(pl.multiple_of(bit * rows, 16), rows), :] = mine_ref[...]
    out_ref[pl.ds(pl.multiple_of((1 - bit) * rows, 16), rows), :] = recv_ref[...]


def add_kernel(left_ref, right_ref, out_ref):
    out_ref[...] = left_ref[...] + right_ref[...]


def small_out_kernel(small_ref, left_ref, right_ref, *out_refs):
    norms = left_ref[...] + right_ref[...]
    for i, ref in enumerate(out_refs):
        row = norms[i : i + 1] if i < 2 else small_ref[i : i + 1, :]
        ref[...] = row[:, 0 : ref.shape[0]].reshape(ref.shape[0])


def ffn_out_kernel(mine_ref, other_ref, up_ref, down_ref):
    core = here()[1]

    def write(first_ref, second_ref):
        up_ref[...] = first_ref[...].astype(f32)
        down_ref[...] = second_ref[...].astype(f32)

    pl.when(core == 0)(lambda: write(mine_ref, other_ref))
    pl.when(core == 1)(lambda: write(other_ref, mine_ref))


def attn_out_kernel(mine_ref, other_ref, q_ref, k_ref, v_ref, o_ref):
    core = here()[1]
    width = o_ref.shape[0]

    def write(first_ref, second_ref):
        q_ref[...] = first_ref[0:width, :].astype(f32)
        k_ref[...] = first_ref[width : 2 * width, :].astype(f32)
        v_ref[...] = second_ref[0:width, :].astype(f32)
        o_ref[...] = second_ref[width : 2 * width, :].astype(f32)

    pl.when(core == 0)(lambda: write(mine_ref, other_ref))
    pl.when(core == 1)(lambda: write(other_ref, mine_ref))


def unpack_kernel(one_ref, pair_ref, got_ref, bias_ref):
    each = one_ref.shape[0]
    rows = each - SMALL
    for i, (ref, row) in enumerate(((one_ref, 0), (pair_ref, 0), (pair_ref, each))):
        got_ref[i * rows : (i + 1) * rows, :] = ref[row : row + rows, :]
        bias_ref[i * SMALL : (i + 1) * SMALL, :] = ref[row + rows : row + each, :]


def rows_kernel(moves, count, *refs):
    for parts, out_ref in zip(moves, refs[count:]):
        to = 0
        for source, row, rows in parts:
            out_ref[to : to + rows, :] = refs[source][row : row + rows, :]
            to += rows


def stack_kernel(*refs):
    out_ref = refs[-1]
    row = 0
    for ref in refs[:-1]:
        out_ref[row : row + ref.shape[0], :] = ref[...]
        row += ref.shape[0]


def own_rows(ref, length):
    return ref[pl.ds(pl.multiple_of(here()[0] * length, 16), length), :]


def eighths(refs, shard, rows):
    _, own_core, (first, second), _, _ = here()
    for flip, ref in enumerate(refs):
        bits = (second, first) if flip else (first, second)
        at = (1, 0, 2)[shard] if flip else shard
        for i in range(4):
            place = (own_core ^ flip) * 4 + (bits[0] ^ (i % 2)) * 2 + (bits[1] ^ (i // 2))
            yield place, ref, (i * 3 + at) * rows


def lay_attention(w_s, n, own_refs, stacks, shard, rows):
    if shard < 0:
        for i, ref in enumerate(own_refs):
            w_s[n, i * WIDE : i * WIDE + rows, :] = ref[...]
    else:
        piece = rows // 2
        for place, ref, row in eighths(stacks, shard, piece):
            to = pl.multiple_of((place >> 1) * WIDE + (place & 1) * piece, 16)
            w_s[n, pl.ds(to, piece), :] = ref[row : row + piece, :]


def lay_ffn(up_s, down_s, stacks, shard, rows):
    for place, ref, row in eighths(stacks[:2], shard, rows):
        up_s[pl.ds(pl.multiple_of(place * rows, 16), rows), :] = ref[row : row + rows, :]
    _, own_core, (first, second), _, _ = here()
    each = 2 * rows
    for flip, ref in enumerate(stacks[2:]):
        at = (1, 0, 2)[shard] if flip else shard
        for i in range(2):
            place = (own_core ^ flip) * 2 + ((second if flip else first) ^ i)
            row = (i * 3 + at) * each
            to = pl.ds(pl.multiple_of(place * each, 16), each)
            down_s[to, :] = ref[row : row + each, :]


def local_attn_kernel(near, rows, span_ref, acc_ref, normed_ref, vec_ref, bias_ref, *refs):
    own = 4 if near else 0
    own_refs, stacks, rest = refs[:own], refs[own : own + 2], refs[own + 2 :]
    if near:
        qkv_ref, resid_ref, w_s, acc_s = rest
    else:
        qkv_ref, resid_ref, normed_two_ref, resid_win_ref, normed_win_ref, w_s, acc_s = rest
    length, model = resid_ref.shape
    normed = own_rows(normed_ref, length)
    if near:
        acc_s[...] = own_rows(acc_ref, length).astype(f32)
    else:
        acc_s[...] = acc_ref[...]
    pad = jnp.zeros((1, WIDE - rows), f32)
    for n, shard in enumerate((-1, 0) if near else (1, 2)):
        for i in range(3):
            w_s[n, i * WIDE + rows : (i + 1) * WIDE, :] = jnp.zeros((WIDE - rows, model), bf16)
        lay_attention(w_s, n, own_refs, stacks, shard, rows)
        if shard < 0:
            bias_q, bias_v = row_of(vec_ref, B_QUERY, rows), row_of(vec_ref, B_VALUE, rows)
        else:
            block = bias_ref[shard * SMALL : (shard + 1) * SMALL, :].astype(f32)
            bias_q, bias_v = block[1:2, 0:rows], block[2:3, 0:rows]
        bias = jnp.concatenate([bias_q, pad, jnp.zeros((1, WIDE), f32), bias_v, pad], 1)
        qkv = (mm_nt(normed, w_s[n, 0 : 3 * WIDE, :]) + bias).astype(bf16)
        qkv_ref[n] = qkv
        keys, values = qkv[:, WIDE : 2 * WIDE], qkv[:, 2 * WIDE : 3 * WIDE]
        mixed = jnp.concatenate(
            [
                attend(qkv[first : first + WIN, 0:WIDE], keys, values, rows // HD)
                for first in range(0, length, WIN)
            ],
            0,
        )
        acc_s[...] += mm(mixed[:, 0:rows], w_s[n, 3 * WIDE : 3 * WIDE + rows, :])
    resid = acc_s[...]
    if not near:
        resid += row_of(vec_ref, B_OUT)
        unit, _ = unit_of(resid)
        normed = (unit * row_of(vec_ref, GAIN_TWO) + row_of(vec_ref, SHIFT_TWO)).astype(bf16)
        normed_two_ref[...] = normed
        pick, _ = window_of(span_ref, here()[0], length)
        normed_win_ref[...] = mm(pick, normed).astype(bf16)
        high = resid.astype(bf16)
        rest = resid - high.astype(f32)
        low = rest.astype(bf16)
        last = (rest - low.astype(f32)).astype(bf16)
        resid_win_ref[...] = mm(pick, high) + mm(pick, low) + mm(pick, last)
    resid_ref[...] = resid


def local_back_kernel(
    near, rows, span_ref, acc_ref, x_ref, gresid_ref, gb_ref, qkv_ref, vec_ref, *refs
):
    own = 4 if near else 0
    own_refs, stacks = refs[:own], refs[own : own + 2]
    out_ref, w_s = refs[own + 2 :]
    length, model = out_ref.shape
    pick, _ = window_of(span_ref, here()[0], length)
    total = None if near else acc_ref[...]
    for n, shard in enumerate((-1, 0) if near else (1, 2)):
        for i in range(3):
            w_s[n, i * WIDE + rows : (i + 1) * WIDE, :] = jnp.zeros((WIDE - rows, model), bf16)
        lay_attention(w_s, n, own_refs, stacks, shard, rows)
        qkv = qkv_ref[n]
        query = mm(pick, qkv[:, 0:WIDE]).astype(bf16)
        w_out = w_s[n, 3 * WIDE : 3 * WIDE + rows, :]
        grad_mixed = mm_nt(gb_ref[0:WIN, :], w_out).astype(bf16)
        grad_mixed = jnp.concatenate([grad_mixed, jnp.zeros((WIN, WIDE - rows), bf16)], 1)
        grad_q, grad_k, grad_v = attend_back(
            query, qkv[:, WIDE : 2 * WIDE], qkv[:, 2 * WIDE : 3 * WIDE], grad_mixed, rows // HD
        )
        grad_q = mm_tn(pick, grad_q).astype(bf16)
        part = mm(jnp.concatenate([grad_q, grad_k, grad_v], 1), w_s[n, 0 : 3 * WIDE, :])
        total = part if total is None else total + part
    if near:
        out_ref[...] = total
    else:
        unit, rstd = unit_of(own_rows(x_ref, length).astype(f32))
        grad = norm_back(total, unit, rstd, row_of(vec_ref, GAIN_ONE))
        resid = gresid_ref[...]
        high = resid.astype(bf16)
        low = (resid - high.astype(f32)).astype(bf16)
        out_ref[...] = (grad + mm_tn(pick, high) + mm_tn(pick, low)).astype(bf16)


def local_ffn_kernel(near, rows, acc_ref, normed_ref, vec_ref, bias_ref, *refs):
    own = 2 if near else 0
    own_refs, stacks = refs[:own], refs[own : own + 4]
    out_ref, up_s, down_s = refs[own + 4 :]
    normed = normed_ref[...]
    total = acc_ref[...]
    for n, shard in enumerate((-1, 0) if near else (1, 2)):
        if shard < 0:
            up, down, bias = own_refs[0][...], own_refs[1][...], row_of(vec_ref, B_UP)
        else:
            lay_ffn(up_s.at[n], down_s.at[n], stacks, shard, rows)
            up, down = up_s[n], down_s[n]
            bias = bias_ref[shard * SMALL : (shard + 1) * SMALL, :].astype(f32)[0:1]
        pre = mm(normed, up) + bias
        hidden = (pre * gelu_parts(pre)).astype(bf16)
        total += mm(hidden, down)
    if near:
        out_ref[...] = total
    else:
        out_ref[...] = (total + row_of(vec_ref, B_DOWN)).astype(bf16)


def sds(shape, dtype):
    return jax.ShapeDtypeStruct(shape, dtype)


def params(mib=48):
    return pltpu.CompilerParams(vmem_limit_bytes=mib * MIB)


LONG = 30


MICROS = {
    "prepare": 2.5, "windows_forward": 8, "windows_pick": 1.2, "own_attention_own": 2.7,
    "own_attention_rest": 9.0, "own_window": 4.1, "own_probabilities": 3.5, "windows_ffn": 3.4,
    "windows_attention_back_near": 3.3, "windows_attention_back_far": 3.9, "own_ffn_near": 2.8,
    "own_ffn_far": 3.8, "own_back_near": 4.8, "own_back_far": 6.1, "ffn_gradients": 2.5,
    "attention_gradients": 1.6, "small_gradients": 0.6,
}


def cost(name):
    micros = MICROS.get(name, 0.1) * 0.1
    return pl.CostEstimate(
        flops=int(micros * 1e9), bytes_accessed=int(micros * 3e6), transcendentals=0
    )


SMEM = pl.BlockSpec(memory_space=pltpu.SMEM)
VMEM = pl.BlockSpec(memory_space=pltpu.VMEM)
ANY = pl.BlockSpec(memory_space=pl.ANY)
DMA = pltpu.SemaphoreType.DMA


def after(value, *deps):
    return lax.optimization_barrier((value,) + deps)[0]


def call(kernel, name, mib, args, outs, scratch=(), scalars=0):
    return pl.pallas_call(
        kernel,
        in_specs=[SMEM] * scalars + [VMEM] * (len(args) - scalars),
        out_specs=[VMEM] * len(outs),
        out_shape=outs,
        scratch_shapes=list(scratch),
        compiler_params=params(mib),
        cost_estimate=cost(name),
        name=name,
    )(*args)


def local(
    dp_size, mp_size, inputs, cotangent, span_table, ln1_gain, ln1_shift, w_query, b_query, w_key,
    w_value, b_value, w_out, b_out, ln2_gain, ln2_shift, w_up, b_up, w_down, b_down,
):
    tok_rows, model = inputs.shape
    seqs = span_table.shape[0]
    length = tok_rows // seqs
    width = w_query.shape[1]
    units = w_up.shape[1]
    dp_bits = dp_size.bit_length() - 1
    core_bit, x_bit, y_bit = 1, 2, 1 << (dp_bits - 1)
    def joint(value, flip):
        pairs = []
        for i in range(dp_size):
            for j in range(mp_size):
                dp_flip, mp_flip = flip(i & 1)
                pairs.append((i * mp_size + j, (i ^ dp_flip) * mp_size + (j ^ mp_flip)))
        return lax.ppermute(value, ("dp", "mp"), pairs)

    def trade(value, bits):
        return joint(value, lambda core: (0, bits))

    def step_one(value):
        return joint(value, lambda core: (0, 2 if core else 1))

    def step_two(value):
        return joint(value, lambda core: (0, 1 if core else 2))

    def swap(value, bits):
        return joint(value, lambda core: (bits, 0))

    def cross_one(value):
        return joint(value, lambda core: ((y_bit, 0) if core else (x_bit, 0)))

    def cross_halves(value):
        rows = value.shape[0] // 2
        return cross_one(value[:rows]), cross_one(value[rows:])

    def cross_two(value):
        return joint(value, lambda core: ((x_bit, 0) if core else (y_bit, 0)))

    wq, wk, wv = w_query.T, w_key.T, w_value.T
    spans = span_table.T

    def rows_of(count, dtype=bf16):
        return sds((count, model), dtype)

    def stack(name, *arrays):
        rows = sum(a.shape[0] for a in arrays)
        return call(stack_kernel, name, 8, arrays, [rows_of(rows)])[0]

    vectors = (ln1_gain, ln1_shift, ln2_gain, ln2_shift, b_out, b_down, b_up, b_query, b_value)
    eighth = model // 8
    vec, att_sent, ffn_sent, att_piece, ffn_piece = pl.pallas_call(
        functools.partial(prepare_kernel, len(vectors)),
        in_specs=[ANY] * (len(vectors) + 6),
        out_specs=[VMEM] * 5,
        out_shape=[rows_of(len(vectors), f32)]
        + [rows_of(eighth + SMALL), rows_of(3 * eighth)] * 2,
        scratch_shapes=[pltpu.VMEM(v.shape, bf16) for v in vectors] + [DMA((len(vectors) + 3,))],
        compiler_params=params(60),
        cost_estimate=cost("prepare"),
        name="prepare",
    )(*vectors, wq, wk, wv, w_out, w_up, w_down)
    att_one = step_one(att_sent)
    ffn_one = step_one(ffn_sent)

    win_rows = seqs * WIN
    normed, nw, qw, keys, values, mh = pl.pallas_call(
        first_kernel,
        in_specs=[SMEM] + [ANY] * 4 + [VMEM],
        out_specs=[VMEM] * 6,
        out_shape=[
            rows_of(tok_rows),
            rows_of(win_rows),
            sds((win_rows, width), bf16),
            sds((tok_rows, width), bf16),
            sds((tok_rows, width), bf16),
            sds((seqs, WIN, width), bf16),
        ],
        scratch_shapes=[
            pltpu.VMEM((seqs, length, model), bf16),
            pltpu.VMEM((3, width, model), bf16),
            DMA((seqs + 3,)),
        ],
        compiler_params=params(24),
        cost_estimate=cost("windows_forward"),
        name="windows_forward",
    )(spans, inputs, wq, wk, wv, vec)
    def pick_rows(name, ins, moves):
        outs = [rows_of(sum(part[2] for part in parts)) for parts in moves]
        return call(functools.partial(rows_kernel, moves, len(ins)), name, 8, ins, outs)

    att_pair = step_two(stack("attention_pair", after(att_piece, normed), att_one))
    ffn_pair = step_two(stack("ffn_pair", after(ffn_piece, normed), ffn_one))
    (gw,) = call(
        pick_kernel, "windows_pick", 16, (spans, after(cotangent, normed)), [rows_of(win_rows)],
        scalars=1,
    )
    att_got, biases = call(
        unpack_kernel, "attention_got", 4, (att_one, after(att_pair, gw)),
        [rows_of(3 * eighth), rows_of(3 * SMALL)],
    )
    att_over = cross_one(att_got)

    att_both = stack("attention_both", att_got, att_over)
    att_over = cross_two(att_both)
    third = 3 * eighth
    up_got, down_got = pick_rows(
        "ffn_got",
        [ffn_one, after(ffn_pair, att_both)],
        [
            ((0, 0, eighth), (1, 0, eighth), (1, third, eighth)),
            ((0, eighth, 2 * eighth), (1, eighth, 2 * eighth), (1, third + eighth, 2 * eighth)),
        ],
    )
    up_over, down_over = cross_one(up_got), cross_one(down_got)
    up_both = stack("up_both", up_got, up_over)
    up_over = cross_two(up_both)
    att_all = stack("attention_all", att_both, after(att_over, up_both))
    att_weights = [att_all, swap(att_all, core_bit)]
    own_weights = [wq, wk, wv, w_out]

    def attention_part(near, acc, weights, name):
        outs = [sds((2, length, 3 * WIDE), bf16), rows_of(length, f32)]
        if not near:
            outs += [rows_of(length), rows_of(WIN, f32), rows_of(WIN)]
        return call(
            functools.partial(local_attn_kernel, near, width), name, 16,
            (spans, acc, normed, vec, biases, *weights), outs,
            [pltpu.VMEM((2, 4 * WIDE, model), bf16), pltpu.VMEM((length, model), f32)], scalars=1,
        )

    def ffn_part(near, acc, weights, name):
        return call(
            functools.partial(local_ffn_kernel, near, eighth), name, 16,
            (acc, normed_two, vec, biases, *weights), [rows_of(length, f32 if near else bf16)],
            [pltpu.VMEM((2, model, units), bf16), pltpu.VMEM((2, units, model), bf16)],
        )[0]

    def back_part(near, acc, qkv, weights, name):
        return call(
            functools.partial(local_back_kernel, near, width), name, 16,
            (spans, acc, inputs, gresid, gb, qkv, vec, *weights),
            [rows_of(length, f32 if near else bf16)],
            [pltpu.VMEM((2, 4 * WIDE, model), bf16)], scalars=1
        )[0]

    qkv_near, resid_near = attention_part(
        True, inputs, own_weights + att_weights, "own_attention_near"
    )
    qkv_far, resid, normed_two, resid_win, normed_win = attention_part(
        False, resid_near, att_weights, "own_attention_far"
    )

    nt_one = step_one(normed_win)
    nt_pair = step_two(stack("normed_pair", normed_win, nt_one))
    down_all = stack("down_all", down_got, after(down_over, normed_win))
    up_all = stack("up_all", up_both, after(up_over, nt_one))
    ffn_weights = [up_all, swap(up_all, core_bit), down_all, swap(down_all, core_bit)]

    gresid, gb = call(
        functools.partial(own_window_kernel, eighth),
        "own_window",
        24,
        (normed_win, resid_win, gw, vec, biases, w_up, w_down, *ffn_weights),
        [rows_of(WIN, f32), rows_of(WIN + SMALL)],
        [pltpu.VMEM((3, model, units), bf16), pltpu.VMEM((3, units, model), bf16)],
    )
    gb_one = step_one(gb)
    def sum_split(keep, recv, small, which, name):
        rows = (keep.shape[0] - small) // 2 + small
        return call(
            functools.partial(split_kernel, small, which), name, 8, (keep, recv),
            [rows_of(rows, f32), rows_of(rows)],
        )

    def sum_total(mine, recv, name):
        return call(total_kernel, name, 8, (mine, recv), [rows_of(mine.shape[0])])[0]

    def across_two(rows, name):
        for bit in range(2, dp_bits - 1):
            rows = pair(rows, swap(rows, 1 << bit), name)
        return rows, cross_two(rows)

    def pair(left, right, name):
        return call(pair_kernel, name, 8, (left, right), [rows_of(left.shape[0])])[0]

    def join(mine, recv, which, name):
        return call(
            functools.partial(join_kernel, which), name, 8, (mine, recv),
            [rows_of(2 * mine.shape[0])],
        )[0]

    ffn_keep, ffn_send, ffn_small = call(
        ffn_kernel,
        "windows_ffn",
        24,
        (after(normed_win, gb), nt_one, nt_pair, gw, vec, w_up, w_down),
        [rows_of(model)] * 2 + [rows_of(8, f32)],
        [pltpu.VMEM((win_rows, model), bf16)],
    )
    gb_pair = step_two(stack("branch_pair", after(gb, ffn_keep), gb_one))
    attn_args = (mh, nw, qw, keys, values, normed, wq, wk, wv, w_out)
    acc, cols = call(
        functools.partial(attn_kernel, False),
        "windows_attention_back_near",
        24,
        (gb, gb_one, *attn_args),
        [sds((4, width, model), f32), rows_of(8, f32)],
    )

    ffn_recv = swap(after(ffn_send, gb_one), core_bit)
    ffn_mine, ffn_send = sum_split(ffn_keep, ffn_recv, 0, 0, "ffn_split_one")
    ffn_recv = stack("ffn_halves", *cross_halves(ffn_send))
    ffn_acc = ffn_part(True, after(resid, ffn_send), [w_up, w_down] + ffn_weights, "own_ffn_near")
    att_rows = 2 * width + SMALL
    keep, send = call(
        functools.partial(attn_kernel, True),
        "windows_attention_back_far",
        24,
        (after(gb_pair, ffn_acc, ffn_recv), gb_pair, *attn_args, vec, ffn_small, acc, cols),
        [rows_of(att_rows)] * 2,
        [pltpu.VMEM((4, width, model), f32), pltpu.VMEM((8, model), f32)]
    )

    att_recv = swap(send, core_bit)
    ffn_sum, ffn_recv = across_two(
        sum_total(ffn_mine, after(ffn_recv, keep), "ffn_total"), "ffn_more"
    )
    att_mine, att_send = sum_split(keep, after(att_recv, ffn_sum), SMALL, 0, "att_split")
    att_recv = cross_one(att_send)
    layer_out = ffn_part(False, after(ffn_acc, att_send), ffn_weights, "own_ffn_far")
    att_sum, att_recv = across_two(
        sum_total(att_mine, after(att_recv, layer_out), "att_total"), "att_more"
    )
    back_acc = back_part(
        True, after(gresid, att_sum), qkv_near, own_weights + att_weights, "own_back_near"
    )
    ffn_rows = pair(ffn_sum, after(ffn_recv, att_sum), "ffn_pair_two")
    ffn_next = cross_one(ffn_rows)
    att_rows, small, norms = call(
        last_pair_kernel, "att_pair_two", 8, (att_sum, after(att_recv, back_acc)),
        [rows_of(width), rows_of(SMALL, f32), rows_of(8, f32)],
    )
    att_next = cross_one(att_rows)
    norms_got = trade(norms, 1)
    grad_inputs = back_part(False, after(back_acc, att_rows), qkv_far, att_weights, "own_back_far")
    (norms,) = call(
        add_kernel, "norm_sums", 4, (norms, after(norms_got, grad_inputs)), [rows_of(8, f32)]
    )
    norms_got = trade(norms, 2)
    att_half = join(att_rows, after(att_next, norms), 0, "att_join")
    att_other = swap(att_half, core_bit)
    ffn_half = join(ffn_rows, after(ffn_next, att_half), 0, "ffn_join")
    ffn_other = swap(ffn_half, core_bit)
    grad_w_up, grad_w_down = call(
        ffn_out_kernel, "ffn_gradients", 16, (ffn_half, after(ffn_other, att_half)),
        [rows_of(model, f32)] * 2,
    )
    small_outs = call(
        small_out_kernel, "small_gradients", 4, (small, norms, after(norms_got, grad_w_up)),
        [sds((model,), f32)] * 7 + [sds((width,), f32)] * 2,
    )
    grad_w_query, grad_w_key, grad_w_value, grad_w_out = call(
        attn_out_kernel, "attention_gradients", 16, (att_half, after(att_other, small_outs[0])),
        [rows_of(width, f32)] * 4,
    )
    (
        grad_ln1_gain, grad_ln1_shift, grad_b_up, grad_b_down, grad_b_out, grad_ln2_gain,
        grad_ln2_shift, grad_b_query, grad_b_value,
    ) = small_outs

    return (
        layer_out,
        grad_inputs,
        grad_ln1_gain,
        grad_ln1_shift,
        grad_w_query.T,
        grad_b_query,
        grad_w_key.T,
        grad_w_value.T,
        grad_b_value,
        grad_w_out,
        grad_b_out,
        grad_ln2_gain,
        grad_ln2_shift,
        grad_w_up,
        grad_b_up,
        grad_w_down,
        grad_b_down,
    )


def solution(mesh):
    return jax.shard_map(
        functools.partial(local, mesh.shape["dp"], mesh.shape["mp"]),
        mesh=mesh,
        in_specs=(
            P("dp", None),
            P("dp", None),
            P("dp", None),
            P(),
            P(),
            P(None, "mp"),
            P("mp"),
            P(None, "mp"),
            P(None, "mp"),
            P("mp"),
            P("mp", None),
            P(),
            P(),
            P(),
            P(None, "mp"),
            P("mp"),
            P("mp", None),
            P(),
        ),
        out_specs=(
            P(("dp", "mp"), None),
            P(("dp", "mp"), None),
            P(),
            P(),
            P(None, "mp"),
            P("mp"),
            P(None, "mp"),
            P(None, "mp"),
            P("mp"),
            P("mp", None),
            P(),
            P(),
            P(),
            P(None, "mp"),
            P("mp"),
            P("mp", None),
            P(),
        ),
        check_vma=False,
    )
```

```python
import functools

import jax
import jax.numpy as jnp
from jax import lax
from jax.experimental import pallas as pl
from jax.experimental.pallas import tpu as pltpu
from jax.sharding import PartitionSpec as P

HD = 64
WIN = 128
EPS = 1e-06
SMALL = 16
WIDE = 256
MIB = 1 << 20

bf16 = jnp.bfloat16
f32 = jnp.float32


def mm(left, right):
    return lax.dot_general(left, right, (((1,), (0,)), ((), ())), preferred_element_type=f32)


def mm_nt(left, right):
    return lax.dot_general(left, right, (((1,), (1,)), ((), ())), preferred_element_type=f32)


def mm_tn(left, right):
    return lax.dot_general(left, right, (((0,), (0,)), ((), ())), preferred_element_type=f32)


def row_of(vec_ref, index, cols=None):
    return vec_ref[index : index + 1, 0 : (cols or vec_ref.shape[1])]


GAIN_ONE, SHIFT_ONE, GAIN_TWO, SHIFT_TWO, B_OUT, B_DOWN, B_UP, B_QUERY, B_VALUE = range(9)


def here():
    at, own = lax.axis_index("dp"), lax.axis_index("mp")
    core = at & 1
    at_x, at_y = (at >> 1) & 1, at >> (lax.axis_size("dp").bit_length() - 2)
    turn = (at_x ^ at_y) * core
    return own, core, (at_x ^ turn, at_y ^ turn), 1 + core, 2 - core


def unit_of(values):
    centered = values - jnp.mean(values, -1, keepdims=True)
    rstd = lax.rsqrt(jnp.mean(centered * centered, -1, keepdims=True) + EPS)
    return centered * rstd, rstd


def norm_back(grad_norm, unit, rstd, gain):
    scaled = grad_norm * gain
    return rstd * (
        scaled
        - jnp.mean(scaled, -1, keepdims=True)
        - unit * jnp.mean(scaled * unit, -1, keepdims=True)
    )


def window_of(span_ref, seq, length):
    start = span_ref[0, seq]
    count = span_ref[1, seq]
    first = jnp.minimum(start, length - WIN)
    row = lax.broadcasted_iota(jnp.int32, (WIN, length), 0) + first
    col = lax.broadcasted_iota(jnp.int32, (WIN, length), 1)
    pick = row == col
    inside = pick & (row >= start) & (row < start + count)
    return pick.astype(f32).astype(bf16), inside.astype(f32).astype(bf16)


def per_head(rows, heads):
    lane = lax.broadcasted_iota(jnp.int32, (1, rows.shape[1]), 1)
    zeros = jnp.zeros_like(rows)
    parts = [
        jnp.where((lane >= h * HD) & (lane < (h + 1) * HD), rows, zeros) for h in range(heads)
    ]
    return jnp.concatenate(parts, 0)


def own_head(stacked, heads):
    rows = stacked.shape[0] // heads
    lane = lax.broadcasted_iota(jnp.int32, (1, stacked.shape[1]), 1)
    result = stacked[0:rows]
    for h in range(1, heads):
        result = jnp.where(lane >= h * HD, stacked[h * rows : (h + 1) * rows], result)
    return result


def softmax_parts(query, keys):
    scores = mm_nt(query, keys)
    terms = jnp.exp2((scores - jnp.max(scores, -1, keepdims=True)) * (0.125 * 1.4426950408889634))
    return terms, 1.0 / jnp.sum(terms, -1, keepdims=True)


def attend(query, keys, values, heads):
    terms, inverse = softmax_parts(per_head(query, heads), keys)
    return own_head(mm(terms.astype(bf16), values) * inverse, heads).astype(bf16)


def attend_back(query, keys, values, grad_mixed, heads):
    query, grad_mixed = per_head(query, heads), per_head(grad_mixed, heads)
    terms, inverse = softmax_parts(query, keys)
    prob = terms * inverse
    grad_prob = mm_nt(grad_mixed, values)
    row_dot = jnp.sum(prob * grad_prob, -1, keepdims=True)
    grad_scores = (prob * (grad_prob - row_dot)).astype(bf16)
    grad_q = own_head(mm(grad_scores, keys), heads) * 0.125
    grad_k = mm_tn(grad_scores, query) * 0.125
    grad_v = mm_tn(prob.astype(bf16), grad_mixed)
    return grad_q.astype(bf16), grad_k.astype(bf16), grad_v.astype(bf16)


def gelu_parts(values):
    phi = 0.5 * (1.0 + lax.erf(values * 0.7071067811865476))
    return phi


def start_all(copies):
    for copy in copies:
        copy.start()


def wait_all(copies):
    for copy in copies:
        copy.wait()


def prepare_kernel(count, *refs):
    vectors, (wq_ref, wk_ref, wv_ref, wo_ref, wup_ref, wdown_ref) = refs[:count], refs[count : count + 6]
    vec_ref, att_ref, ffn_ref, att_kept_ref, ffn_kept_ref = refs[count + 6 : count + 11]
    *rows_s, sems = refs[count + 11 :]
    _, core, (first, second), _, _ = here()
    rows = ffn_ref.shape[0] // 3
    place = core * 4 + first * 2 + second
    copies = [
        pltpu.make_async_copy(ref, rows_s[i], sems.at[i]) for i, ref in enumerate(vectors)
    ]
    weights = []
    for i, (ref, row, count_rows, to) in enumerate(
        ((wup_ref, place * rows, rows, 0), (wdown_ref, (core * 2 + first) * 2 * rows, 2 * rows, rows))
    ):
        weights.append(
            pltpu.make_async_copy(
                ref.at[pl.ds(pl.multiple_of(row, 16), count_rows), :],
                ffn_ref.at[pl.ds(to, count_rows), :],
                sems.at[count + i],
            )
        )
    attention = [
        pltpu.make_async_copy(
            ref.at[pl.ds(pl.multiple_of(second * rows, 16), rows), :],
            att_ref.at[pl.ds(0, rows), :],
            sems.at[count + 2],
        )
        for ref in (wq_ref, wk_ref, wv_ref, wo_ref)
    ]
    for i, copy in enumerate(attention):
        pl.when(core * 2 + first == i)(copy.start)
    start_all(weights + copies)
    wait_all(copies)
    vec_ref[...] = jnp.zeros_like(vec_ref)
    for i, ref in enumerate(vectors):
        size = ref.shape[0]
        vec_ref[i : i + 1, 0:size] = rows_s[i][...].astype(f32).reshape(1, size)
    bias = [row_of(vec_ref, index) for index in (B_UP, B_QUERY, B_VALUE)]
    bias = jnp.concatenate(bias + [jnp.zeros((SMALL - 3, vec_ref.shape[1]), f32)], 0)
    att_ref[rows:, :] = bias.astype(bf16)
    wait_all(weights + attention[:1])
    att_kept_ref[...] = att_ref[...]
    ffn_kept_ref[...] = ffn_ref[...]


def first_kernel(
    span_ref, x_hbm, wq_hbm, wk_hbm, wv_hbm, vec_ref,
    normed_ref, nw_ref, qw_ref, k_ref, v_ref, mh_ref, x_s, w_s, sems,
):
    seqs = span_ref.shape[1]
    length = x_hbm.shape[0] // seqs
    width = wq_hbm.shape[0]
    inputs = [
        pltpu.make_async_copy(x_hbm.at[pl.ds(seq * length, length), :], x_s.at[seq], sems.at[seq])
        for seq in range(seqs)
    ]
    weights = [
        pltpu.make_async_copy(ref, w_s.at[i], sems.at[seqs + i])
        for i, ref in enumerate((wq_hbm, wk_hbm, wv_hbm))
    ]
    start_all(inputs[:1] + weights + inputs[1:])
    for seq in range(seqs):
        rows = slice(seq * length, (seq + 1) * length)
        win = slice(seq * WIN, (seq + 1) * WIN)
        inputs[seq].wait()
        unit, _ = unit_of(x_s[seq].astype(f32))
        normed = (unit * row_of(vec_ref, GAIN_ONE) + row_of(vec_ref, SHIFT_ONE)).astype(bf16)
        normed_ref[rows, :] = normed
        pick, _ = window_of(span_ref, seq, length)
        nw = mm(pick, normed).astype(bf16)
        nw_ref[win, :] = nw
        if seq == 0:
            wait_all(weights)
        query = (mm_nt(nw, w_s[0]) + row_of(vec_ref, B_QUERY, width)).astype(bf16)
        keys = mm_nt(normed, w_s[1]).astype(bf16)
        values = (mm_nt(normed, w_s[2]) + row_of(vec_ref, B_VALUE, width)).astype(bf16)
        qw_ref[win, :] = query
        k_ref[rows, :] = keys
        v_ref[rows, :] = values
        mh_ref[seq] = attend(query, keys, values, width // HD)


def pick_kernel(span_ref, cot_ref, gw_ref):
    seqs = span_ref.shape[1]
    length = cot_ref.shape[0] // seqs
    for seq in range(seqs):
        _, inside = window_of(span_ref, seq, length)
        rows = slice(seq * length, (seq + 1) * length)
        gw_ref[seq * WIN : (seq + 1) * WIN, :] = mm(inside, cot_ref[rows, :]).astype(bf16)


def feed_back(normed, grad_out, up, down, bias):
    pre = mm(normed, up) + bias
    phi = gelu_parts(pre)
    slope = phi + pre * (0.3989422804014327 * jnp.exp(-0.5 * pre * pre))
    grad_pre = (slope * mm_nt(grad_out, down)).astype(bf16)
    return (pre * phi).astype(bf16), grad_pre


def ffn_kernel(
    own_ref, one_ref, pair_ref, gw_ref, vec_ref, wup_ref, wdown_ref,
    keep_ref, send_ref, small_ref, normed_s,
):
    own, core, _, one, two = here()
    sources = (
        (own, own_ref, 0), (own ^ one, one_ref, 0), (own ^ two, pair_ref, 0),
        (own ^ one ^ two, pair_ref, WIN),
    )
    for seq, ref, row in sources:
        normed_s[pl.ds(pl.multiple_of(seq * WIN, 16), WIN), :] = ref[row : row + WIN, :]
    normed, grad_out = normed_s[...], gw_ref[...]
    hidden, grad_pre = feed_back(
        normed, grad_out, wup_ref[...], wdown_ref[...], row_of(vec_ref, B_UP)
    )
    grad_up = mm_tn(normed, grad_pre).astype(bf16)
    grad_down = mm_tn(hidden, grad_out).astype(bf16)

    @pl.when(core == 0)
    def _():
        keep_ref[...] = grad_up
        send_ref[...] = grad_down

    @pl.when(core == 1)
    def _():
        keep_ref[...] = grad_down
        send_ref[...] = grad_up

    small_ref[...] = jnp.zeros_like(small_ref)
    small_ref[0:1, :] = jnp.sum(grad_pre.astype(f32), 0, keepdims=True)
    small_ref[1:2, :] = jnp.sum(grad_out.astype(f32), 0, keepdims=True)


def own_window_kernel(
    rows, normed_ref, resid_ref, gw_ref, vec_ref, bias_ref, own_up_ref, own_down_ref, *refs
):
    *stacks, gresid_ref, gb_ref, up_s, down_s = refs
    normed = normed_ref[...]
    grad_out = gw_ref[pl.ds(pl.multiple_of(here()[0] * WIN, 16), WIN), :]
    grad_norm = None
    for shard in range(-1, 3):
        if shard < 0:
            up, down, bias = own_up_ref[...], own_down_ref[...], row_of(vec_ref, B_UP)
        else:
            lay_ffn(up_s.at[shard], down_s.at[shard], stacks, shard, rows)
            up, down = up_s[shard], down_s[shard]
            bias = bias_ref[shard * SMALL : (shard + 1) * SMALL, :].astype(f32)[0:1]
        _, grad_pre = feed_back(normed, grad_out, up, down, bias)
        part = mm_nt(grad_pre, up)
        grad_norm = part if grad_norm is None else grad_norm + part
    unit, rstd = unit_of(resid_ref[...])
    grad = grad_out.astype(f32) + norm_back(grad_norm, unit, rstd, row_of(vec_ref, GAIN_TWO))
    gresid_ref[...] = grad
    gb_ref[0:WIN, :] = grad.astype(bf16)
    sums = [jnp.sum(grad_norm * unit, 0, keepdims=True), jnp.sum(grad_norm, 0, keepdims=True)]
    sums.append(jnp.zeros((SMALL - 2, grad.shape[1]), f32))
    gb_ref[WIN : WIN + SMALL, :] = jnp.concatenate(sums, 0).astype(bf16)


def attn_kernel(
    last, ga_ref, gb_ref, mh_ref, nw_ref, qw_ref, k_ref, v_ref, normed_ref,
    wq_ref, wk_ref, wv_ref, wo_ref, *refs,
):
    if last:
        vec_ref, small_ref, acc_in_ref, col_in_ref = refs[:4]
        keep_ref, send_ref, acc_ref, col_ref = refs[4:]
        acc_ref[...] = acc_in_ref[...]
        col_ref[...] = col_in_ref[...]
    else:
        acc_ref, col_ref = refs
        acc_ref[...] = jnp.zeros_like(acc_ref)
        col_ref[...] = jnp.zeros_like(col_ref)
    own, core, _, one, two = here()
    width, model = wq_ref.shape
    seqs = mh_ref.shape[0]
    length = normed_ref.shape[0] // seqs
    first = own ^ two if last else own
    block_rows = WIN + SMALL
    for seq, ref, row in ((first, ga_ref, 0), (first ^ one, gb_ref, block_rows if last else 0)):
        rows = pl.ds(pl.multiple_of(seq * length, length), length)
        win = pl.ds(pl.multiple_of(seq * WIN, WIN), WIN)
        grad_branch = ref[row : row + WIN, :]
        sums = ref[row + WIN : row + block_rows, :].astype(f32)
        grad_mixed = mm_nt(grad_branch, wo_ref[...]).astype(bf16)
        grad_q, grad_k, grad_v = attend_back(
            qw_ref[win, :], k_ref[rows, :], v_ref[rows, :], grad_mixed, width // HD
        )
        normed = normed_ref[rows, :]
        acc_ref[0] += mm_tn(grad_q, nw_ref[win, :])
        acc_ref[1] += mm_tn(grad_k, normed)
        acc_ref[2] += mm_tn(grad_v, normed)
        acc_ref[3] += mm_tn(mh_ref[seq], grad_branch)
        for i, grad in enumerate((grad_q, grad_k, grad_v, grad_branch)):
            col_ref[i : i + 1, 0 : grad.shape[1]] += jnp.sum(grad.astype(f32), 0, keepdims=True)
        col_ref[4:6, :] += sums[0:2]
    if not last:
        return

    sums = jnp.zeros((1, model), f32)
    total = jnp.zeros((1, model), f32)
    pad = jnp.zeros((1, model - width), f32)
    for i, w_ref in enumerate((wq_ref, wk_ref, wv_ref)):
        sums += jnp.sum(w_ref[...].astype(f32) * acc_ref[i], 0, keepdims=True)
        cols = col_ref[i : i + 1, 0:width]
        high = cols.astype(bf16)
        low = (cols - high.astype(f32)).astype(bf16)
        both = jnp.concatenate([high, low, jnp.zeros((14, width), bf16)], 0)
        total += jnp.sum(mm(both, w_ref[...]), 0, keepdims=True)
    gain = (sums - row_of(vec_ref, SHIFT_ONE) * total) / row_of(vec_ref, GAIN_ONE)
    small = jnp.concatenate(
        [
            gain,
            total,
            small_ref[0:2, :],
            col_ref[3:6, :],
            jnp.concatenate([col_ref[0:1, 0:width], pad], 1),
            jnp.concatenate([col_ref[2:3, 0:width], pad], 1),
            jnp.zeros((SMALL - 9, model), f32),
        ],
        0,
    ).astype(bf16)
    first = jnp.concatenate([acc_ref[0], acc_ref[1]], 0).astype(bf16)
    second = jnp.concatenate([acc_ref[2], acc_ref[3]], 0).astype(bf16)
    rows = first.shape[0]
    keep_ref[rows : rows + SMALL, :] = small
    send_ref[rows : rows + SMALL, :] = small

    @pl.when(core == 0)
    def _():
        keep_ref[0:rows, :] = first
        send_ref[0:rows, :] = second

    @pl.when(core == 1)
    def _():
        keep_ref[0:rows, :] = second
        send_ref[0:rows, :] = first


def split_kernel(small, which, keep_ref, recv_ref, mine_ref, send_ref):
    bit = here()[2][which]
    rows = mine_ref.shape[0] - small

    def total(first, count):
        part = pl.ds(first, count)
        return keep_ref[part, :].astype(f32) + recv_ref[part, :].astype(f32)

    mine_ref[0:rows, :] = total(pl.multiple_of(bit * rows, 16), rows)
    send_ref[0:rows, :] = total(pl.multiple_of((1 - bit) * rows, 16), rows).astype(bf16)
    if small:
        block = total(2 * rows, small).astype(bf16)
        mine_ref[rows:, :] = block.astype(f32)
        send_ref[rows:, :] = block


def total_kernel(mine_ref, recv_ref, out_ref):
    out_ref[...] = (mine_ref[...] + recv_ref[...].astype(f32)).astype(bf16)


def pair_kernel(left_ref, right_ref, out_ref):
    out_ref[...] = (left_ref[...].astype(f32) + right_ref[...].astype(f32)).astype(bf16)


def last_pair_kernel(left_ref, right_ref, out_ref, small_ref, norms_ref):
    total = left_ref[...].astype(f32) + right_ref[...].astype(f32)
    rows = out_ref.shape[0]
    out_ref[...] = total[0:rows].astype(bf16)
    small_ref[...] = total[rows:]
    norms_ref[...] = total[rows : rows + 8]


def join_kernel(which, mine_ref, recv_ref, out_ref):
    bit = here()[2][which]
    rows = mine_ref.shape[0]
    out_ref[pl.ds(pl.multiple_of(bit * rows, 16), rows), :] = mine_ref[...]
    out_ref[pl.ds(pl.multiple_of((1 - bit) * rows, 16), rows), :] = recv_ref[...]


def add_kernel(left_ref, right_ref, out_ref):
    out_ref[...] = left_ref[...] + right_ref[...]


def small_out_kernel(small_ref, left_ref, right_ref, *out_refs):
    norms = left_ref[...] + right_ref[...]
    for i, ref in enumerate(out_refs):
        row = norms[i : i + 1] if i < 2 else small_ref[i : i + 1, :]
        ref[...] = row[:, 0 : ref.shape[0]].reshape(ref.shape[0])


def ffn_out_kernel(mine_ref, other_ref, up_ref, down_ref):
    core = here()[1]

    def write(first_ref, second_ref):
        up_ref[...] = first_ref[...].astype(f32)
        down_ref[...] = second_ref[...].astype(f32)

    pl.when(core == 0)(lambda: write(mine_ref, other_ref))
    pl.when(core == 1)(lambda: write(other_ref, mine_ref))


def attn_out_kernel(
    mine_ref, other_ref, small_ref, left_ref, right_ref, q_ref, k_ref, v_ref, o_ref, *small_refs
):
    small_out_kernel(small_ref, left_ref, right_ref, *small_refs)
    core = here()[1]
    width = o_ref.shape[0]

    def write(first_ref, second_ref):
        q_ref[...] = first_ref[0:width, :].astype(f32)
        k_ref[...] = first_ref[width : 2 * width, :].astype(f32)
        v_ref[...] = second_ref[0:width, :].astype(f32)
        o_ref[...] = second_ref[width : 2 * width, :].astype(f32)

    pl.when(core == 0)(lambda: write(mine_ref, other_ref))
    pl.when(core == 1)(lambda: write(other_ref, mine_ref))


def unpack_kernel(one_ref, pair_ref, got_ref, bias_ref):
    each = one_ref.shape[0]
    rows = each - SMALL
    for i, (ref, row) in enumerate(((one_ref, 0), (pair_ref, 0), (pair_ref, each))):
        got_ref[i * rows : (i + 1) * rows, :] = ref[row : row + rows, :]
        bias_ref[i * SMALL : (i + 1) * SMALL, :] = ref[row + rows : row + each, :]


def rows_kernel(moves, count, *refs):
    for parts, out_ref in zip(moves, refs[count:]):
        to = 0
        for source, row, rows in parts:
            out_ref[to : to + rows, :] = refs[source][row : row + rows, :]
            to += rows


def stack_kernel(*refs):
    out_ref = refs[-1]
    row = 0
    for ref in refs[:-1]:
        out_ref[row : row + ref.shape[0], :] = ref[...]
        row += ref.shape[0]


def own_rows(ref, length):
    return ref[pl.ds(pl.multiple_of(here()[0] * length, 16), length), :]


def eighths(refs, shard, rows):
    _, own_core, (first, second), _, _ = here()
    for flip, ref in enumerate(refs):
        bits = (second, first) if flip else (first, second)
        at = (1, 0, 2)[shard] if flip else shard
        for i in range(4):
            place = (own_core ^ flip) * 4 + (bits[0] ^ (i % 2)) * 2 + (bits[1] ^ (i // 2))
            yield place, ref, (i * 3 + at) * rows


def lay_attention(w_s, n, own_refs, stacks, shard, rows):
    if shard < 0:
        for i, ref in enumerate(own_refs):
            w_s[n, i * WIDE : i * WIDE + rows, :] = ref[...]
    else:
        piece = rows // 2
        for place, ref, row in eighths(stacks, shard, piece):
            to = pl.multiple_of((place >> 1) * WIDE + (place & 1) * piece, 16)
            w_s[n, pl.ds(to, piece), :] = ref[row : row + piece, :]


def lay_ffn(up_s, down_s, stacks, shard, rows):
    for place, ref, row in eighths(stacks[:2], shard, rows):
        up_s[pl.ds(pl.multiple_of(place * rows, 16), rows), :] = ref[row : row + rows, :]
    _, own_core, (first, second), _, _ = here()
    each = 2 * rows
    for flip, ref in enumerate(stacks[2:]):
        at = (1, 0, 2)[shard] if flip else shard
        for i in range(2):
            place = (own_core ^ flip) * 2 + ((second if flip else first) ^ i)
            row = (i * 3 + at) * each
            to = pl.ds(pl.multiple_of(place * each, 16), each)
            down_s[to, :] = ref[row : row + each, :]


def local_attn_kernel(near, rows, span_ref, acc_ref, normed_ref, vec_ref, bias_ref, *refs):
    own = 4 if near else 0
    own_refs, stacks, rest = refs[:own], refs[own : own + 2], refs[own + 2 :]
    if near:
        qkv_ref, resid_ref, w_s, acc_s = rest
    else:
        qkv_ref, resid_ref, normed_two_ref, resid_win_ref, normed_win_ref, w_s, acc_s = rest
    length, model = resid_ref.shape
    normed = own_rows(normed_ref, length)
    if near:
        acc_s[...] = own_rows(acc_ref, length).astype(f32)
    else:
        acc_s[...] = acc_ref[...]
    pad = jnp.zeros((1, WIDE - rows), f32)
    for n, shard in enumerate((-1, 0) if near else (1, 2)):
        for i in range(3):
            w_s[n, i * WIDE + rows : (i + 1) * WIDE, :] = jnp.zeros((WIDE - rows, model), bf16)
        lay_attention(w_s, n, own_refs, stacks, shard, rows)
        if shard < 0:
            bias_q, bias_v = row_of(vec_ref, B_QUERY, rows), row_of(vec_ref, B_VALUE, rows)
        else:
            block = bias_ref[shard * SMALL : (shard + 1) * SMALL, :].astype(f32)
            bias_q, bias_v = block[1:2, 0:rows], block[2:3, 0:rows]
        bias = jnp.concatenate([bias_q, pad, jnp.zeros((1, WIDE), f32), bias_v, pad], 1)
        qkv = (mm_nt(normed, w_s[n, 0 : 3 * WIDE, :]) + bias).astype(bf16)
        qkv_ref[n] = qkv
        keys, values = qkv[:, WIDE : 2 * WIDE], qkv[:, 2 * WIDE : 3 * WIDE]
        mixed = jnp.concatenate(
            [
                attend(qkv[first : first + WIN, 0:WIDE], keys, values, rows // HD)
                for first in range(0, length, WIN)
            ],
            0,
        )
        acc_s[...] += mm(mixed[:, 0:rows], w_s[n, 3 * WIDE : 3 * WIDE + rows, :])
    resid = acc_s[...]
    if not near:
        resid += row_of(vec_ref, B_OUT)
        unit, _ = unit_of(resid)
        normed = (unit * row_of(vec_ref, GAIN_TWO) + row_of(vec_ref, SHIFT_TWO)).astype(bf16)
        normed_two_ref[...] = normed
        pick, _ = window_of(span_ref, here()[0], length)
        normed_win_ref[...] = mm(pick, normed).astype(bf16)
        high = resid.astype(bf16)
        rest = resid - high.astype(f32)
        low = rest.astype(bf16)
        last = (rest - low.astype(f32)).astype(bf16)
        resid_win_ref[...] = mm(pick, high) + mm(pick, low) + mm(pick, last)
    resid_ref[...] = resid


def local_back_kernel(
    near, rows, span_ref, acc_ref, x_ref, gresid_ref, gb_ref, qkv_ref, vec_ref, *refs
):
    own = 4 if near else 0
    own_refs, stacks = refs[:own], refs[own : own + 2]
    out_ref, w_s = refs[own + 2 :]
    length, model = out_ref.shape
    pick, _ = window_of(span_ref, here()[0], length)
    total = None if near else acc_ref[...]
    for n, shard in enumerate((-1, 0) if near else (1, 2)):
        for i in range(3):
            w_s[n, i * WIDE + rows : (i + 1) * WIDE, :] = jnp.zeros((WIDE - rows, model), bf16)
        lay_attention(w_s, n, own_refs, stacks, shard, rows)
        qkv = qkv_ref[n]
        query = mm(pick, qkv[:, 0:WIDE]).astype(bf16)
        w_out = w_s[n, 3 * WIDE : 3 * WIDE + rows, :]
        grad_mixed = mm_nt(gb_ref[0:WIN, :], w_out).astype(bf16)
        grad_mixed = jnp.concatenate([grad_mixed, jnp.zeros((WIN, WIDE - rows), bf16)], 1)
        grad_q, grad_k, grad_v = attend_back(
            query, qkv[:, WIDE : 2 * WIDE], qkv[:, 2 * WIDE : 3 * WIDE], grad_mixed, rows // HD
        )
        grad_q = mm_tn(pick, grad_q).astype(bf16)
        part = mm(jnp.concatenate([grad_q, grad_k, grad_v], 1), w_s[n, 0 : 3 * WIDE, :])
        total = part if total is None else total + part
    if near:
        out_ref[...] = total
    else:
        unit, rstd = unit_of(own_rows(x_ref, length).astype(f32))
        grad = norm_back(total, unit, rstd, row_of(vec_ref, GAIN_ONE))
        resid = gresid_ref[...]
        high = resid.astype(bf16)
        low = (resid - high.astype(f32)).astype(bf16)
        out_ref[...] = (grad + mm_tn(pick, high) + mm_tn(pick, low)).astype(bf16)


def local_ffn_kernel(near, rows, acc_ref, normed_ref, vec_ref, bias_ref, *refs):
    own = 2 if near else 0
    own_refs, stacks = refs[:own], refs[own : own + 4]
    out_ref, up_s, down_s = refs[own + 4 :]
    normed = normed_ref[...]
    total = acc_ref[...]
    for n, shard in enumerate((-1, 0) if near else (1, 2)):
        if shard < 0:
            up, down, bias = own_refs[0][...], own_refs[1][...], row_of(vec_ref, B_UP)
        else:
            lay_ffn(up_s.at[n], down_s.at[n], stacks, shard, rows)
            up, down = up_s[n], down_s[n]
            bias = bias_ref[shard * SMALL : (shard + 1) * SMALL, :].astype(f32)[0:1]
        pre = mm(normed, up) + bias
        hidden = (pre * gelu_parts(pre)).astype(bf16)
        total += mm(hidden, down)
    if near:
        out_ref[...] = total
    else:
        out_ref[...] = (total + row_of(vec_ref, B_DOWN)).astype(bf16)


def sds(shape, dtype):
    return jax.ShapeDtypeStruct(shape, dtype)


def params(mib=48):
    return pltpu.CompilerParams(vmem_limit_bytes=mib * MIB)


LONG = 30


MICROS = {
    "prepare": 2.5, "windows_forward": 8, "windows_pick": 1.2, "own_attention_own": 2.7,
    "own_attention_rest": 9.0, "own_window": 4.1, "own_probabilities": 3.5, "windows_ffn": 3.4,
    "windows_attention_back_near": 3.3, "windows_attention_back_far": 3.9, "own_ffn_near": 2.8,
    "own_ffn_far": 3.8, "own_back_near": 4.8, "own_back_far": 6.1, "ffn_gradients": 2.5,
    "attention_gradients": 1.6, "small_gradients": 0.6,
}


def cost(name):
    micros = MICROS.get(name, 0.1) * 0.1
    return pl.CostEstimate(
        flops=int(micros * 1e9), bytes_accessed=int(micros * 3e6), transcendentals=0
    )


SMEM = pl.BlockSpec(memory_space=pltpu.SMEM)
VMEM = pl.BlockSpec(memory_space=pltpu.VMEM)
ANY = pl.BlockSpec(memory_space=pl.ANY)
DMA = pltpu.SemaphoreType.DMA


def after(value, *deps):
    return lax.optimization_barrier((value,) + deps)[0]


def call(kernel, name, mib, args, outs, scratch=(), scalars=0):
    return pl.pallas_call(
        kernel,
        in_specs=[SMEM] * scalars + [VMEM] * (len(args) - scalars),
        out_specs=[VMEM] * len(outs),
        out_shape=outs,
        scratch_shapes=list(scratch),
        compiler_params=params(mib),
        cost_estimate=cost(name),
        name=name,
    )(*args)


def local(
    dp_size, mp_size, inputs, cotangent, span_table, ln1_gain, ln1_shift, w_query, b_query, w_key,
    w_value, b_value, w_out, b_out, ln2_gain, ln2_shift, w_up, b_up, w_down, b_down,
):
    tok_rows, model = inputs.shape
    seqs = span_table.shape[0]
    length = tok_rows // seqs
    width = w_query.shape[1]
    units = w_up.shape[1]
    dp_bits = dp_size.bit_length() - 1
    core_bit, x_bit, y_bit = 1, 2, 1 << (dp_bits - 1)
    def joint(value, flip):
        pairs = []
        for i in range(dp_size):
            for j in range(mp_size):
                dp_flip, mp_flip = flip(i & 1)
                pairs.append((i * mp_size + j, (i ^ dp_flip) * mp_size + (j ^ mp_flip)))
        return lax.ppermute(value, ("dp", "mp"), pairs)

    def trade(value, bits):
        return joint(value, lambda core: (0, bits))

    def step_one(value):
        return joint(value, lambda core: (0, 2 if core else 1))

    def step_two(value):
        return joint(value, lambda core: (0, 1 if core else 2))

    def swap(value, bits):
        return joint(value, lambda core: (bits, 0))

    def cross_one(value):
        return joint(value, lambda core: ((y_bit, 0) if core else (x_bit, 0)))

    def cross_halves(value):
        rows = value.shape[0] // 2
        return cross_one(value[:rows]), cross_one(value[rows:])

    def cross_two(value):
        return joint(value, lambda core: ((x_bit, 0) if core else (y_bit, 0)))

    wq, wk, wv = w_query.T, w_key.T, w_value.T
    spans = span_table.T

    def rows_of(count, dtype=bf16):
        return sds((count, model), dtype)

    def stack(name, *arrays):
        rows = sum(a.shape[0] for a in arrays)
        return call(stack_kernel, name, 8, arrays, [rows_of(rows)])[0]

    vectors = (ln1_gain, ln1_shift, ln2_gain, ln2_shift, b_out, b_down, b_up, b_query, b_value)
    eighth = model // 8
    vec, att_sent, ffn_sent, att_piece, ffn_piece = pl.pallas_call(
        functools.partial(prepare_kernel, len(vectors)),
        in_specs=[ANY] * (len(vectors) + 6),
        out_specs=[VMEM] * 5,
        out_shape=[rows_of(len(vectors), f32)]
        + [rows_of(eighth + SMALL), rows_of(3 * eighth)] * 2,
        scratch_shapes=[pltpu.VMEM(v.shape, bf16) for v in vectors] + [DMA((len(vectors) + 3,))],
        compiler_params=params(60),
        cost_estimate=cost("prepare"),
        name="prepare",
    )(*vectors, wq, wk, wv, w_out, w_up, w_down)
    att_one = step_one(att_sent)
    ffn_one = step_one(ffn_sent)

    win_rows = seqs * WIN
    normed, nw, qw, keys, values, mh = pl.pallas_call(
        first_kernel,
        in_specs=[SMEM] + [ANY] * 4 + [VMEM],
        out_specs=[VMEM] * 6,
        out_shape=[
            rows_of(tok_rows),
            rows_of(win_rows),
            sds((win_rows, width), bf16),
            sds((tok_rows, width), bf16),
            sds((tok_rows, width), bf16),
            sds((seqs, WIN, width), bf16),
        ],
        scratch_shapes=[
            pltpu.VMEM((seqs, length, model), bf16),
            pltpu.VMEM((3, width, model), bf16),
            DMA((seqs + 3,)),
        ],
        compiler_params=params(24),
        cost_estimate=cost("windows_forward"),
        name="windows_forward",
    )(spans, inputs, wq, wk, wv, vec)
    def pick_rows(name, ins, moves):
        outs = [rows_of(sum(part[2] for part in parts)) for parts in moves]
        return call(functools.partial(rows_kernel, moves, len(ins)), name, 8, ins, outs)

    att_pair = step_two(stack("attention_pair", after(att_piece, normed), att_one))
    ffn_pair = step_two(stack("ffn_pair", after(ffn_piece, normed), ffn_one))
    att_got, biases = call(
        unpack_kernel, "attention_got", 4, (att_one, att_pair),
        [rows_of(3 * eighth), rows_of(3 * SMALL)],
    )
    att_over = cross_one(att_got)

    att_both = stack("attention_both", att_got, att_over)
    att_over = cross_two(att_both)
    (gw,) = call(
        pick_kernel, "windows_pick", 16, (spans, after(cotangent, att_both)), [rows_of(win_rows)],
        scalars=1,
    )
    third = 3 * eighth
    up_got, down_got = pick_rows(
        "ffn_got",
        [ffn_one, after(ffn_pair, gw)],
        [
            ((0, 0, eighth), (1, 0, eighth), (1, third, eighth)),
            ((0, eighth, 2 * eighth), (1, eighth, 2 * eighth), (1, third + eighth, 2 * eighth)),
        ],
    )
    up_over, down_over = cross_one(up_got), cross_one(down_got)
    up_both = stack("up_both", up_got, up_over)
    up_over = cross_two(up_both)
    att_all = stack("attention_all", att_both, after(att_over, up_both))
    att_weights = [att_all, swap(att_all, core_bit)]
    own_weights = [wq, wk, wv, w_out]

    def attention_part(near, acc, weights, name):
        outs = [sds((2, length, 3 * WIDE), bf16), rows_of(length, f32)]
        if not near:
            outs += [rows_of(length), rows_of(WIN, f32), rows_of(WIN)]
        return call(
            functools.partial(local_attn_kernel, near, width), name, 16,
            (spans, acc, normed, vec, biases, *weights), outs,
            [pltpu.VMEM((2, 4 * WIDE, model), bf16), pltpu.VMEM((length, model), f32)], scalars=1,
        )

    def ffn_part(near, acc, weights, name):
        return call(
            functools.partial(local_ffn_kernel, near, eighth), name, 16,
            (acc, normed_two, vec, biases, *weights), [rows_of(length, f32 if near else bf16)],
            [pltpu.VMEM((2, model, units), bf16), pltpu.VMEM((2, units, model), bf16)],
        )[0]

    def back_part(near, acc, qkv, weights, name):
        return call(
            functools.partial(local_back_kernel, near, width), name, 16,
            (spans, acc, inputs, gresid, gb, qkv, vec, *weights),
            [rows_of(length, f32 if near else bf16)],
            [pltpu.VMEM((2, 4 * WIDE, model), bf16)], scalars=1
        )[0]

    qkv_near, resid_near = attention_part(
        True, inputs, own_weights + att_weights, "own_attention_near"
    )
    qkv_far, resid, normed_two, resid_win, normed_win = attention_part(
        False, resid_near, att_weights, "own_attention_far"
    )

    nt_one = step_one(normed_win)
    nt_pair = step_two(stack("normed_pair", normed_win, nt_one))
    down_all = stack("down_all", down_got, after(down_over, normed_win))
    up_all = stack("up_all", up_both, after(up_over, nt_one))
    ffn_weights = [up_all, swap(up_all, core_bit), down_all, swap(down_all, core_bit)]

    gresid, gb = call(
        functools.partial(own_window_kernel, eighth),
        "own_window",
        24,
        (normed_win, resid_win, gw, vec, biases, w_up, w_down, *ffn_weights),
        [rows_of(WIN, f32), rows_of(WIN + SMALL)],
        [pltpu.VMEM((3, model, units), bf16), pltpu.VMEM((3, units, model), bf16)],
    )
    gb_one = step_one(gb)
    def sum_split(keep, recv, small, which, name):
        rows = (keep.shape[0] - small) // 2 + small
        return call(
            functools.partial(split_kernel, small, which), name, 8, (keep, recv),
            [rows_of(rows, f32), rows_of(rows)],
        )

    def sum_total(mine, recv, name):
        return call(total_kernel, name, 8, (mine, recv), [rows_of(mine.shape[0])])[0]

    def across_two(rows, name):
        for bit in range(2, dp_bits - 1):
            rows = pair(rows, swap(rows, 1 << bit), name)
        return rows, cross_two(rows)

    def pair(left, right, name):
        return call(pair_kernel, name, 8, (left, right), [rows_of(left.shape[0])])[0]

    def join(mine, recv, which, name):
        return call(
            functools.partial(join_kernel, which), name, 8, (mine, recv),
            [rows_of(2 * mine.shape[0])],
        )[0]

    ffn_keep, ffn_send, ffn_small = call(
        ffn_kernel,
        "windows_ffn",
        24,
        (after(normed_win, gb), nt_one, nt_pair, gw, vec, w_up, w_down),
        [rows_of(model)] * 2 + [rows_of(8, f32)],
        [pltpu.VMEM((win_rows, model), bf16)],
    )
    gb_pair = step_two(stack("branch_pair", after(gb, ffn_keep), gb_one))
    attn_args = (mh, nw, qw, keys, values, normed, wq, wk, wv, w_out)
    acc, cols = call(
        functools.partial(attn_kernel, False),
        "windows_attention_back_near",
        24,
        (gb, gb_one, *attn_args),
        [sds((4, width, model), f32), rows_of(8, f32)],
    )

    ffn_recv = swap(after(ffn_send, gb_one), core_bit)
    ffn_mine, ffn_send = sum_split(ffn_keep, ffn_recv, 0, 0, "ffn_split_one")
    ffn_recv = stack("ffn_halves", *cross_halves(ffn_send))
    ffn_acc = ffn_part(True, after(resid, ffn_send), [w_up, w_down] + ffn_weights, "own_ffn_near")
    att_rows = 2 * width + SMALL
    keep, send = call(
        functools.partial(attn_kernel, True),
        "windows_attention_back_far",
        24,
        (after(gb_pair, ffn_acc, ffn_recv), gb_pair, *attn_args, vec, ffn_small, acc, cols),
        [rows_of(att_rows)] * 2,
        [pltpu.VMEM((4, width, model), f32), pltpu.VMEM((8, model), f32)]
    )

    att_recv = swap(send, core_bit)
    ffn_sum, ffn_recv = across_two(
        sum_total(ffn_mine, after(ffn_recv, keep), "ffn_total"), "ffn_more"
    )
    att_mine, att_send = sum_split(keep, after(att_recv, ffn_sum), SMALL, 0, "att_split")
    att_recv = cross_one(att_send)
    layer_out = ffn_part(False, after(ffn_acc, att_send), ffn_weights, "own_ffn_far")
    att_sum, att_recv = across_two(
        sum_total(att_mine, after(att_recv, layer_out), "att_total"), "att_more"
    )
    back_acc = back_part(
        True, after(gresid, att_sum), qkv_near, own_weights + att_weights, "own_back_near"
    )
    ffn_rows = pair(ffn_sum, after(ffn_recv, att_sum), "ffn_pair_two")
    ffn_next = cross_one(ffn_rows)
    att_rows, small, norms = call(
        last_pair_kernel, "att_pair_two", 8, (att_sum, after(att_recv, back_acc)),
        [rows_of(width), rows_of(SMALL, f32), rows_of(8, f32)],
    )
    att_next = cross_one(att_rows)
    norms_got = trade(norms, 1)
    grad_inputs = back_part(False, after(back_acc, att_rows), qkv_far, att_weights, "own_back_far")
    (norms,) = call(
        add_kernel, "norm_sums", 4, (norms, after(norms_got, grad_inputs)), [rows_of(8, f32)]
    )
    norms_got = trade(norms, 2)
    att_half = join(att_rows, after(att_next, norms), 0, "att_join")
    att_other = swap(att_half, core_bit)
    ffn_half = join(ffn_rows, after(ffn_next, att_half), 0, "ffn_join")
    ffn_other = swap(ffn_half, core_bit)
    grad_w_up, grad_w_down = call(
        ffn_out_kernel, "ffn_gradients", 16, (ffn_half, after(ffn_other, att_half)),
        [rows_of(model, f32)] * 2,
    )
    grad_w_query, grad_w_key, grad_w_value, grad_w_out, *small_outs = call(
        attn_out_kernel, "attention_gradients", 16,
        (att_half, after(att_other, grad_w_up), small, norms, norms_got),
        [rows_of(width, f32)] * 4 + [sds((model,), f32)] * 7 + [sds((width,), f32)] * 2,
    )
    (
        grad_ln1_gain, grad_ln1_shift, grad_b_up, grad_b_down, grad_b_out, grad_ln2_gain,
        grad_ln2_shift, grad_b_query, grad_b_value,
    ) = small_outs

    return (
        layer_out,
        grad_inputs,
        grad_ln1_gain,
        grad_ln1_shift,
        grad_w_query.T,
        grad_b_query,
        grad_w_key.T,
        grad_w_value.T,
        grad_b_value,
        grad_w_out,
        grad_b_out,
        grad_ln2_gain,
        grad_ln2_shift,
        grad_w_up,
        grad_b_up,
        grad_w_down,
        grad_b_down,
    )


def solution(mesh):
    return jax.shard_map(
        functools.partial(local, mesh.shape["dp"], mesh.shape["mp"]),
        mesh=mesh,
        in_specs=(
            P("dp", None),
            P("dp", None),
            P("dp", None),
            P(),
            P(),
            P(None, "mp"),
            P("mp"),
            P(None, "mp"),
            P(None, "mp"),
            P("mp"),
            P("mp", None),
            P(),
            P(),
            P(),
            P(None, "mp"),
            P("mp"),
            P("mp", None),
            P(),
        ),
        out_specs=(
            P(("dp", "mp"), None),
            P(("dp", "mp"), None),
            P(),
            P(),
            P(None, "mp"),
            P("mp"),
            P(None, "mp"),
            P(None, "mp"),
            P("mp"),
            P("mp", None),
            P(),
            P(),
            P(),
            P(None, "mp"),
            P("mp"),
            P("mp", None),
            P(),
        ),
        check_vma=False,
    )
```
